128 devices in a mesh: src: 4 (over y), gz: 32 (over x, z, core).
Axes of the slice: x: 4, y: 4, z: 4, core: 2. Of those that a mesh axis runs over, the one named last changes fastest.
Arguments:
- fields_e: float32 [4, 3, 8, 256, 4096], P('src', None, None, None, 'gz'), may hold values from -12 to 12
- fields_h: float32 [4, 3, 8, 256, 4096], P('src', None, None, None, 'gz'), may hold values from -0.0007324219 to 0.0007324219
- cot_e: float32 [4, 3, 8, 256, 4096], P('src', None, None, None, 'gz'), may hold values from -6 to 6
- cot_h: float32 [4, 3, 8, 256, 4096], P('src', None, None, None, 'gz'), may hold values from -6 to 6
- labels: int32 [8, 256, 4096], P(None, None, 'gz'), may hold values from 0 to 3
- region_eps: float32 [4], replicated, may hold values from 1 to 12
- angle_index: int32 [4], P('src'), may hold values from 0 to 7
- profiles: float32 [8, 2, 8, 256], replicated, may hold values from -6 to 6
- zsheet: float32 [4096], P('gz'), may hold values from -0.0007324219 to 0.0007324219
- layer_term: float32 [4096], P('gz'), as said below
- block_inverse: float32 [4096, 128], P('gz'), as said below
Outputs:
- e_new: float32 [4, 3, 8, 256, 4096], P('src', None, None, None, 'gz')
- h_new: float32 [4, 3, 8, 256, 4096], P('src', None, None, None, 'gz')
- eps_grad: float32 [8, 256, 4096], P(None, None, 'gz')
The draws below stay inside these ranges and needn't reach their ends.
Inputs may be any that keep to these rules, and one draw needn't show every extreme that they name: `layer_term`: each value is between 1 / (256 * 128^2) and 8 / (256 * 128^2). `block_inverse`: each block of 128 rows is symmetric with positive entries; with the couplings of the steps the matrix M is symmetric positive definite.
All inputs are finite; a program needn't handle non-finite values.
Results may differ from the reference program's by a relative error of at most 0.0003.
Values sent between devices are 32-bit elements; how exact they have to be, the bound alone decides.
No kernel may reach another device: no remote copies, remote signals or barrier semaphores. Data moves between devices by JAX's collectives and lax.ppermute only.
A program may use at most 128 MiB of HBM per device.

```python
import math
import jax
import jax.numpy as jnp
from jax import lax

X = 8
Y = 256
CZ = 128
REGIONS = 4
ANGLES = 8
SRCS = 4
NZ = 4096


def layer_values(key):
    uniform_draw = jax.random.uniform(jax.random.fold_in(key, 11), (NZ,), jnp.float32)
    lowest = jnp.log(jnp.float32(1.0 / (256.0 * CZ * CZ)))
    highest = jnp.log(jnp.float32(8.0 / (256.0 * CZ * CZ)))
    return jnp.exp(lowest + uniform_draw * (highest - lowest))


def draw_layer_term(key, part):
    return layer_values(key)


def draw_block_inverse(key, part):
    layered = layer_values(key).reshape(NZ // CZ, CZ)
    identity_mat = jnp.eye(CZ, dtype=jnp.float32)
    neighbours = jnp.eye(CZ, k=1, dtype=jnp.float32) + jnp.eye(CZ, k=-1, dtype=jnp.float32)
    matrices = layered[:, :, None] * identity_mat + 2.0 * identity_mat - neighbours
    return jnp.linalg.inv(matrices).reshape(NZ, CZ)


def scaled_values(key, shape_full):
    level = 0.5 / float(NZ)
    values = jax.random.truncated_normal(key, -6.0, 6.0, shape_full, jnp.float32)
    return values * level


def draw_fields_h(key, part):
    key = jax.random.fold_in(key, 5)
    return scaled_values(key, (SRCS, 3, X, Y, NZ))


def draw_zsheet(key, part):
    key = jax.random.fold_in(key, 7)
    return scaled_values(key, (NZ,))


def place_ends(entries, stream_key, least, top_value):
    dims = entries.shape
    spot = [jax.random.randint(jax.random.fold_in(stream_key, axis), (), 0, dims[axis]) for axis in range(len(dims))]
    entries = entries.at[tuple(spot)].set(least)
    longest = dims.index(max(dims))
    spot[longest] = (spot[longest] + 1) % dims[longest]
    return entries.at[tuple(spot)].set(top_value)


def levels(rng, shape, shards, low, largest):
    level, own = 1.0, jax.random.fold_in(rng, 6)
    for axis_at, blocks in shards:
        heights = jnp.exp(jax.random.uniform(jax.random.fold_in(own, axis_at), (blocks,), jnp.float32, low / len(shards), largest / len(shards)))
        level = level * jnp.repeat(heights, shape[axis_at] // blocks).reshape([-1 if axis == axis_at else 1 for axis in range(len(shape))])
    return level


def scatter_about(own_key, extent, spread, reach, shards=(), kind=jnp.bfloat16):
    array = spread * jax.random.normal(own_key, extent, jnp.float32)
    if shards:
        array = array * levels(own_key, extent, shards, -0.22, 0.18)
    return jnp.clip(array, -reach, reach).astype(kind)


def setup_inputs(seed: int = 0) -> dict:
    splits = jax.random.split(jax.random.key(seed), 12)
    fields_e = scatter_about(splits[0], (SRCS, 3, X, Y, NZ), 2.0, 12.0, ((0, 4), (4, 32)), jnp.float32)
    fields_h = draw_fields_h(jax.random.fold_in(splits[11], 71), 0)
    cot_e = scatter_about(splits[2], (SRCS, 3, X, Y, NZ), 1.0, 6.0, ((0, 4), (4, 32)), jnp.float32)
    cot_h = scatter_about(splits[3], (SRCS, 3, X, Y, NZ), 1.0, 6.0, ((0, 4), (4, 32)), jnp.float32)
    labels = place_ends(jax.random.randint(splits[4], (X, Y, NZ), 0, REGIONS), jax.random.fold_in(splits[4], 1), 0, REGIONS - 1).astype(jnp.int32)
    region_eps = jnp.clip(jnp.exp(jax.random.uniform(splits[5], (REGIONS,), jnp.float32, math.log(1.0), math.log(12.0))), 1.0, 12.0)
    angle_index = place_ends(jax.random.randint(splits[6], (SRCS,), 0, ANGLES), jax.random.fold_in(splits[6], 1), 0, ANGLES - 1).astype(jnp.int32)
    profiles = scatter_about(splits[7], (ANGLES, 2, X, Y), 1.0, 6.0, (), jnp.float32)
    zsheet = draw_zsheet(jax.random.fold_in(splits[11], 71), 0)
    layer_term = draw_layer_term(jax.random.fold_in(splits[11], 71), 0)
    block_inverse = draw_block_inverse(jax.random.fold_in(splits[11], 71), 0)
    return dict(fields_e=fields_e, fields_h=fields_h, cot_e=cot_e, cot_h=cot_h, labels=labels, region_eps=region_eps, angle_index=angle_index, profiles=profiles, zsheet=zsheet, layer_term=layer_term, block_inverse=block_inverse)


HIGH = lax.Precision.HIGHEST

def step_up(values, axis_id):
    axis_id = axis_id % values.ndim
    length = values.shape[axis_id]
    tail = lax.slice_in_dim(values, 1, length, axis=axis_id)
    zero_rim = jnp.zeros_like(lax.slice_in_dim(values, 0, 1, axis=axis_id))
    return jnp.concatenate([tail, zero_rim], axis_id) - values

def step_down(values, axis_id):
    axis_id = axis_id % values.ndim
    length = values.shape[axis_id]
    head = lax.slice_in_dim(values, 0, length - 1, axis=axis_id)
    zero_rim = jnp.zeros_like(lax.slice_in_dim(values, 0, 1, axis=axis_id))
    return values - jnp.concatenate([zero_rim, head], axis_id)

def chain_terms(corners):

    def advance(q_carry, corner_row):
        denom = 1.0 - corner_row[0] * q_carry
        q_next = corner_row[3] + corner_row[1] * q_carry * corner_row[2] / denom
        return (q_next, (q_carry, denom))
    unused, (q_prev, denom) = lax.scan(advance, jnp.zeros((), corners.dtype), corners)
    return (q_prev, denom)

def reduced_sweeps(first_vals, last_vals, corners, q_prev, denom):
    shape_tail = (1,) * (first_vals.ndim - 1)
    q_col = q_prev.reshape((-1,) + shape_tail)
    d_col = denom.reshape((-1,) + shape_tail)
    v_first = corners[:, 0].reshape((-1,) + shape_tail)
    v_last = corners[:, 1].reshape((-1,) + shape_tail)
    w_first = corners[:, 2].reshape((-1,) + shape_tail)
    mult = jnp.broadcast_to(v_last / d_col, first_vals.shape)
    offset = last_vals + v_last * q_col / d_col * first_vals

    def sweep_up(p_carry, inputs):
        return (inputs[1] + inputs[0] * p_carry, p_carry)
    unused, p_prev = lax.scan(sweep_up, jnp.zeros(first_vals.shape[1:], first_vals.dtype), (mult, offset))
    gain = (first_vals + v_first * p_prev) / d_col
    slope = jnp.broadcast_to(w_first / d_col, first_vals.shape)

    def sweep_down(t_carry, inputs):
        return (inputs[1] + inputs[0] * t_carry, t_carry)
    unused2, t_next = lax.scan(sweep_down, jnp.zeros(first_vals.shape[1:], first_vals.dtype), (slope, gain), reverse=True)
    return (p_prev, t_next, gain, slope, q_col)

def solve_lines(rhs, block_inverse):
    blocks = NZ // CZ
    lead = rhs.shape[:-1]
    pieces = rhs.reshape(lead + (blocks, CZ))
    inverse = block_inverse.reshape(blocks, CZ, CZ)
    local = jnp.einsum('...bz,bwz->...bw', pieces, inverse, precision=HIGH)
    corners = jnp.stack([inverse[:, 0, 0], inverse[:, -1, 0], inverse[:, 0, -1], inverse[:, -1, -1]], -1)
    q_prev, denom = chain_terms(corners)
    first_vals = jnp.moveaxis(local[..., 0], -1, 0)
    last_vals = jnp.moveaxis(local[..., -1], -1, 0)
    p_prev, t_next, gain, slope, q_col = reduced_sweeps(first_vals, last_vals, corners, q_prev, denom)
    t_self = gain + slope * t_next
    b_prev = p_prev + q_col * t_self
    b_prev = jnp.moveaxis(b_prev, 0, -1)
    t_next = jnp.moveaxis(t_next, 0, -1)
    solved = local + inverse[:, :, 0] * b_prev[..., None] + inverse[:, :, -1] * t_next[..., None]
    return solved.reshape(lead + (NZ,))

def reference(fields_e, fields_h, cot_e, cot_h, labels, region_eps, angle_index, profiles, zsheet, layer_term, block_inverse):
    permit = jnp.zeros(labels.shape, jnp.float32)
    for region in range(REGIONS):
        permit = permit + jnp.where(labels == region, region_eps[region], jnp.float32(0.0))
    inv_eps = 1.0 / permit
    chosen = profiles[angle_index]
    current = chosen[..., None] * zsheet
    e_x, e_y, e_z = (fields_e[:, 0], fields_e[:, 1], fields_e[:, 2])
    h_x, h_y, h_z = (fields_h[:, 0], fields_h[:, 1], fields_h[:, 2])
    g_ex, g_ey, g_ez = (cot_e[:, 0], cot_e[:, 1], cot_e[:, 2])
    g_hx, g_hy, g_hz = (cot_h[:, 0], cot_h[:, 1], cot_h[:, 2])
    p_x = step_down(h_z, -2) - step_down(h_y, -1) - current[:, 0]
    p_y = step_down(h_x, -1) - step_down(h_z, -3) - current[:, 1]
    rhs_x = layer_term * e_x + inv_eps * p_x
    rhs_y = layer_term * e_y + inv_eps * p_y
    scaled_gez = inv_eps * g_ez
    bar_hy = g_hy - step_up(scaled_gez, -3)
    bar_hx = g_hx + step_up(scaled_gez, -2)
    adj_x = g_ex - step_down(g_hz, -2) - step_down(bar_hy, -1)
    adj_y = g_ey + step_down(g_hz, -3) - step_down(bar_hx, -1)
    solved = solve_lines(jnp.stack([rhs_x, rhs_y, adj_x, adj_y], 1), block_inverse)
    new_ex, new_ey, lam_x, lam_y = (solved[:, 0], solved[:, 1], solved[:, 2], solved[:, 3])
    new_hy = h_y + step_up(new_ex, -1) - step_up(e_z, -3)
    new_hx = h_x + step_up(new_ey, -1) - step_up(e_z, -2)
    curl_z = step_down(new_hy, -3) - step_down(new_hx, -2)
    new_ez = e_z + inv_eps * curl_z
    new_hz = h_z - step_up(new_ey, -3) + step_up(new_ex, -2)
    grad_terms = g_ez * curl_z + lam_x * p_x + lam_y * p_y
    eps_grad = -inv_eps * inv_eps * jnp.sum(grad_terms, 0)
    e_new = jnp.stack([new_ex, new_ey, new_ez], 1)
    h_new = jnp.stack([new_hx, new_hy, new_hz], 1)
    return (e_new, h_new, eps_grad)
```

```python
import jax
import jax.numpy as jnp
from jax import lax
from jax.experimental import pallas as pl
from jax.experimental.pallas import tpu as pltpu
from jax.sharding import PartitionSpec as P

F32 = jnp.float32
BF = jnp.bfloat16
X, Y, CZ = 8, 256, 128
NN = (((1,), (0,)), ((), ()))
NT = (((1,), (1,)), ((), ()))
SLABS = 17
LIMIT = 40 * 1024 * 1024


def split(v):
    one = v.astype(BF)
    rest = v - one.astype(F32)
    two = rest.astype(BF)
    three = (rest - two.astype(F32)).astype(BF)
    return one, two, three


def mm(a, b, dims=NN):
    return lax.dot_general(a, b, dims, preferred_element_type=F32)


def iota(shape, axis):
    return lax.broadcasted_iota(jnp.int32, shape, axis)


def y_down(v):
    return v - jnp.where(iota(v.shape, 0) == 0, 0.0, pltpu.roll(v, 1, 0))


def y_up(v):
    n = v.shape[0]
    return jnp.where(iota(v.shape, 0) == n - 1, 0.0, pltpu.roll(v, n - 1, 0)) - v


def z_down(v):
    return v - jnp.where(iota(v.shape, 1) == 0, 0.0, pltpu.roll(v, 1, 1))


def z_up(v):
    n = v.shape[1]
    return jnp.where(iota(v.shape, 1) == n - 1, 0.0, pltpu.roll(v, n - 1, 1)) - v


def inverse_eps(labels, eps_ref):
    rows = [1.0 / jnp.full((1, CZ), eps_ref[r], F32) for r in range(4)]
    out = jnp.where(labels == 2, rows[2], rows[3])
    out = jnp.where(labels == 1, rows[1], out)
    return jnp.where(labels == 0, rows[0], out)


def six_rows(rows):
    one, two, three = (part.astype(F32) for part in split(rows))
    return [one, two, three, one, two, one]


def six_table(line, piece):
    one, two, three = (part.astype(F32) for part in split(line))
    return jnp.where(piece < 3, one, jnp.where(piece < 5, two, three))


def rhs_kernel(
    angle, eps, e, h, ge, gh, lab, ge_next, lab_next, prof, zs, lt, w,
    rx_o, ry_o, ax_o, ay_o, psx_o, psy_o, keep_o, send_o,
    hz_s, ghz_s, prof_s,
):
    i = pl.program_id(0)
    core = lax.rem(lax.axis_index("gz"), 2)

    @pl.when(i == 0)
    def _():
        hz_s[...] = jnp.zeros_like(hz_s)
        ghz_s[...] = jnp.zeros_like(ghz_s)
        a = angle[0]
        both = jnp.concatenate([prof[a, 0], prof[a, 1]], 0)
        rows = jnp.concatenate(six_rows(both) + [jnp.zeros((32, Y), F32)], 0)
        prof_s[...] = rows.T.astype(BF)
        for row, (p, q) in enumerate(((0, 0), (0, CZ - 1), (CZ - 1, CZ - 1))):
            corner = jnp.broadcast_to(w[p:p + 1, q:q + 1], (1, CZ))
            keep_o[16, row:row + 1, :] = corner
            send_o[16, row:row + 1, :] = corner
        keep_o[16, 3:8, :] = jnp.zeros((5, CZ), F32)
        send_o[16, 3:8, :] = jnp.zeros((5, CZ), F32)

    row16 = iota((16, CZ), 0)
    lane16 = iota((16, CZ), 1)
    ends = jnp.where(row16 < 8, w[0:1, :], w[CZ - 1:CZ, :])
    ends_parts = [part.astype(F32) for part in split(ends)]
    slot = lax.rem(row16, 8)

    rowz = iota((CZ, CZ), 0)
    piece, within = rowz // 16, lax.rem(rowz, 16)
    z_table = jnp.where(piece < 6, six_table(zs[...], piece), 0.0)

    lane = iota((Y, CZ), 1)
    inv0 = inverse_eps(lab[0], eps)
    inv1 = inverse_eps(lab[1], eps)
    inv2 = inverse_eps(lab_next[0], eps)
    more = (i < 3).astype(F32)
    sg = [inv0 * ge[2, 0], inv1 * ge[2, 1], inv2 * ge_next[0, 0] * more]
    inv = [inv0, inv1]
    acc_ends = jnp.zeros((16, Y), F32)
    acc_tops = jnp.zeros((16, Y), F32)
    for j in range(2):
        x = 2 * i + j
        z_pick = jnp.concatenate(
            [jnp.where(within == x, z_table, 0.0), jnp.where(within == 8 + x, z_table, 0.0)], 1
        ).astype(BF)
        cur = mm(prof_s[...], z_pick)
        h_x, h_y, h_z = h[0, j], h[1, j], h[2, j]
        hz_prev = hz_s[...] if j == 0 else h[2, 0]
        ghz_prev = ghz_s[...] if j == 0 else gh[2, 0]
        g_hz = gh[2, j]
        bar_hy = gh[1, j] - (sg[j + 1] - sg[j])
        bar_hx = gh[0, j] + y_up(sg[j])
        p_x = y_down(h_z) - z_down(h_y) - cur[:, :CZ]
        p_y = z_down(h_x) - (h_z - hz_prev) - cur[:, CZ:]
        r_x = lt[...] * e[0, j] + inv[j] * p_x
        r_y = lt[...] * e[1, j] + inv[j] * p_y
        a_x = ge[0, j] - y_down(g_hz) - z_down(bar_hy)
        a_y = ge[1, j] + (g_hz - ghz_prev) - z_down(bar_hx)
        scale = -inv[j] * inv[j]
        rx_o[j], ry_o[j], ax_o[j], ay_o[j] = r_x, r_y, a_x, a_y
        psx_o[j] = scale * p_x
        psy_o[j] = scale * p_y

        thirds = []
        for c, field in enumerate((r_x, r_y, a_x, a_y)):
            one, two, three = split(field)
            mask = slot == 4 * j + c
            w1, w2, w3 = (jnp.where(mask, part, 0.0) for part in ends_parts)
            lhs = jnp.concatenate(
                [
                    jnp.concatenate([w1, w1], 1),
                    jnp.concatenate([w2, w2], 1),
                    jnp.concatenate([w3, jnp.zeros_like(w3)], 1),
                ],
                0,
            ).astype(BF)
            out = mm(lhs, jnp.concatenate([one, two], 1), NT)
            acc_ends += out[0:16] + out[16:32] + out[32:48]
            thirds.append((w1, three))
        for c in (0, 2):
            (wa, ta), (wb, tb) = thirds[c], thirds[c + 1]
            lhs = jnp.concatenate([wa, wb], 1).astype(BF)
            acc_ends += mm(lhs, jnp.concatenate([ta, tb], 1), NT)

        packed = jnp.where(lane == CZ - 1, h_y, inv[j])
        packed = jnp.where(lane == CZ - 2, -pltpu.roll(h_x, CZ - 1, 1), packed)
        packed = jnp.where(lane == CZ - 3, pltpu.roll(bar_hy, CZ - 2, 1), packed)
        packed = jnp.where(lane == CZ - 4, pltpu.roll(bar_hx, CZ - 3, 1), packed)
        one, two, three = split(packed)
        c16 = slot - 4 * j
        own = (c16 >= 0) & (c16 < 4)
        pick = jnp.where(
            own & (row16 < 8) & (lane16 == CZ - 1 - c16), 1.0,
            jnp.where(own & (row16 >= 8) & (c16 < 2) & (lane16 == 0), 1.0, 0.0),
        )
        acc_tops += mm(jnp.concatenate([pick, pick], 1).astype(BF), jnp.concatenate([one, two], 1), NT)
        acc_tops += mm(pick.astype(BF), three, NT)

    row_y = iota((16, Y), 0)
    acc_tops = jnp.where((row_y >= 8) & (lax.rem(row_y, 4) >= 2), 1.0, acc_tops)
    hz_s[...] = h[2, 1]
    ghz_s[...] = gh[2, 1]
    for base, acc in ((0, acc_ends), (8, acc_tops)):
        low, high = acc[:, :CZ], acc[:, CZ:]
        keep = jnp.where(core == 0, low, high)
        send = jnp.where(core == 0, high, low)
        for part in range(2):
            keep_o[base + 4 * part + i] = keep[8 * part:8 * part + 8]
            send_o[base + 4 * part + i] = send[8 * part:8 * part + 8]


def unpack(ref):
    m = ref[...]
    return dict(
        f=m[0:4], l=m[4:8], t=m[8:12], k=m[12:16],
        a=m[16, 0:1, :], c=m[16, 1:2, :], z=m[16, 2:3, :],
    )


def repack(s, ref):
    ref[0:4] = s["f"]
    ref[4:8] = s["l"]
    ref[8:12] = s["t"]
    ref[12:16] = s["k"]
    ref[16] = jnp.concatenate([s["a"], s["c"], s["z"], jnp.zeros((5, CZ), F32)], 0)


def order(bit, own, other):
    lower = {n: jnp.where(bit == 0, own[n], other[n]) for n in own}
    upper = {n: jnp.where(bit == 0, other[n], own[n]) for n in own}
    return lower, upper


def coupled(lower, upper):
    delta = upper["k"] * lower["t"]
    f_up = upper["f"] + upper["a"] * delta
    l_up = upper["l"] + upper["c"] * delta
    inv = 1.0 / (1.0 - upper["a"] * lower["z"])
    return f_up, l_up, inv


def combine(lower, upper):
    f_up, l_up, inv = coupled(lower, upper)
    t = (f_up + upper["a"] * lower["l"]) * inv
    u = (lower["l"] + lower["z"] * f_up) * inv
    return dict(
        f=lower["f"] + lower["c"] * t,
        l=l_up + upper["c"] * u,
        t=upper["t"],
        k=lower["k"],
        a=lower["a"] + lower["c"] * lower["c"] * upper["a"] * inv,
        c=lower["c"] * upper["c"] * inv,
        z=upper["z"] + upper["c"] * upper["c"] * lower["z"] * inv,
    )


def outside(lower, upper, below, above):
    f_up, _, inv = coupled(lower, upper)
    l_low = lower["l"] + lower["c"] * below
    f_up = f_up + upper["c"] * above
    return (f_up + upper["a"] * l_low) * inv, (l_low + lower["z"] * f_up) * inv


def pick_outside(bit, lower, upper, below, above):
    t, u = outside(lower, upper, below, above)
    return jnp.where(bit == 0, below, u), jnp.where(bit == 0, t, above)


def bits():
    gz = lax.axis_index("gz")
    core, low_z, high_z = lax.rem(gz, 2), lax.rem(gz // 2, 2), lax.rem(gz // 4, 2)
    return core, low_z, high_z, lax.rem(gz // 8, 2), gz // 16


def chip_kernel(own, other, out):
    core = bits()[0]
    repack(combine(*order(core, unpack(own), unpack(other))), out)


def four(low, high, own, m1, m2, m3):
    first = order(low, own, m1)
    pair = combine(*first)
    return first, order(high, pair, combine(*order(low, m2, m3)))


def group_kernel(m0, m1, m2, m3, out):
    _, low, high, _, _ = bits()
    repack(combine(*four(low, high, *(unpack(m) for m in (m0, m1, m2, m3)))[1]), out)


def back_kernel(a0, a1, m0, m1, m2, m3, n0, n1, n2, n3, keep_o, send_o):
    core, zl, zh, xl, xh = bits()
    chip = order(core, unpack(a0), unpack(a1))
    m0, m1, m2, m3 = (unpack(m) for m in (m0, m1, m2, m3))
    n0, n1, n2, n3 = (unpack(n) for n in (n0, n1, n2, n3))
    z_first, z_second = four(zl, zh, m0, m1, m2, m3)
    x_first, x_second = four(xl, xh, n0, n1, n2, n3)
    zero = jnp.zeros_like(m0["f"])
    edge = (zero, zero)
    edge = pick_outside(xh, *x_second, *edge)
    edge = pick_outside(xl, *x_first, *edge)
    edge = pick_outside(zh, *z_second, *edge)
    edge = pick_outside(zl, *z_first, *edge)
    lower, upper = chip
    t, u = outside(lower, upper, *edge)
    under_x = jnp.where(xl == 1, n1["t"], jnp.where(xh == 1, n3["t"], zero))
    under = jnp.where(zl == 1, m1["t"], jnp.where(zh == 1, m3["t"], under_x))
    results = []
    for block, below, above, plane in ((lower, edge[0], t, under), (upper, u, edge[1], lower["t"])):
        below = below + block["k"] * plane
        first = block["f"] + block["a"] * below + block["c"] * above
        extra = jnp.stack([first[q] * pltpu.roll(plane[q], 2, 0) for q in range(4)])
        results.append((below, above, extra))
    for part in range(3):
        low, high = results[0][part], results[1][part]
        keep_o[4 * part:4 * part + 4] = jnp.where(core == 0, low, high)
        send_o[4 * part:4 * part + 4] = jnp.where(core == 0, high, low)


def product_tables(w):
    one, two, three = split(w.T)
    full = jnp.concatenate([one, two], 1)
    return jnp.concatenate([full, full], 0), jnp.concatenate([one, three], 0)


def product(field, tables):
    one, two, three = split(field)
    wide = mm(jnp.concatenate([one, two], 1), tables[0])
    narrow = mm(jnp.concatenate([three, one], 1), tables[1])
    return wide[:, :CZ] + wide[:, CZ:] + narrow


def adjoint_kernel(ax, ay, psx, psy, w, out):
    tables = product_tables(w[...])
    for j in range(2):
        out[j] = psx[j] * product(ax[j], tables) + psy[j] * product(ay[j], tables)


def primal_kernel(eps, rx, ry, h, ez, ez_next, gez, lab, part, w, ex_o, ey_o, grad_o, hy_s):
    i = pl.program_id(0)

    @pl.when(i == 0)
    def _():
        hy_s[...] = jnp.zeros_like(hy_s)

    tables = product_tables(w[...])
    more = (i < 3).astype(F32)
    up = [ez[0, 0], ez[0, 1], ez_next[0, 0] * more]
    hy_prev = hy_s[...]
    for j in range(2):
        e_x, e_y = product(rx[j], tables), product(ry[j], tables)
        ex_o[j], ey_o[j] = e_x, e_y
        hy = h[1, j] + z_up(e_x) - (up[j + 1] - up[j])
        hx = h[0, j] + z_up(e_y) - y_up(up[j])
        curl = hy - hy_prev - y_down(hx)
        hy_prev = hy
        inv = inverse_eps(lab[j], eps)
        grad_o[j] = part[j] - inv * inv * gez[0, j] * curl
    hy_s[...] = hy_prev


def edge_rows(keep, recv, slab):
    core = lax.rem(lax.axis_index("gz"), 2)
    a, b = keep[slab], recv[slab]
    return jnp.concatenate([jnp.where(core == 0, a, b), jnp.where(core == 0, b, a)], 1)


def columns(below, above):
    rows = six_rows(below) + six_rows(above) + [jnp.zeros((32, Y), F32)]
    return jnp.concatenate(rows, 0).T.astype(BF)


def edge_table(first, last):
    piece = iota((CZ, CZ), 0) // 8
    table = jnp.where(piece < 6, six_table(first, piece), six_table(last, piece - 6))
    return jnp.where(piece < 12, table, 0.0)


def picked(table, row):
    return jnp.where(lax.rem(iota((CZ, CZ), 0), 8) == row, table, 0.0)


def gradient_kernel(k, eps, grad, psx, psy, gez, lab, keep, recv, w, out):
    q = lax.axis_index("src") ^ k
    below, above, extra = (edge_rows(keep, recv, 4 * part + q) for part in range(3))
    before = jnp.maximum(q - 1, 0)
    has = (q > 0).astype(F32)
    row = iota((8, Y), 0)
    lane = iota((8, Y), 1)

    def curl_rows(now, previous):
        shifted = jnp.where(row < 4, pltpu.roll(previous, 4, 0), pltpu.roll(now, 4, 0))
        along_y = now - jnp.where(lane == 0, 0.0, pltpu.roll(now, 1, 1))
        return now - shifted - pltpu.roll(along_y, 7, 0)

    curl_below = curl_rows(below, edge_rows(keep, recv, before) * has)
    curl_above = curl_rows(above, edge_rows(keep, recv, 4 + before) * has)
    kind = lax.rem(row, 4)
    plane = pltpu.roll(extra, 7, 0) + pltpu.roll(extra, 6, 0)
    below = jnp.where(kind == 0, curl_below, jnp.where(kind == 1, plane, below))
    above = jnp.where(kind == 0, curl_above, jnp.where(kind == 1, 0.0, above))
    cols = columns(below, above)
    wt = w[...].T
    first, last = wt[0:1, :], wt[CZ - 1:CZ, :]
    lane1 = iota((1, CZ), 1)
    top = jnp.where(lane1 == CZ - 1, 1.0, 0.0)
    first_up = jnp.where(lane1 == CZ - 1, 0.0, pltpu.roll(first, CZ - 1, 1)) - first
    last_up = jnp.where(lane1 == CZ - 1, 0.0, pltpu.roll(last, CZ - 1, 1)) - last + top
    lam_table = edge_table(first, last)
    curl_table = edge_table(first_up, last_up)
    plane_table = edge_table(jnp.where(lane1 == 0, 1.0, 0.0), jnp.zeros((1, CZ), F32))
    for j in range(2):
        r = 4 * j
        lam = mm(cols, jnp.concatenate([picked(lam_table, r + 2), picked(lam_table, r + 3)], 1).astype(BF))
        rest = mm(cols, jnp.concatenate([picked(curl_table, r), picked(plane_table, r + 1)], 1).astype(BF))
        inv = inverse_eps(lab[j], eps)
        out[j] = (
            grad[j] + psx[j] * lam[:, :CZ] + psy[j] * lam[:, CZ:]
            - inv * inv * (gez[0, j] * rest[:, :CZ] + rest[:, CZ:])
        )


def output_kernel(eps, ex, ey, ey_next, h, ez, ez_next, lab, keep, recv, w, e_o, h_o, hy_s):
    i = pl.program_id(0)

    @pl.when(i == 0)
    def _():
        hy_s[...] = jnp.zeros_like(hy_s)

    more = (i < 3).astype(F32)
    following = jnp.minimum(i + 1, 3)
    below, above = edge_rows(keep, recv, i), edge_rows(keep, recv, 4 + i)
    wt = w[...].T
    table = edge_table(wt[0:1, :], wt[CZ - 1:CZ, :])
    cols = columns(below, above)
    cols_next = columns(edge_rows(keep, recv, following), edge_rows(keep, recv, 4 + following))

    def corrected(source, j, comp):
        return mm(source, picked(table, 4 * j + comp).astype(BF))

    lane = iota((CZ, CZ), 1)
    piece = iota((CZ, CZ), 0) // 8
    ones = jnp.where((piece >= 6) & (piece < 9) & (lane == CZ - 1), 1.0, 0.0)

    def up(v, j, comp):
        return z_up(v) + mm(cols, picked(ones, 4 * j + comp).astype(BF))

    e_x = [ex[j] + corrected(cols, j, 0) for j in range(2)]
    e_y = [ey[j] + corrected(cols, j, 1) for j in range(2)]
    e_y.append((ey_next[0] + corrected(cols_next, 0, 1)) * more)
    e_z = [ez[0, 0], ez[0, 1], ez_next[0, 0] * more]
    hy_prev = hy_s[...]
    for j in range(2):
        hy = h[1, j] + up(e_x[j], j, 0) - (e_z[j + 1] - e_z[j])
        hx = h[0, j] + up(e_y[j], j, 1) - y_up(e_z[j])
        curl = hy - hy_prev - y_down(hx)
        hy_prev = hy
        e_o[0, j] = e_x[j]
        e_o[1, j] = e_y[j]
        e_o[2, j] = e_z[j] + inverse_eps(lab[j], eps) * curl
        h_o[0, j] = hx
        h_o[1, j] = hy
        h_o[2, j] = h[2, j] - (e_y[j + 1] - e_y[j]) + y_up(e_x[j])
    hy_s[...] = hy_prev


def place_kernel(g0, g1, g2, g3, out, sems):
    src = lax.axis_index("src")
    copies = []
    for k, g in enumerate((g0, g1, g2, g3)):
        copies.append(pltpu.make_async_copy(g, out.at[pl.ds(2 * (src ^ k), 2)], sems.at[k]))
    for copy in copies:
        copy.start()
    for copy in copies:
        copy.wait()


def swap(block, axis, mask):
    return lax.ppermute(block, axis, [(i, i ^ mask) for i in range(lax.axis_size(axis))])


SMEM = pl.BlockSpec(memory_space=pltpu.SMEM)
WHOLE = pl.BlockSpec(memory_space=pltpu.VMEM)
ANY = pl.BlockSpec(memory_space=pl.ANY)


def shape(*dims):
    return jax.ShapeDtypeStruct(dims, F32)


def cost(us):
    return pl.CostEstimate(flops=1000, bytes_accessed=int(us * 3.0e6), transcendentals=0)


def params(limit=LIMIT):
    return pltpu.CompilerParams(vmem_limit_bytes=limit)


def body(
    fields_e, fields_h, cot_e, cot_h, labels, region_eps, angle_index, profiles, zsheet,
    layer_term, block_inverse,
):
    e, h, ge, gh = fields_e[0], fields_h[0], cot_e[0], cot_h[0]
    w = block_inverse
    zs, lt = zsheet.reshape(1, CZ), layer_term.reshape(1, CZ)

    pair = pl.BlockSpec((2, Y, CZ), lambda i: (i, 0, 0))

    def comps(n, index=0):
        return pl.BlockSpec((n, 2, Y, CZ), lambda i: (index, i, 0, 0))

    def const(*dims):
        return pl.BlockSpec(dims, lambda i: (0,) * len(dims))

    z_next = pl.BlockSpec((1, 1, Y, CZ), lambda i: (2, jnp.minimum(2 * i + 2, 7), 0, 0))
    x_next = pl.BlockSpec((1, Y, CZ), lambda i: (jnp.minimum(2 * i + 2, 7), 0, 0))
    slab = shape(X, Y, CZ)
    message = shape(SLABS, 8, CZ)

    rx, ry, ax, ay, psx, psy, keep, send = pl.pallas_call(
        rhs_kernel,
        grid=(4,),
        in_specs=[
            SMEM, SMEM, comps(2), comps(3), comps(3), comps(3), pair, z_next, x_next,
            const(8, 2, X, Y), const(1, CZ), const(1, CZ), const(CZ, CZ),
        ],
        out_specs=[pair] * 6 + [const(SLABS, 8, CZ)] * 2,
        out_shape=[slab] * 6 + [message] * 2,
        scratch_shapes=[pltpu.VMEM((Y, CZ), F32), pltpu.VMEM((Y, CZ), F32), pltpu.VMEM((Y, CZ), BF)],
        compiler_params=params(),
        cost_estimate=cost(6),
        name="right_hand_sides",
    )(angle_index, region_eps, e, h, ge, gh, labels, ge, labels, profiles, zs, lt, w)

    def small(kernel, name, n_in, outs):
        return pl.pallas_call(
            kernel, in_specs=[WHOLE] * n_in, out_specs=[WHOLE] * len(outs), out_shape=outs,
            compiler_params=params(), cost_estimate=cost(0.5), name=name,
        )

    other = swap(send, "gz", 1)
    (m0,) = small(chip_kernel, "chip", 2, [message])(keep, other)
    m1, m2, m3 = (swap(m0, "gz", 2 * k) for k in (1, 2, 3))

    adjoint = pl.pallas_call(
        adjoint_kernel,
        grid=(4,),
        in_specs=[pair] * 4 + [const(CZ, CZ)],
        out_specs=pair,
        out_shape=slab,
        compiler_params=params(),
        cost_estimate=cost(3),
        name="adjoint_products",
    )(ax, ay, psx, psy, w)

    (n0,) = small(group_kernel, "group", 4, [message])(m0, m1, m2, m3)
    n1, n2, n3 = (swap(n0, "gz", 8 * k) for k in (1, 2, 3))

    ex, ey, grad = pl.pallas_call(
        primal_kernel,
        grid=(4,),
        in_specs=[
            SMEM, pair, pair, comps(2), comps(1, 2), z_next, comps(1, 2), pair, pair, const(CZ, CZ),
        ],
        out_specs=[pair] * 3,
        out_shape=[slab] * 3,
        scratch_shapes=[pltpu.VMEM((Y, CZ), F32)],
        compiler_params=params(),
        cost_estimate=cost(4),
        name="primal_products",
    )(region_eps, rx, ry, h, e, e, ge, labels, adjoint, w)

    edges = shape(12, 8, CZ)
    own_edges, send_edges = small(back_kernel, "back", 10, [edges] * 2)(
        keep, other, m0, m1, m2, m3, n0, n1, n2, n3
    )
    other_edges = swap(send_edges, "gz", 1)

    def gradient(k):
        def at(*tail):
            return lambda i: (lax.axis_index("src") ^ k,) + tail

        quarter = pl.BlockSpec((2, Y, CZ), at(0, 0))
        gez_quarter = pl.BlockSpec((1, 2, Y, CZ), lambda i: (2, lax.axis_index("src") ^ k, 0, 0))
        return pl.pallas_call(
            lambda *refs: gradient_kernel(k, *refs),
            grid=(1,),
            in_specs=[
                SMEM, quarter, quarter, quarter, gez_quarter, quarter,
                const(12, 8, CZ), const(12, 8, CZ), const(CZ, CZ),
            ],
            out_specs=const(2, Y, CZ),
            out_shape=shape(2, Y, CZ),
            compiler_params=params(),
            cost_estimate=cost(1),
            name=f"gradient_{k}",
        )(region_eps, grad, psx, psy, ge, labels, own_edges, other_edges, w)

    arrived = [swap(gradient(k), "src", k) for k in (2, 1, 3)]
    own = gradient(0)

    e_new, h_new = pl.pallas_call(
        output_kernel,
        grid=(4,),
        in_specs=[
            SMEM, pair, pair, x_next, comps(3), comps(1, 2), z_next, pair,
            const(12, 8, CZ), const(12, 8, CZ), const(CZ, CZ),
        ],
        out_specs=[comps(3), comps(3)],
        out_shape=[shape(3, X, Y, CZ)] * 2,
        scratch_shapes=[pltpu.VMEM((Y, CZ), F32)],
        compiler_params=params(),
        cost_estimate=cost(6),
        name="outputs",
    )(region_eps, ex, ey, ey, h, e, e, labels, own_edges, other_edges, w)

    total = own + arrived[0] + arrived[1] + arrived[2]
    two, one, three = (swap(total, "src", k) for k in (2, 1, 3))
    eps_grad = pl.pallas_call(
        place_kernel,
        in_specs=[ANY] * 4,
        out_specs=ANY,
        out_shape=slab,
        scratch_shapes=[pltpu.SemaphoreType.DMA((4,))],
        compiler_params=params(),
        cost_estimate=cost(1),
        name="place",
    )(total, one, two, three)
    return (e_new[None], h_new[None], eps_grad)


def solution(mesh):
    field = P("src", None, None, None, "gz")
    return jax.shard_map(
        body,
        mesh=mesh,
        in_specs=(
            field, field, field, field, P(None, None, "gz"), P(), P("src"), P(), P("gz"), P("gz"),
            P("gz", None),
        ),
        out_specs=(field, field, P(None, None, "gz")),
        check_vma=False,
    )
```

```python
import jax
import jax.numpy as jnp
from jax import lax
from jax.experimental import pallas as pl
from jax.experimental.pallas import tpu as pltpu
from jax.sharding import PartitionSpec as P

F32 = jnp.float32
BF = jnp.bfloat16
X, Y, CZ = 8, 256, 128
NN = (((1,), (0,)), ((), ()))
NT = (((1,), (1,)), ((), ()))
SLABS = 17
LIMIT = 40 * 1024 * 1024
BIG = 60 * 1024 * 1024


def split(v):
    one = v.astype(BF)
    rest = v - one.astype(F32)
    two = rest.astype(BF)
    three = (rest - two.astype(F32)).astype(BF)
    return one, two, three


def mm(a, b, dims=NN):
    return lax.dot_general(a, b, dims, preferred_element_type=F32)


def iota(shape, axis):
    return lax.broadcasted_iota(jnp.int32, shape, axis)


def y_down(v):
    return v - jnp.where(iota(v.shape, 0) == 0, 0.0, pltpu.roll(v, 1, 0))


def y_up(v):
    n = v.shape[0]
    return jnp.where(iota(v.shape, 0) == n - 1, 0.0, pltpu.roll(v, n - 1, 0)) - v


def z_down(v):
    return v - jnp.where(iota(v.shape, 1) == 0, 0.0, pltpu.roll(v, 1, 1))


def z_up(v):
    n = v.shape[1]
    return jnp.where(iota(v.shape, 1) == n - 1, 0.0, pltpu.roll(v, n - 1, 1)) - v


def inverse_eps(labels, eps_ref):
    rows = [1.0 / jnp.full((1, CZ), eps_ref[r], F32) for r in range(4)]
    out = jnp.where(labels == 2, rows[2], rows[3])
    out = jnp.where(labels == 1, rows[1], out)
    return jnp.where(labels == 0, rows[0], out)


def six_rows(rows):
    one, two, three = (part.astype(F32) for part in split(rows))
    return [one, two, three, one, two, one]


def six_table(line, piece):
    one, two, three = (part.astype(F32) for part in split(line))
    return jnp.where(piece < 3, one, jnp.where(piece < 5, two, three))


def rhs_kernel(
    angle, eps, e, h, ge, gh, lab, ge_next, lab_next, prof, zs, lt, w,
    rx_o, ry_o, ax_o, ay_o, psx_o, psy_o, keep_o, send_o,
    hz_s, ghz_s, prof_s,
):
    i = pl.program_id(0)
    core = lax.rem(lax.axis_index("gz"), 2)

    @pl.when(i == 0)
    def _():
        hz_s[...] = jnp.zeros_like(hz_s)
        ghz_s[...] = jnp.zeros_like(ghz_s)
        a = angle[0]
        both = jnp.concatenate([prof[a, 0], prof[a, 1]], 0)
        rows = jnp.concatenate(six_rows(both) + [jnp.zeros((32, Y), F32)], 0)
        prof_s[...] = rows.T.astype(BF)
        for row, (p, q) in enumerate(((0, 0), (0, CZ - 1), (CZ - 1, CZ - 1))):
            corner = jnp.broadcast_to(w[p:p + 1, q:q + 1], (1, CZ))
            keep_o[16, row:row + 1, :] = corner
            send_o[16, row:row + 1, :] = corner
        keep_o[16, 3:8, :] = jnp.zeros((5, CZ), F32)
        send_o[16, 3:8, :] = jnp.zeros((5, CZ), F32)

    row16 = iota((16, CZ), 0)
    lane16 = iota((16, CZ), 1)
    ends = jnp.where(row16 < 8, w[0:1, :], w[CZ - 1:CZ, :])
    ends_parts = [part.astype(F32) for part in split(ends)]
    slot = lax.rem(row16, 8)

    rowz = iota((CZ, CZ), 0)
    piece, within = rowz // 16, lax.rem(rowz, 16)
    z_table = jnp.where(piece < 6, six_table(zs[...], piece), 0.0)

    lane = iota((Y, CZ), 1)
    inv0 = inverse_eps(lab[0], eps)
    inv1 = inverse_eps(lab[1], eps)
    inv2 = inverse_eps(lab_next[0], eps)
    more = (i < 3).astype(F32)
    sg = [inv0 * ge[2, 0], inv1 * ge[2, 1], inv2 * ge_next[0, 0] * more]
    inv = [inv0, inv1]
    acc_ends = jnp.zeros((16, Y), F32)
    acc_tops = jnp.zeros((16, Y), F32)
    for j in range(2):
        x = 2 * i + j
        z_pick = jnp.concatenate(
            [jnp.where(within == x, z_table, 0.0), jnp.where(within == 8 + x, z_table, 0.0)], 1
        ).astype(BF)
        cur = mm(prof_s[...], z_pick)
        h_x, h_y, h_z = h[0, j], h[1, j], h[2, j]
        hz_prev = hz_s[...] if j == 0 else h[2, 0]
        ghz_prev = ghz_s[...] if j == 0 else gh[2, 0]
        g_hz = gh[2, j]
        bar_hy = gh[1, j] - (sg[j + 1] - sg[j])
        bar_hx = gh[0, j] + y_up(sg[j])
        p_x = y_down(h_z) - z_down(h_y) - cur[:, :CZ]
        p_y = z_down(h_x) - (h_z - hz_prev) - cur[:, CZ:]
        r_x = lt[...] * e[0, j] + inv[j] * p_x
        r_y = lt[...] * e[1, j] + inv[j] * p_y
        a_x = ge[0, j] - y_down(g_hz) - z_down(bar_hy)
        a_y = ge[1, j] + (g_hz - ghz_prev) - z_down(bar_hx)
        scale = -inv[j] * inv[j]
        rx_o[j], ry_o[j], ax_o[j], ay_o[j] = r_x, r_y, a_x, a_y
        psx_o[j] = scale * p_x
        psy_o[j] = scale * p_y

        thirds = []
        for c, field in enumerate((r_x, r_y, a_x, a_y)):
            one, two, three = split(field)
            mask = slot == 4 * j + c
            w1, w2, w3 = (jnp.where(mask, part, 0.0) for part in ends_parts)
            lhs = jnp.concatenate(
                [
                    jnp.concatenate([w1, w1], 1),
                    jnp.concatenate([w2, w2], 1),
                    jnp.concatenate([w3, jnp.zeros_like(w3)], 1),
                ],
                0,
            ).astype(BF)
            out = mm(lhs, jnp.concatenate([one, two], 1), NT)
            acc_ends += out[0:16] + out[16:32] + out[32:48]
            thirds.append((w1, three))
        for c in (0, 2):
            (wa, ta), (wb, tb) = thirds[c], thirds[c + 1]
            lhs = jnp.concatenate([wa, wb], 1).astype(BF)
            acc_ends += mm(lhs, jnp.concatenate([ta, tb], 1), NT)

        packed = jnp.where(lane == CZ - 1, h_y, inv[j])
        packed = jnp.where(lane == CZ - 2, -pltpu.roll(h_x, CZ - 1, 1), packed)
        packed = jnp.where(lane == CZ - 3, pltpu.roll(bar_hy, CZ - 2, 1), packed)
        packed = jnp.where(lane == CZ - 4, pltpu.roll(bar_hx, CZ - 3, 1), packed)
        one, two, three = split(packed)
        c16 = slot - 4 * j
        own = (c16 >= 0) & (c16 < 4)
        pick = jnp.where(
            own & (row16 < 8) & (lane16 == CZ - 1 - c16), 1.0,
            jnp.where(own & (row16 >= 8) & (c16 < 2) & (lane16 == 0), 1.0, 0.0),
        )
        acc_tops += mm(jnp.concatenate([pick, pick], 1).astype(BF), jnp.concatenate([one, two], 1), NT)
        acc_tops += mm(pick.astype(BF), three, NT)

    row_y = iota((16, Y), 0)
    acc_tops = jnp.where((row_y >= 8) & (lax.rem(row_y, 4) >= 2), 1.0, acc_tops)
    hz_s[...] = h[2, 1]
    ghz_s[...] = gh[2, 1]
    for base, acc in ((0, acc_ends), (8, acc_tops)):
        low, high = acc[:, :CZ], acc[:, CZ:]
        keep = jnp.where(core == 0, low, high)
        send = jnp.where(core == 0, high, low)
        for part in range(2):
            keep_o[base + 4 * part + i] = keep[8 * part:8 * part + 8]
            send_o[base + 4 * part + i] = send[8 * part:8 * part + 8]


def unpack(ref):
    m = ref[...]
    return dict(
        f=m[0:4], l=m[4:8], t=m[8:12], k=m[12:16],
        a=m[16, 0:1, :], c=m[16, 1:2, :], z=m[16, 2:3, :],
    )


def repack(s, ref):
    ref[0:4] = s["f"]
    ref[4:8] = s["l"]
    ref[8:12] = s["t"]
    ref[12:16] = s["k"]
    ref[16] = jnp.concatenate([s["a"], s["c"], s["z"], jnp.zeros((5, CZ), F32)], 0)


def order(bit, own, other):
    lower = {n: jnp.where(bit == 0, own[n], other[n]) for n in own}
    upper = {n: jnp.where(bit == 0, other[n], own[n]) for n in own}
    return lower, upper


def coupled(lower, upper):
    delta = upper["k"] * lower["t"]
    f_up = upper["f"] + upper["a"] * delta
    l_up = upper["l"] + upper["c"] * delta
    inv = 1.0 / (1.0 - upper["a"] * lower["z"])
    return f_up, l_up, inv


def combine(lower, upper):
    f_up, l_up, inv = coupled(lower, upper)
    t = (f_up + upper["a"] * lower["l"]) * inv
    u = (lower["l"] + lower["z"] * f_up) * inv
    return dict(
        f=lower["f"] + lower["c"] * t,
        l=l_up + upper["c"] * u,
        t=upper["t"],
        k=lower["k"],
        a=lower["a"] + lower["c"] * lower["c"] * upper["a"] * inv,
        c=lower["c"] * upper["c"] * inv,
        z=upper["z"] + upper["c"] * upper["c"] * lower["z"] * inv,
    )


def outside(lower, upper, below, above):
    f_up, _, inv = coupled(lower, upper)
    l_low = lower["l"] + lower["c"] * below
    f_up = f_up + upper["c"] * above
    return (f_up + upper["a"] * l_low) * inv, (l_low + lower["z"] * f_up) * inv


def pick_outside(bit, lower, upper, below, above):
    t, u = outside(lower, upper, below, above)
    return jnp.where(bit == 0, below, u), jnp.where(bit == 0, t, above)


def bits():
    gz = lax.axis_index("gz")
    core, low_z, high_z = lax.rem(gz, 2), lax.rem(gz // 2, 2), lax.rem(gz // 4, 2)
    return core, low_z, high_z, lax.rem(gz // 8, 2), gz // 16


def chip_kernel(own, other, out):
    core = bits()[0]
    repack(combine(*order(core, unpack(own), unpack(other))), out)


def four(low, high, own, m1, m2, m3):
    first = order(low, own, m1)
    pair = combine(*first)
    return first, order(high, pair, combine(*order(low, m2, m3)))


def group_kernel(m0, m1, m2, m3, after, out):
    _, low, high, _, _ = bits()
    repack(combine(*four(low, high, *(unpack(m) for m in (m0, m1, m2, m3)))[1]), out)


def back_kernel(a0, a1, m0, m1, m2, m3, n0, n1, n2, n3, after, keep_o, send_o):
    core, zl, zh, xl, xh = bits()
    chip = order(core, unpack(a0), unpack(a1))
    m0, m1, m2, m3 = (unpack(m) for m in (m0, m1, m2, m3))
    n0, n1, n2, n3 = (unpack(n) for n in (n0, n1, n2, n3))
    z_first, z_second = four(zl, zh, m0, m1, m2, m3)
    x_first, x_second = four(xl, xh, n0, n1, n2, n3)
    zero = jnp.zeros_like(m0["f"])
    edge = (zero, zero)
    edge = pick_outside(xh, *x_second, *edge)
    edge = pick_outside(xl, *x_first, *edge)
    edge = pick_outside(zh, *z_second, *edge)
    edge = pick_outside(zl, *z_first, *edge)
    lower, upper = chip
    t, u = outside(lower, upper, *edge)
    under_x = jnp.where(xl == 1, n1["t"], jnp.where(xh == 1, n3["t"], zero))
    under = jnp.where(zl == 1, m1["t"], jnp.where(zh == 1, m3["t"], under_x))
    results = []
    for block, below, above, plane in ((lower, edge[0], t, under), (upper, u, edge[1], lower["t"])):
        below = below + block["k"] * plane
        first = block["f"] + block["a"] * below + block["c"] * above
        extra = jnp.stack([first[q] * pltpu.roll(plane[q], 2, 0) for q in range(4)])
        results.append((below, above, extra))
    for part in range(3):
        low, high = results[0][part], results[1][part]
        keep_o[4 * part:4 * part + 4] = jnp.where(core == 0, low, high)
        send_o[4 * part:4 * part + 4] = jnp.where(core == 0, high, low)


def product_tables(w):
    one, two, three = split(w.T)
    full = jnp.concatenate([one, two], 1)
    return jnp.concatenate([full, full], 0), jnp.concatenate([one, three], 0)


def product(field, tables):
    one, two, three = split(field)
    wide = mm(jnp.concatenate([one, two], 1), tables[0])
    narrow = mm(jnp.concatenate([three, one], 1), tables[1])
    return wide[:, :CZ] + wide[:, CZ:] + narrow


def adjoint_kernel(ax, ay, psx, psy, w, after, out):
    tables = product_tables(w[...])
    for j in range(2):
        out[j] = psx[j] * product(ax[j], tables) + psy[j] * product(ay[j], tables)


def primal_kernel(eps, rx, ry, h, ez, ez_next, gez, lab, part, w, after, ex_o, ey_o, grad_o, hy_s):
    i = pl.program_id(0)

    @pl.when(i == 0)
    def _():
        hy_s[...] = jnp.zeros_like(hy_s)

    tables = product_tables(w[...])
    more = (i < 3).astype(F32)
    up = [ez[0, 0], ez[0, 1], ez_next[0, 0] * more]
    hy_prev = hy_s[...]
    for j in range(2):
        e_x, e_y = product(rx[j], tables), product(ry[j], tables)
        ex_o[j], ey_o[j] = e_x, e_y
        hy = h[1, j] + z_up(e_x) - (up[j + 1] - up[j])
        hx = h[0, j] + z_up(e_y) - y_up(up[j])
        curl = hy - hy_prev - y_down(hx)
        hy_prev = hy
        inv = inverse_eps(lab[j], eps)
        grad_o[j] = part[j] - inv * inv * gez[0, j] * curl
    hy_s[...] = hy_prev


def edge_rows(keep, recv, slab):
    core = lax.rem(lax.axis_index("gz"), 2)
    a, b = keep[slab], recv[slab]
    return jnp.concatenate([jnp.where(core == 0, a, b), jnp.where(core == 0, b, a)], 1)


def columns(below, above):
    rows = six_rows(below) + six_rows(above) + [jnp.zeros((32, Y), F32)]
    return jnp.concatenate(rows, 0).T.astype(BF)


def edge_table(first, last):
    piece = iota((CZ, CZ), 0) // 8
    table = jnp.where(piece < 6, six_table(first, piece), six_table(last, piece - 6))
    return jnp.where(piece < 12, table, 0.0)


def picked(table, row):
    return jnp.where(lax.rem(iota((CZ, CZ), 0), 8) == row, table, 0.0)


def gradient_kernel(k, eps, grad, psx, psy, gez, lab, keep, recv, w, out):
    q = lax.axis_index("src") ^ k
    below, above, extra = (edge_rows(keep, recv, 4 * part + q) for part in range(3))
    before = jnp.maximum(q - 1, 0)
    has = (q > 0).astype(F32)
    row = iota((8, Y), 0)
    lane = iota((8, Y), 1)

    def curl_rows(now, previous):
        shifted = jnp.where(row < 4, pltpu.roll(previous, 4, 0), pltpu.roll(now, 4, 0))
        along_y = now - jnp.where(lane == 0, 0.0, pltpu.roll(now, 1, 1))
        return now - shifted - pltpu.roll(along_y, 7, 0)

    curl_below = curl_rows(below, edge_rows(keep, recv, before) * has)
    curl_above = curl_rows(above, edge_rows(keep, recv, 4 + before) * has)
    kind = lax.rem(row, 4)
    plane = pltpu.roll(extra, 7, 0) + pltpu.roll(extra, 6, 0)
    below = jnp.where(kind == 0, curl_below, jnp.where(kind == 1, plane, below))
    above = jnp.where(kind == 0, curl_above, jnp.where(kind == 1, 0.0, above))
    cols = columns(below, above)
    wt = w[...].T
    first, last = wt[0:1, :], wt[CZ - 1:CZ, :]
    lane1 = iota((1, CZ), 1)
    top = jnp.where(lane1 == CZ - 1, 1.0, 0.0)
    first_up = jnp.where(lane1 == CZ - 1, 0.0, pltpu.roll(first, CZ - 1, 1)) - first
    last_up = jnp.where(lane1 == CZ - 1, 0.0, pltpu.roll(last, CZ - 1, 1)) - last + top
    lam_table = edge_table(first, last)
    curl_table = edge_table(first_up, last_up)
    plane_table = edge_table(jnp.where(lane1 == 0, 1.0, 0.0), jnp.zeros((1, CZ), F32))
    for j in range(2):
        r = 4 * j
        lam = mm(cols, jnp.concatenate([picked(lam_table, r + 2), picked(lam_table, r + 3)], 1).astype(BF))
        rest = mm(cols, jnp.concatenate([picked(curl_table, r), picked(plane_table, r + 1)], 1).astype(BF))
        inv = inverse_eps(lab[j], eps)
        out[j] = (
            grad[j] + psx[j] * lam[:, :CZ] + psy[j] * lam[:, CZ:]
            - inv * inv * (gez[0, j] * rest[:, :CZ] + rest[:, CZ:])
        )


def output_kernel(eps, ex, ey, ey_next, h, ez, ez_next, lab, keep, recv, w, e_o, h_o, hy_s):
    i = pl.program_id(0)

    @pl.when(i == 0)
    def _():
        hy_s[...] = jnp.zeros_like(hy_s)

    more = (i < 3).astype(F32)
    following = jnp.minimum(i + 1, 3)
    below, above = edge_rows(keep, recv, i), edge_rows(keep, recv, 4 + i)
    wt = w[...].T
    table = edge_table(wt[0:1, :], wt[CZ - 1:CZ, :])
    cols = columns(below, above)
    cols_next = columns(edge_rows(keep, recv, following), edge_rows(keep, recv, 4 + following))

    def corrected(source, j, comp):
        return mm(source, picked(table, 4 * j + comp).astype(BF))

    lane = iota((CZ, CZ), 1)
    piece = iota((CZ, CZ), 0) // 8
    ones = jnp.where((piece >= 6) & (piece < 9) & (lane == CZ - 1), 1.0, 0.0)

    def up(v, j, comp):
        return z_up(v) + mm(cols, picked(ones, 4 * j + comp).astype(BF))

    e_x = [ex[j] + corrected(cols, j, 0) for j in range(2)]
    e_y = [ey[j] + corrected(cols, j, 1) for j in range(2)]
    e_y.append((ey_next[0] + corrected(cols_next, 0, 1)) * more)
    e_z = [ez[0, 0], ez[0, 1], ez_next[0, 0] * more]
    hy_prev = hy_s[...]
    for j in range(2):
        hy = h[1, j] + up(e_x[j], j, 0) - (e_z[j + 1] - e_z[j])
        hx = h[0, j] + up(e_y[j], j, 1) - y_up(e_z[j])
        curl = hy - hy_prev - y_down(hx)
        hy_prev = hy
        e_o[0, j] = e_x[j]
        e_o[1, j] = e_y[j]
        e_o[2, j] = e_z[j] + inverse_eps(lab[j], eps) * curl
        h_o[0, j] = hx
        h_o[1, j] = hy
        h_o[2, j] = h[2, j] - (e_y[j + 1] - e_y[j]) + y_up(e_x[j])
    hy_s[...] = hy_prev


def place_kernel(g0, g1, g2, g3, out, sems):
    src = lax.axis_index("src")
    copies = []
    for k, g in enumerate((g0, g1, g2, g3)):
        copies.append(pltpu.make_async_copy(g, out.at[pl.ds(2 * (src ^ k), 2)], sems.at[k]))
    for copy in copies:
        copy.start()
    for copy in copies:
        copy.wait()


def swap(block, axis, mask):
    return lax.ppermute(block, axis, [(i, i ^ mask) for i in range(lax.axis_size(axis))])


SMEM = pl.BlockSpec(memory_space=pltpu.SMEM)
WHOLE = pl.BlockSpec(memory_space=pltpu.VMEM)
ANY = pl.BlockSpec(memory_space=pl.ANY)


def shape(*dims):
    return jax.ShapeDtypeStruct(dims, F32)


def cost(us):
    return pl.CostEstimate(flops=1000, bytes_accessed=int(us * 3.0e6), transcendentals=0)


def params(limit=LIMIT):
    return pltpu.CompilerParams(vmem_limit_bytes=limit)


def body(
    fields_e, fields_h, cot_e, cot_h, labels, region_eps, angle_index, profiles, zsheet,
    layer_term, block_inverse,
):
    e, h, ge, gh = fields_e[0], fields_h[0], cot_e[0], cot_h[0]
    w = block_inverse
    zs, lt = zsheet.reshape(1, CZ), layer_term.reshape(1, CZ)

    pair = pl.BlockSpec((2, Y, CZ), lambda i: (i, 0, 0))

    def comps(n, index=0):
        return pl.BlockSpec((n, 2, Y, CZ), lambda i: (index, i, 0, 0))

    def const(*dims):
        return pl.BlockSpec(dims, lambda i: (0,) * len(dims))

    z_next = pl.BlockSpec((1, 1, Y, CZ), lambda i: (2, jnp.minimum(2 * i + 2, 7), 0, 0))
    x_next = pl.BlockSpec((1, Y, CZ), lambda i: (jnp.minimum(2 * i + 2, 7), 0, 0))
    slab = shape(X, Y, CZ)
    message = shape(SLABS, 8, CZ)

    rx, ry, ax, ay, psx, psy, keep, send = pl.pallas_call(
        rhs_kernel,
        grid=(4,),
        in_specs=[
            SMEM, SMEM, comps(2), comps(3), comps(3), comps(3), pair, z_next, x_next,
            const(8, 2, X, Y), const(1, CZ), const(1, CZ), const(CZ, CZ),
        ],
        out_specs=[pair] * 6 + [const(SLABS, 8, CZ)] * 2,
        out_shape=[slab] * 6 + [message] * 2,
        scratch_shapes=[pltpu.VMEM((Y, CZ), F32), pltpu.VMEM((Y, CZ), F32), pltpu.VMEM((Y, CZ), BF)],
        compiler_params=params(BIG),
        cost_estimate=cost(6),
        name="right_hand_sides",
    )(angle_index, region_eps, e, h, ge, gh, labels, ge, labels, profiles, zs, lt, w)

    def small(kernel, name, n_in, outs, after=0):
        return pl.pallas_call(
            kernel, in_specs=[WHOLE] * n_in + [ANY] * after, out_specs=[WHOLE] * len(outs), out_shape=outs,
            compiler_params=params(), cost_estimate=cost(0.5), name=name,
        )

    other = swap(send, "gz", 1)
    (m0,) = small(chip_kernel, "chip", 2, [message])(keep, other)
    m1, m2, m3 = (swap(m0, "gz", 2 * k) for k in (1, 2, 3))

    adjoint = pl.pallas_call(
        adjoint_kernel,
        grid=(4,),
        in_specs=[pair] * 4 + [const(CZ, CZ), ANY],
        out_specs=pair,
        out_shape=slab,
        compiler_params=params(),
        cost_estimate=cost(3),
        name="adjoint_products",
    )(ax, ay, psx, psy, w, m0)

    (n0,) = small(group_kernel, "group", 4, [message], 1)(m0, m1, m2, m3, adjoint)
    n1, n2, n3 = (swap(n0, "gz", 8 * k) for k in (1, 2, 3))

    ex, ey, grad = pl.pallas_call(
        primal_kernel,
        grid=(4,),
        in_specs=[
            SMEM, pair, pair, comps(2), comps(1, 2), z_next, comps(1, 2), pair, pair, const(CZ, CZ), ANY,
        ],
        out_specs=[pair] * 3,
        out_shape=[slab] * 3,
        scratch_shapes=[pltpu.VMEM((Y, CZ), F32)],
        compiler_params=params(),
        cost_estimate=cost(4),
        name="primal_products",
    )(region_eps, rx, ry, h, e, e, ge, labels, adjoint, w, n0)

    edges = shape(12, 8, CZ)
    own_edges, send_edges = small(back_kernel, "back", 10, [edges] * 2, 1)(
        keep, other, m0, m1, m2, m3, n0, n1, n2, n3, ex
    )
    other_edges = swap(send_edges, "gz", 1)

    def gradient(k):
        def at(*tail):
            return lambda i: (lax.axis_index("src") ^ k,) + tail

        quarter = pl.BlockSpec((2, Y, CZ), at(0, 0))
        gez_quarter = pl.BlockSpec((1, 2, Y, CZ), lambda i: (2, lax.axis_index("src") ^ k, 0, 0))
        return pl.pallas_call(
            lambda *refs: gradient_kernel(k, *refs),
            grid=(1,),
            in_specs=[
                SMEM, quarter, quarter, quarter, gez_quarter, quarter,
                const(12, 8, CZ), const(12, 8, CZ), const(CZ, CZ),
            ],
            out_specs=const(2, Y, CZ),
            out_shape=shape(2, Y, CZ),
            compiler_params=params(),
            cost_estimate=cost(1),
            name=f"gradient_{k}",
        )(region_eps, grad, psx, psy, ge, labels, own_edges, other_edges, w)

    arrived = [swap(gradient(k), "src", k) for k in (2, 1, 3)]
    own = gradient(0)

    e_new, h_new = pl.pallas_call(
        output_kernel,
        grid=(4,),
        in_specs=[
            SMEM, pair, pair, x_next, comps(3), comps(1, 2), z_next, pair,
            const(12, 8, CZ), const(12, 8, CZ), const(CZ, CZ),
        ],
        out_specs=[comps(3), comps(3)],
        out_shape=[shape(3, X, Y, CZ)] * 2,
        scratch_shapes=[pltpu.VMEM((Y, CZ), F32)],
        compiler_params=params(),
        cost_estimate=cost(6),
        name="outputs",
    )(region_eps, ex, ey, ey, h, e, e, labels, own_edges, other_edges, w)

    total = own + arrived[0] + arrived[1] + arrived[2]
    two, one, three = (swap(total, "src", k) for k in (2, 1, 3))
    eps_grad = pl.pallas_call(
        place_kernel,
        in_specs=[ANY] * 4,
        out_specs=ANY,
        out_shape=slab,
        scratch_shapes=[pltpu.SemaphoreType.DMA((4,))],
        compiler_params=params(),
        cost_estimate=cost(1),
        name="place",
    )(total, one, two, three)
    return (e_new[None], h_new[None], eps_grad)


def solution(mesh):
    field = P("src", None, None, None, "gz")
    return jax.shard_map(
        body,
        mesh=mesh,
        in_specs=(
            field, field, field, field, P(None, None, "gz"), P(), P("src"), P(), P("gz"), P("gz"),
            P("gz", None),
        ),
        out_specs=(field, field, P(None, None, "gz")),
        check_vma=False,
    )
```

```python
import jax
import jax.numpy as jnp
from jax import lax
from jax.experimental import pallas as pl
from jax.experimental.pallas import tpu as pltpu
from jax.sharding import PartitionSpec as P

F32 = jnp.float32
BF = jnp.bfloat16
X, Y, CZ = 8, 256, 128
NN = (((1,), (0,)), ((), ()))
NT = (((1,), (1,)), ((), ()))
SLABS = 17
MIB = 1024 * 1024


def split(v):
    one = v.astype(BF)
    rest = v - one.astype(F32)
    two = rest.astype(BF)
    three = (rest - two.astype(F32)).astype(BF)
    return one, two, three


def mm(a, b, dims=NN):
    return lax.dot_general(a, b, dims, preferred_element_type=F32)


def iota(shape, axis):
    return lax.broadcasted_iota(jnp.int32, shape, axis)


def y_down(v):
    return v - jnp.where(iota(v.shape, 0) == 0, 0.0, pltpu.roll(v, 1, 0))


def y_up(v):
    n = v.shape[0]
    return jnp.where(iota(v.shape, 0) == n - 1, 0.0, pltpu.roll(v, n - 1, 0)) - v


def z_down(v):
    return v - jnp.where(iota(v.shape, 1) == 0, 0.0, pltpu.roll(v, 1, 1))


def z_up(v):
    n = v.shape[1]
    return jnp.where(iota(v.shape, 1) == n - 1, 0.0, pltpu.roll(v, n - 1, 1)) - v


def inverse_eps(labels, eps_ref):
    rows = [1.0 / jnp.full((1, CZ), eps_ref[r], F32) for r in range(4)]
    out = jnp.where(labels == 2, rows[2], rows[3])
    out = jnp.where(labels == 1, rows[1], out)
    return jnp.where(labels == 0, rows[0], out)


def six_rows(rows):
    one, two, three = (part.astype(F32) for part in split(rows))
    return [one, two, three, one, two, one]


def six_table(line, piece):
    one, two, three = (part.astype(F32) for part in split(line))
    return jnp.where(piece < 3, one, jnp.where(piece < 5, two, three))


def rhs_kernel(
    angle, eps, e, h, ge, gh, lab, prof_in, zs_in, lt_in, w_in,
    rx_o, ry_o, ax_o, ay_o, psx_o, psy_o, gs_o, inv_o, ez_o, h_o, w, keep_o, send_o,
    e_s, ge_s, gh_s, lab_s, sems, prof_s, prof, zs, lt,
):
    core = lax.rem(lax.axis_index("gz"), 2)

    def fetch(which, x):
        at = pl.ds(x, 1)
        return (
            lambda: pltpu.make_async_copy(lab.at[at], lab_s.at[at], sems.at[0, x]),
            lambda: pltpu.make_async_copy(ge.at[:, at], ge_s.at[:, at], sems.at[1, x]),
            lambda: pltpu.make_async_copy(h.at[:, at], h_o.at[:, at], sems.at[2, x]),
            lambda: pltpu.make_async_copy(gh.at[:, at], gh_s.at[:, at], sems.at[3, x]),
            lambda: pltpu.make_async_copy(e.at[pl.ds(0, 2), at], e_s.at[:, at], sems.at[4, x]),
        )[which]()

    tables = [
        pltpu.make_async_copy(source, target, sems.at[5, n + 1])
        for n, (source, target) in enumerate(
            ((prof_in.at[angle[0]], prof), (w_in, w), (zs_in, zs), (lt_in, lt))
        )
    ]
    for copy in tables:
        copy.start()
    early, late = (0, 1), (2, 3, 4)
    for which in early:
        fetch(which, 0).start()
    for x in range(X):
        if x + 1 < X:
            for which in early:
                fetch(which, x + 1).start()
        for which in late:
            fetch(which, x).start()
    ez_copy = pltpu.make_async_copy(e.at[2], ez_o, sems.at[5, 0])
    ez_copy.start()

    for copy in tables:
        copy.wait()
    both = jnp.concatenate([prof[0], prof[1]], 0)
    rows = jnp.concatenate(six_rows(both) + [jnp.zeros((32, Y), F32)], 0)
    prof_s[...] = rows.T.astype(BF)
    corners = [
        jnp.broadcast_to(w[p:p + 1, q:q + 1], (1, CZ))
        for p, q in ((0, 0), (0, CZ - 1), (CZ - 1, CZ - 1))
    ]
    corners = jnp.concatenate(corners + [jnp.zeros((5, CZ), F32)], 0)
    keep_o[16] = corners
    send_o[16] = corners

    row16 = iota((16, CZ), 0)
    lane16 = iota((16, CZ), 1)
    ends = jnp.where(row16 < 8, w[0:1, :], w[CZ - 1:CZ, :])
    ends_parts = [part.astype(F32) for part in split(ends)]
    slot = lax.rem(row16, 8)

    rowz = iota((CZ, CZ), 0)
    piece, within = rowz // 16, lax.rem(rowz, 16)
    z_table = jnp.where(piece < 6, six_table(zs[...], piece), 0.0)

    lane = iota((Y, CZ), 1)
    row_y = iota((16, Y), 0)
    for which in early:
        fetch(which, 0).wait()
    inv_o[0] = inverse_eps(lab_s[0], eps)

    def one_pair(i, carry):
        acc_ends = jnp.zeros((16, Y), F32)
        acc_tops = jnp.zeros((16, Y), F32)
        for j in range(2):
            x = 2 * i + j
            following = jnp.minimum(x + 1, X - 1)
            previous = jnp.maximum(x - 1, 0)
            more = (x < X - 1).astype(F32)
            less = (x > 0).astype(F32)

            @pl.when(x < X - 1)
            def _():
                for which in early:
                    fetch(which, x + 1).wait()

            for which in late:
                fetch(which, x).wait()
            inv = inv_o[x]
            inv_up = inverse_eps(lab_s[following], eps)
            inv_o[following] = inv_up
            sg = inv * ge_s[2, x]
            sg_up = inv_up * ge_s[2, following] * more
            z_pick = jnp.concatenate(
                [jnp.where(within == x, z_table, 0.0), jnp.where(within == 8 + x, z_table, 0.0)], 1
            ).astype(BF)
            cur = mm(prof_s[...], z_pick)
            h_x, h_y, h_z = h_o[0, x], h_o[1, x], h_o[2, x]
            g_hz = gh_s[2, x]
            bar_hy = gh_s[1, x] - (sg_up - sg)
            bar_hx = gh_s[0, x] + y_up(sg)
            p_x = y_down(h_z) - z_down(h_y) - cur[:, :CZ]
            p_y = z_down(h_x) - (h_z - h_o[2, previous] * less) - cur[:, CZ:]
            r_x = lt[...] * e_s[0, x] + inv * p_x
            r_y = lt[...] * e_s[1, x] + inv * p_y
            a_x = ge_s[0, x] - y_down(g_hz) - z_down(bar_hy)
            a_y = ge_s[1, x] + (g_hz - gh_s[2, previous] * less) - z_down(bar_hx)
            rx_o[x], ry_o[x], ax_o[x], ay_o[x] = r_x, r_y, a_x, a_y
            psx_o[x] = -inv * (inv * p_x)
            psy_o[x] = -inv * (inv * p_y)
            gs_o[x] = -inv * sg
            thirds = []
            for c, field in enumerate((r_x, r_y, a_x, a_y)):
                one, two, three = split(field)
                mask = slot == 4 * j + c
                w1, w2, w3 = (jnp.where(mask, part, 0.0) for part in ends_parts)
                lhs = jnp.concatenate(
                    [
                        jnp.concatenate([w1, w1], 1),
                        jnp.concatenate([w2, w2], 1),
                        jnp.concatenate([w3, jnp.zeros_like(w3)], 1),
                    ],
                    0,
                ).astype(BF)
                out = mm(lhs, jnp.concatenate([one, two], 1), NT)
                acc_ends += out[0:16] + out[16:32] + out[32:48]
                thirds.append((w1, three))
            for c in (0, 2):
                (wa, ta), (wb, tb) = thirds[c], thirds[c + 1]
                lhs = jnp.concatenate([wa, wb], 1).astype(BF)
                acc_ends += mm(lhs, jnp.concatenate([ta, tb], 1), NT)

            packed = jnp.where(lane == CZ - 1, h_y, inv)
            packed = jnp.where(lane == CZ - 2, -pltpu.roll(h_x, CZ - 1, 1), packed)
            packed = jnp.where(lane == CZ - 3, pltpu.roll(bar_hy, CZ - 2, 1), packed)
            packed = jnp.where(lane == CZ - 4, pltpu.roll(bar_hx, CZ - 3, 1), packed)
            one, two, three = split(packed)
            c16 = slot - 4 * j
            own = (c16 >= 0) & (c16 < 4)
            pick = jnp.where(
                own & (row16 < 8) & (lane16 == CZ - 1 - c16), 1.0,
                jnp.where(own & (row16 >= 8) & (c16 < 2) & (lane16 == 0), 1.0, 0.0),
            )
            acc_tops += mm(jnp.concatenate([pick, pick], 1).astype(BF), jnp.concatenate([one, two], 1), NT)
            acc_tops += mm(pick.astype(BF), three, NT)

        acc_tops = jnp.where((row_y >= 8) & (lax.rem(row_y, 4) >= 2), 1.0, acc_tops)
        for base, acc in ((0, acc_ends), (8, acc_tops)):
            low, high = acc[:, :CZ], acc[:, CZ:]
            keep = jnp.where(core == 0, low, high)
            send = jnp.where(core == 0, high, low)
            for part in range(2):
                keep_o[base + 4 * part + i] = keep[8 * part:8 * part + 8]
                send_o[base + 4 * part + i] = send[8 * part:8 * part + 8]
        return carry

    lax.fori_loop(0, X // 2, one_pair, 0)
    ez_copy.wait()


def unpack(ref):
    m = ref[...]
    return dict(
        f=m[0:4], l=m[4:8], t=m[8:12], k=m[12:16],
        a=m[16, 0:1, :], c=m[16, 1:2, :], z=m[16, 2:3, :],
    )


def repack(s, ref):
    ref[0:4] = s["f"]
    ref[4:8] = s["l"]
    ref[8:12] = s["t"]
    ref[12:16] = s["k"]
    ref[16] = jnp.concatenate([s["a"], s["c"], s["z"], jnp.zeros((5, CZ), F32)], 0)


def order(bit, own, other):
    lower = {n: jnp.where(bit == 0, own[n], other[n]) for n in own}
    upper = {n: jnp.where(bit == 0, other[n], own[n]) for n in own}
    return lower, upper


def coupled(lower, upper):
    delta = upper["k"] * lower["t"]
    f_up = upper["f"] + upper["a"] * delta
    l_up = upper["l"] + upper["c"] * delta
    inv = 1.0 / (1.0 - upper["a"] * lower["z"])
    return f_up, l_up, inv


def combine(lower, upper):
    f_up, l_up, inv = coupled(lower, upper)
    t = (f_up + upper["a"] * lower["l"]) * inv
    u = (lower["l"] + lower["z"] * f_up) * inv
    return dict(
        f=lower["f"] + lower["c"] * t,
        l=l_up + upper["c"] * u,
        t=upper["t"],
        k=lower["k"],
        a=lower["a"] + lower["c"] * lower["c"] * upper["a"] * inv,
        c=lower["c"] * upper["c"] * inv,
        z=upper["z"] + upper["c"] * upper["c"] * lower["z"] * inv,
    )


def outside(lower, upper, below, above):
    f_up, _, inv = coupled(lower, upper)
    l_low = lower["l"] + lower["c"] * below
    f_up = f_up + upper["c"] * above
    return (f_up + upper["a"] * l_low) * inv, (l_low + lower["z"] * f_up) * inv


def pick_outside(bit, lower, upper, below, above):
    t, u = outside(lower, upper, below, above)
    return jnp.where(bit == 0, below, u), jnp.where(bit == 0, t, above)


def bits():
    gz = lax.axis_index("gz")
    core, low_z, high_z = lax.rem(gz, 2), lax.rem(gz // 2, 2), lax.rem(gz // 4, 2)
    return core, low_z, high_z, lax.rem(gz // 8, 2), gz // 16


def chip_kernel(own, other, out):
    core = bits()[0]
    repack(combine(*order(core, unpack(own), unpack(other))), out)


def four(low, high, own, m1, m2, m3):
    first = order(low, own, m1)
    pair = combine(*first)
    return first, order(high, pair, combine(*order(low, m2, m3)))


def group_kernel(m0, m1, m2, m3, after, out):
    _, low, high, _, _ = bits()
    repack(combine(*four(low, high, *(unpack(m) for m in (m0, m1, m2, m3)))[1]), out)


def back_kernel(a0, a1, m0, m1, m2, m3, n0, n1, n2, n3, after, keep_o, send_o):
    core, zl, zh, xl, xh = bits()
    chip = order(core, unpack(a0), unpack(a1))
    m0, m1, m2, m3 = (unpack(m) for m in (m0, m1, m2, m3))
    n0, n1, n2, n3 = (unpack(n) for n in (n0, n1, n2, n3))
    z_first, z_second = four(zl, zh, m0, m1, m2, m3)
    x_first, x_second = four(xl, xh, n0, n1, n2, n3)
    zero = jnp.zeros_like(m0["f"])
    edge = (zero, zero)
    edge = pick_outside(xh, *x_second, *edge)
    edge = pick_outside(xl, *x_first, *edge)
    edge = pick_outside(zh, *z_second, *edge)
    edge = pick_outside(zl, *z_first, *edge)
    lower, upper = chip
    t, u = outside(lower, upper, *edge)
    under_x = jnp.where(xl == 1, n1["t"], jnp.where(xh == 1, n3["t"], zero))
    under = jnp.where(zl == 1, m1["t"], jnp.where(zh == 1, m3["t"], under_x))
    results = []
    for block, below, above, plane in ((lower, edge[0], t, under), (upper, u, edge[1], lower["t"])):
        below = below + block["k"] * plane
        first = block["f"] + block["a"] * below + block["c"] * above
        extra = jnp.stack([first[q] * pltpu.roll(plane[q], 2, 0) for q in range(4)])
        results.append((below, above, extra))
    for part in range(3):
        low, high = results[0][part], results[1][part]
        keep_o[4 * part:4 * part + 4] = jnp.where(core == 0, low, high)
        send_o[4 * part:4 * part + 4] = jnp.where(core == 0, high, low)


def product_tables(w):
    one, two, three = split(w.T)
    full = jnp.concatenate([one, two], 1)
    return jnp.concatenate([full, full], 0), jnp.concatenate([one, three], 0)


def product(field, tables):
    one, two, three = split(field)
    wide = mm(jnp.concatenate([one, two], 1), tables[0])
    narrow = mm(jnp.concatenate([three, one], 1), tables[1])
    return wide[:, :CZ] + wide[:, CZ:] + narrow


def adjoint_kernel(ax, ay, psx, psy, w, after, out):
    tables = product_tables(w[...])

    def one(x, carry):
        out[x] = psx[x] * product(ax[x], tables) + psy[x] * product(ay[x], tables)
        return carry

    lax.fori_loop(0, X, one, 0, unroll=2)


def primal_kernel(rx, ry, h, ez, gs, part, w, after, ex_o, ey_o, grad_o):
    tables = product_tables(w[...])

    def one(x, hy_prev):
        more = (x < X - 1).astype(F32)
        e_x, e_y = product(rx[x], tables), product(ry[x], tables)
        ex_o[x], ey_o[x] = e_x, e_y
        e_z = ez[x]
        hy = h[1, x] + z_up(e_x) - (ez[jnp.minimum(x + 1, X - 1)] * more - e_z)
        hx = h[0, x] + z_up(e_y) - y_up(e_z)
        grad_o[x] = part[x] + gs[x] * (hy - hy_prev - y_down(hx))
        return hy

    lax.fori_loop(0, X, one, jnp.zeros((Y, CZ), F32), unroll=2)


def edge_rows(keep, recv, slab):
    core = lax.rem(lax.axis_index("gz"), 2)
    a, b = keep[slab], recv[slab]
    return jnp.concatenate([jnp.where(core == 0, a, b), jnp.where(core == 0, b, a)], 1)


def columns(below, above):
    rows = six_rows(below) + six_rows(above) + [jnp.zeros((32, Y), F32)]
    return jnp.concatenate(rows, 0).T.astype(BF)


def edge_table(first, last):
    piece = iota((CZ, CZ), 0) // 8
    table = jnp.where(piece < 6, six_table(first, piece), six_table(last, piece - 6))
    return jnp.where(piece < 12, table, 0.0)


def picked(table, row):
    return jnp.where(lax.rem(iota((CZ, CZ), 0), 8) == row, table, 0.0)


def gradient_kernel(k, grad, psx, psy, gs, inv, keep, recv, w, out):
    q = lax.axis_index("src") ^ k
    below, above, extra = (edge_rows(keep, recv, 4 * part + q) for part in range(3))
    before = jnp.maximum(q - 1, 0)
    has = (q > 0).astype(F32)
    row = iota((8, Y), 0)
    lane = iota((8, Y), 1)

    def curl_rows(now, previous):
        shifted = jnp.where(row < 4, pltpu.roll(previous, 4, 0), pltpu.roll(now, 4, 0))
        along_y = now - jnp.where(lane == 0, 0.0, pltpu.roll(now, 1, 1))
        return now - shifted - pltpu.roll(along_y, 7, 0)

    curl_below = curl_rows(below, edge_rows(keep, recv, before) * has)
    curl_above = curl_rows(above, edge_rows(keep, recv, 4 + before) * has)
    kind = lax.rem(row, 4)
    plane = pltpu.roll(extra, 7, 0) + pltpu.roll(extra, 6, 0)
    below = jnp.where(kind == 0, curl_below, jnp.where(kind == 1, plane, below))
    above = jnp.where(kind == 0, curl_above, jnp.where(kind == 1, 0.0, above))
    cols = columns(below, above)
    wt = w[...].T
    first, last = wt[0:1, :], wt[CZ - 1:CZ, :]
    lane1 = iota((1, CZ), 1)
    top = jnp.where(lane1 == CZ - 1, 1.0, 0.0)
    first_up = jnp.where(lane1 == CZ - 1, 0.0, pltpu.roll(first, CZ - 1, 1)) - first
    last_up = jnp.where(lane1 == CZ - 1, 0.0, pltpu.roll(last, CZ - 1, 1)) - last + top
    lam_table = edge_table(first, last)
    curl_table = edge_table(first_up, last_up)
    plane_table = edge_table(jnp.where(lane1 == 0, 1.0, 0.0), jnp.zeros((1, CZ), F32))
    for j in range(2):
        r = 4 * j
        lam = mm(cols, jnp.concatenate([picked(lam_table, r + 2), picked(lam_table, r + 3)], 1).astype(BF))
        rest = mm(cols, jnp.concatenate([picked(curl_table, r), picked(plane_table, r + 1)], 1).astype(BF))
        x = 2 * q + j
        out[j] = (
            grad[x] + psx[x] * lam[:, :CZ] + psy[x] * lam[:, CZ:]
            + gs[x] * rest[:, :CZ] - inv[x] * inv[x] * rest[:, CZ:]
        )


def output_kernel(ex, ey, h, ez, inv, keep, recv, w, e_o, h_o, e_s, h_s, sems):
    wt = w[...].T
    table = edge_table(wt[0:1, :], wt[CZ - 1:CZ, :])
    lane = iota((CZ, CZ), 1)
    piece = iota((CZ, CZ), 0) // 8
    ones = jnp.where((piece >= 6) & (piece < 9) & (lane == CZ - 1), 1.0, 0.0)

    def edges(i):
        return columns(edge_rows(keep, recv, i), edge_rows(keep, recv, 4 + i))

    def corrected(source, table, row):
        return mm(source, picked(table, row).astype(BF))

    def copies(x):
        at = pl.ds(x, 1)
        return (
            pltpu.make_async_copy(e_s.at[:, at], e_o.at[:, at], sems.at[0, x]),
            pltpu.make_async_copy(h_s.at[:, at], h_o.at[:, at], sems.at[1, x]),
        )

    def one_pair(i, carry):
        cols, hy_prev = carry
        last = i == X // 2 - 1
        cols_next = edges(jnp.minimum(i + 1, X // 2 - 1))
        x = 2 * i
        more = jnp.where(last, 0.0, 1.0)
        following = jnp.minimum(x + 2, X - 1)
        e_x = [ex[x + j] + corrected(cols, table, 4 * j) for j in range(2)]
        e_y = [ey[x + j] + corrected(cols, table, 4 * j + 1) for j in range(2)]
        e_y.append((ey[following] + corrected(cols_next, table, 1)) * more)
        e_z = [ez[x], ez[x + 1], ez[following] * more]
        for j in range(2):
            hy = h[1, x + j] + z_up(e_x[j]) + corrected(cols, ones, 4 * j) - (e_z[j + 1] - e_z[j])
            hx = h[0, x + j] + z_up(e_y[j]) + corrected(cols, ones, 4 * j + 1) - y_up(e_z[j])
            curl = hy - hy_prev - y_down(hx)
            hy_prev = hy
            e_s[0, x + j] = e_x[j]
            e_s[1, x + j] = e_y[j]
            e_s[2, x + j] = e_z[j] + inv[x + j] * curl
            h_s[0, x + j] = hx
            h_s[1, x + j] = hy
            h_s[2, x + j] = h[2, x + j] - (e_y[j + 1] - e_y[j]) + y_up(e_x[j])
            for copy in copies(x + j):
                copy.start()
        return cols_next, hy_prev

    lax.fori_loop(0, X // 2, one_pair, (edges(0), jnp.zeros((Y, CZ), F32)))
    for x in range(X):
        for copy in copies(x):
            copy.wait()


def place_kernel(g0, g1, g2, g3, out, sems):
    src = lax.axis_index("src")
    copies = []
    for k, g in enumerate((g0, g1, g2, g3)):
        copies.append(pltpu.make_async_copy(g, out.at[pl.ds(2 * (src ^ k), 2)], sems.at[k]))
    for copy in copies:
        copy.start()
    for copy in copies:
        copy.wait()


def swap(block, axis, mask):
    return lax.ppermute(block, axis, [(i, i ^ mask) for i in range(lax.axis_size(axis))])


SMEM = pl.BlockSpec(memory_space=pltpu.SMEM)
VMEM = pl.BlockSpec(memory_space=pltpu.VMEM)
HBM = pl.BlockSpec(memory_space=pltpu.HBM)
ANY = pl.BlockSpec(memory_space=pl.ANY)


def shape(*dims):
    return jax.ShapeDtypeStruct(dims, F32)


def call(kernel, name, in_specs, outs, us, mib, out_specs=None, scratch=()):
    return pl.pallas_call(
        kernel,
        in_specs=in_specs,
        out_specs=out_specs or [VMEM] * len(outs),
        out_shape=outs,
        scratch_shapes=scratch,
        compiler_params=pltpu.CompilerParams(vmem_limit_bytes=mib * MIB),
        cost_estimate=pl.CostEstimate(flops=1000, bytes_accessed=int(us * 3.0e6), transcendentals=0),
        name=name,
    )


def in_hbm(array):
    return pltpu.with_memory_space_constraint(array, pltpu.HBM)


def body(
    fields_e, fields_h, cot_e, cot_h, labels, region_eps, angle_index, profiles, zsheet,
    layer_term, block_inverse,
):
    e, h, ge, gh = fields_e[0], fields_h[0], cot_e[0], cot_h[0]
    zs, lt = zsheet.reshape(1, CZ), layer_term.reshape(1, CZ)
    slab = shape(X, Y, CZ)
    message = shape(SLABS, 8, CZ)

    def space(*dims, dtype=F32):
        return pltpu.VMEM(dims, dtype)

    rx, ry, ax, ay, psx, psy, gs, inv, ez, hv, w, keep, send = call(
        rhs_kernel, "right_hand_sides",
        [SMEM, SMEM] + [HBM] * 9,
        [slab] * 9 + [shape(3, X, Y, CZ), shape(CZ, CZ)] + [message] * 2,
        6, 24,
        scratch=[
            space(2, X, Y, CZ), space(3, X, Y, CZ), space(3, X, Y, CZ),
            space(X, Y, CZ, dtype=jnp.int32), pltpu.SemaphoreType.DMA((6, X)),
            space(Y, CZ, dtype=BF), space(2, X, Y), space(1, CZ), space(1, CZ),
        ],
    )(angle_index, *map(in_hbm, (region_eps, e, h, ge, gh, labels, profiles, zs, lt, block_inverse)))

    other = swap(send, "gz", 1)
    (m0,) = call(chip_kernel, "chip", [VMEM] * 2, [message], 0.5, 4)(keep, other)
    m1, m2, m3 = (swap(m0, "gz", 2 * k) for k in (1, 2, 3))

    (adjoint,) = call(adjoint_kernel, "adjoint_products", [VMEM] * 5 + [ANY], [slab], 3, 8)(
        ax, ay, psx, psy, w, m0
    )
    (n0,) = call(group_kernel, "group", [VMEM] * 4 + [ANY], [message], 0.5, 4)(m0, m1, m2, m3, adjoint)
    n1, n2, n3 = (swap(n0, "gz", 8 * k) for k in (1, 2, 3))

    ex, ey, grad = call(primal_kernel, "primal_products", [VMEM] * 7 + [ANY], [slab] * 3, 4, 8)(
        rx, ry, hv, ez, gs, adjoint, w, n0
    )
    own_edges, send_edges = call(
        back_kernel, "back", [VMEM] * 10 + [ANY], [shape(12, 8, CZ)] * 2, 0.5, 4
    )(keep, other, m0, m1, m2, m3, n0, n1, n2, n3, ex)
    other_edges = swap(send_edges, "gz", 1)

    def gradient(k):
        return call(
            lambda *refs: gradient_kernel(k, *refs), f"gradient_{k}", [VMEM] * 8,
            [shape(2, Y, CZ)], 1, 8,
        )(grad, psx, psy, gs, inv, own_edges, other_edges, w)[0]

    arrived = [swap(gradient(k), "src", k) for k in (2, 1, 3)]
    own = gradient(0)

    e_new, h_new = call(
        output_kernel, "outputs", [VMEM] * 8, [shape(3, X, Y, CZ)] * 2, 6, 16,
        out_specs=[HBM] * 2,
        scratch=[space(3, X, Y, CZ), space(3, X, Y, CZ), pltpu.SemaphoreType.DMA((2, X))],
    )(ex, ey, hv, ez, inv, own_edges, other_edges, w)

    total = own + arrived[0] + arrived[1] + arrived[2]
    two, one, three = (swap(total, "src", k) for k in (2, 1, 3))
    (eps_grad,) = call(
        place_kernel, "place", [ANY] * 4, [slab], 1, 4, out_specs=[HBM],
        scratch=[pltpu.SemaphoreType.DMA((4,))],
    )(total, one, two, three)
    return (e_new[None], h_new[None], eps_grad)


def solution(mesh):
    field = P("src", None, None, None, "gz")
    return jax.shard_map(
        body,
        mesh=mesh,
        in_specs=(
            field, field, field, field, P(None, None, "gz"), P(), P("src"), P(), P("gz"), P("gz"),
            P("gz", None),
        ),
        out_specs=(field, field, P(None, None, "gz")),
        check_vma=False,
    )
```

```python
import jax
import jax.numpy as jnp
from jax import lax
from jax.experimental import pallas as pl
from jax.experimental.pallas import tpu as pltpu
from jax.sharding import PartitionSpec as P

F32 = jnp.float32
BF = jnp.bfloat16
X, Y, CZ = 8, 256, 128
NN = (((1,), (0,)), ((), ()))
NT = (((1,), (1,)), ((), ()))
SLABS = 17
MIB = 1024 * 1024


def split(v):
    one = v.astype(BF)
    rest = v - one.astype(F32)
    two = rest.astype(BF)
    three = (rest - two.astype(F32)).astype(BF)
    return one, two, three


def in_two(v):
    one = v.astype(BF)
    return jnp.concatenate([one, (v - one.astype(F32)).astype(BF)], 1)


def mm(a, b, dims=NN):
    return lax.dot_general(a, b, dims, preferred_element_type=F32)


def iota(shape, axis):
    return lax.broadcasted_iota(jnp.int32, shape, axis)


def y_down(v):
    return v - jnp.where(iota(v.shape, 0) == 0, 0.0, pltpu.roll(v, 1, 0))


def y_up(v):
    n = v.shape[0]
    return jnp.where(iota(v.shape, 0) == n - 1, 0.0, pltpu.roll(v, n - 1, 0)) - v


def z_down(v):
    return v - jnp.where(iota(v.shape, 1) == 0, 0.0, pltpu.roll(v, 1, 1))


def z_up(v):
    n = v.shape[1]
    return jnp.where(iota(v.shape, 1) == n - 1, 0.0, pltpu.roll(v, n - 1, 1)) - v


def inverse_eps(labels, eps_ref):
    rows = [1.0 / jnp.full((1, CZ), eps_ref[r], F32) for r in range(4)]
    out = jnp.where(labels == 2, rows[2], rows[3])
    out = jnp.where(labels == 1, rows[1], out)
    return jnp.where(labels == 0, rows[0], out)


def six_rows(rows):
    one, two, three = (part.astype(F32) for part in split(rows))
    return [one, two, three, one, two, one]


def six_table(line, piece):
    one, two, three = (part.astype(F32) for part in split(line))
    return jnp.where(piece < 3, one, jnp.where(piece < 5, two, three))


def rhs_kernel(
    angle, eps, e, h, ge, gh, lab, prof_in, zs_in, lt_in, w_in,
    rx_o, ry_o, ax_o, ay_o, psx_o, psy_o, gs_o, inv_o, h_o, w, keep_o, send_o,
    e_s, ge_s, gh_s, lab_s, sems, prof_s, prof, zs, lt,
):
    core = lax.rem(lax.axis_index("gz"), 2)

    def fetch(which, x):
        at = pl.ds(x, 1)
        return (
            lambda: pltpu.make_async_copy(lab.at[at], lab_s.at[at], sems.at[0, x]),
            lambda: pltpu.make_async_copy(ge.at[:, at], ge_s.at[:, at], sems.at[1, x]),
            lambda: pltpu.make_async_copy(h.at[:, at], h_o.at[:, at], sems.at[2, x]),
            lambda: pltpu.make_async_copy(gh.at[:, at], gh_s.at[:, at], sems.at[3, x]),
            lambda: pltpu.make_async_copy(e.at[pl.ds(0, 2), at], e_s.at[:, at], sems.at[4, x]),
        )[which]()

    tables = [
        pltpu.make_async_copy(source, target, sems.at[5, n + 1])
        for n, (source, target) in enumerate(
            ((prof_in.at[angle[0]], prof), (w_in, w), (zs_in, zs), (lt_in, lt))
        )
    ]
    for copy in tables:
        copy.start()
    early, late = (0, 1), (2, 3, 4)
    for which in early:
        fetch(which, 0).start()
    for x in range(X):
        if x + 1 < X:
            for which in early:
                fetch(which, x + 1).start()
        for which in late:
            fetch(which, x).start()

    for copy in tables:
        copy.wait()
    both = jnp.concatenate([prof[0], prof[1]], 0)
    rows = jnp.concatenate(six_rows(both) + [jnp.zeros((32, Y), F32)], 0)
    prof_s[...] = rows.T.astype(BF)
    corners = [
        jnp.broadcast_to(w[p:p + 1, q:q + 1], (1, CZ))
        for p, q in ((0, 0), (0, CZ - 1), (CZ - 1, CZ - 1))
    ]
    corners = jnp.concatenate(corners + [jnp.zeros((5, CZ), F32)], 0)
    keep_o[16] = corners
    send_o[16] = corners

    row16 = iota((16, CZ), 0)
    lane16 = iota((16, CZ), 1)
    ends = jnp.where(row16 < 8, w[0:1, :], w[CZ - 1:CZ, :])
    ends_parts = [part.astype(F32) for part in split(ends)]
    slot = lax.rem(row16, 8)

    rowz = iota((CZ, CZ), 0)
    piece, within = rowz // 16, lax.rem(rowz, 16)
    z_table = jnp.where(piece < 6, six_table(zs[...], piece), 0.0)

    lane = iota((Y, CZ), 1)
    row_y = iota((16, Y), 0)
    for which in early:
        fetch(which, 0).wait()
    inv_o[0] = inverse_eps(lab_s[0], eps)

    def one_pair(i, carry):
        acc_ends = jnp.zeros((16, Y), F32)
        acc_tops = jnp.zeros((16, Y), F32)
        for j in range(2):
            x = 2 * i + j
            following = jnp.minimum(x + 1, X - 1)
            previous = jnp.maximum(x - 1, 0)
            more = (x < X - 1).astype(F32)
            less = (x > 0).astype(F32)

            @pl.when(x < X - 1)
            def _():
                for which in early:
                    fetch(which, x + 1).wait()

            for which in late:
                fetch(which, x).wait()
            inv = inv_o[x]
            inv_up = inverse_eps(lab_s[following], eps)
            inv_o[following] = inv_up
            sg = inv * ge_s[2, x]
            sg_up = inv_up * ge_s[2, following] * more
            z_pick = jnp.concatenate(
                [jnp.where(within == x, z_table, 0.0), jnp.where(within == 8 + x, z_table, 0.0)], 1
            ).astype(BF)
            cur = mm(prof_s[...], z_pick)
            h_x, h_y, h_z = h_o[0, x], h_o[1, x], h_o[2, x]
            g_hz = gh_s[2, x]
            bar_hy = gh_s[1, x] - (sg_up - sg)
            bar_hx = gh_s[0, x] + y_up(sg)
            p_x = y_down(h_z) - z_down(h_y) - cur[:, :CZ]
            p_y = z_down(h_x) - (h_z - h_o[2, previous] * less) - cur[:, CZ:]
            r_x = lt[...] * e_s[0, x] + inv * p_x
            r_y = lt[...] * e_s[1, x] + inv * p_y
            a_x = ge_s[0, x] - y_down(g_hz) - z_down(bar_hy)
            a_y = ge_s[1, x] + (g_hz - gh_s[2, previous] * less) - z_down(bar_hx)
            rx_o[x], ry_o[x], ax_o[x], ay_o[x] = r_x, r_y, a_x, a_y
            psx_o[x] = -inv * (inv * p_x)
            psy_o[x] = -inv * (inv * p_y)
            gs_o[x] = -inv * sg
            for c, field in enumerate((r_x, r_y, a_x, a_y)):
                mask = slot == 4 * j + c
                lhs = jnp.concatenate([jnp.where(mask, part, 0.0) for part in ends_parts], 0)
                lhs = jnp.concatenate([lhs, lhs], 1).astype(BF)
                out = mm(lhs, in_two(field), NT)
                acc_ends += out[0:16] + out[16:32] + out[32:48]

            packed = jnp.where(lane == CZ - 1, h_y, inv)
            packed = jnp.where(lane == CZ - 2, -pltpu.roll(h_x, CZ - 1, 1), packed)
            packed = jnp.where(lane == CZ - 3, pltpu.roll(bar_hy, CZ - 2, 1), packed)
            packed = jnp.where(lane == CZ - 4, pltpu.roll(bar_hx, CZ - 3, 1), packed)
            c16 = slot - 4 * j
            own = (c16 >= 0) & (c16 < 4)
            pick = jnp.where(
                own & (row16 < 8) & (lane16 == CZ - 1 - c16), 1.0,
                jnp.where(own & (row16 >= 8) & (c16 < 2) & (lane16 == 0), 1.0, 0.0),
            )
            acc_tops += mm(jnp.concatenate([pick, pick], 1).astype(BF), in_two(packed), NT)

        acc_tops = jnp.where((row_y >= 8) & (lax.rem(row_y, 4) >= 2), 1.0, acc_tops)
        for base, acc in ((0, acc_ends), (8, acc_tops)):
            low, high = acc[:, :CZ], acc[:, CZ:]
            keep = jnp.where(core == 0, low, high)
            send = jnp.where(core == 0, high, low)
            for part in range(2):
                keep_o[base + 4 * part + i] = keep[8 * part:8 * part + 8]
                send_o[base + 4 * part + i] = send[8 * part:8 * part + 8]
        return carry

    lax.fori_loop(0, X // 2, one_pair, 0)


def unpack(ref):
    m = ref[...]
    return dict(
        f=m[0:4], l=m[4:8], t=m[8:12], k=m[12:16],
        a=m[16, 0:1, :], c=m[16, 1:2, :], z=m[16, 2:3, :],
    )


def repack(s, ref):
    ref[0:4] = s["f"]
    ref[4:8] = s["l"]
    ref[8:12] = s["t"]
    ref[12:16] = s["k"]
    ref[16] = jnp.concatenate([s["a"], s["c"], s["z"], jnp.zeros((5, CZ), F32)], 0)


def order(bit, own, other):
    lower = {n: jnp.where(bit == 0, own[n], other[n]) for n in own}
    upper = {n: jnp.where(bit == 0, other[n], own[n]) for n in own}
    return lower, upper


def coupled(lower, upper):
    delta = upper["k"] * lower["t"]
    f_up = upper["f"] + upper["a"] * delta
    l_up = upper["l"] + upper["c"] * delta
    inv = 1.0 / (1.0 - upper["a"] * lower["z"])
    return f_up, l_up, inv


def combine(lower, upper):
    f_up, l_up, inv = coupled(lower, upper)
    t = (f_up + upper["a"] * lower["l"]) * inv
    u = (lower["l"] + lower["z"] * f_up) * inv
    return dict(
        f=lower["f"] + lower["c"] * t,
        l=l_up + upper["c"] * u,
        t=upper["t"],
        k=lower["k"],
        a=lower["a"] + lower["c"] * lower["c"] * upper["a"] * inv,
        c=lower["c"] * upper["c"] * inv,
        z=upper["z"] + upper["c"] * upper["c"] * lower["z"] * inv,
    )


def outside(lower, upper, below, above):
    f_up, _, inv = coupled(lower, upper)
    l_low = lower["l"] + lower["c"] * below
    f_up = f_up + upper["c"] * above
    return (f_up + upper["a"] * l_low) * inv, (l_low + lower["z"] * f_up) * inv


def pick_outside(bit, lower, upper, below, above):
    t, u = outside(lower, upper, below, above)
    return jnp.where(bit == 0, below, u), jnp.where(bit == 0, t, above)


def bits():
    gz = lax.axis_index("gz")
    core, low_z, high_z = lax.rem(gz, 2), lax.rem(gz // 2, 2), lax.rem(gz // 4, 2)
    return core, low_z, high_z, lax.rem(gz // 8, 2), gz // 16


def chip_kernel(own, other, out):
    core = bits()[0]
    repack(combine(*order(core, unpack(own), unpack(other))), out)


def four(low, high, own, m1, m2, m3):
    first = order(low, own, m1)
    pair = combine(*first)
    return first, order(high, pair, combine(*order(low, m2, m3)))


def group_kernel(m0, m1, m2, m3, after, out):
    _, low, high, _, _ = bits()
    repack(combine(*four(low, high, *(unpack(m) for m in (m0, m1, m2, m3)))[1]), out)


def back_kernel(a0, a1, m0, m1, m2, m3, n0, n1, n2, n3, after, keep_o, send_o):
    core, zl, zh, xl, xh = bits()
    chip = order(core, unpack(a0), unpack(a1))
    m0, m1, m2, m3 = (unpack(m) for m in (m0, m1, m2, m3))
    n0, n1, n2, n3 = (unpack(n) for n in (n0, n1, n2, n3))
    z_first, z_second = four(zl, zh, m0, m1, m2, m3)
    x_first, x_second = four(xl, xh, n0, n1, n2, n3)
    zero = jnp.zeros_like(m0["f"])
    edge = (zero, zero)
    edge = pick_outside(xh, *x_second, *edge)
    edge = pick_outside(xl, *x_first, *edge)
    edge = pick_outside(zh, *z_second, *edge)
    edge = pick_outside(zl, *z_first, *edge)
    lower, upper = chip
    t, u = outside(lower, upper, *edge)
    under_x = jnp.where(xl == 1, n1["t"], jnp.where(xh == 1, n3["t"], zero))
    under = jnp.where(zl == 1, m1["t"], jnp.where(zh == 1, m3["t"], under_x))
    results = []
    for block, below, above, plane in ((lower, edge[0], t, under), (upper, u, edge[1], lower["t"])):
        below = below + block["k"] * plane
        first = block["f"] + block["a"] * below + block["c"] * above
        extra = jnp.stack([first[q] * pltpu.roll(plane[q], 2, 0) for q in range(4)])
        results.append((below, above, extra))
    for part in range(3):
        low, high = results[0][part], results[1][part]
        keep_o[4 * part:4 * part + 4] = jnp.where(core == 0, low, high)
        send_o[4 * part:4 * part + 4] = jnp.where(core == 0, high, low)


def product_tables(w):
    one, two, three = split(w.T)
    full = jnp.concatenate([one, two], 1)
    return jnp.concatenate([full, full], 0), jnp.concatenate([one, three], 0)


def product(field, tables):
    one, two, three = split(field)
    wide = mm(jnp.concatenate([one, two], 1), tables[0])
    narrow = mm(jnp.concatenate([three, one], 1), tables[1])
    return wide[:, :CZ] + wide[:, CZ:] + narrow


def adjoint_kernel(ax, ay, psx, psy, w, e, after, out, ez_o, sem):
    ez_copy = pltpu.make_async_copy(e.at[2], ez_o, sem)
    ez_copy.start()
    tables = product_tables(w[...])

    def one(x, carry):
        out[x] = psx[x] * product(ax[x], tables) + psy[x] * product(ay[x], tables)
        return carry

    lax.fori_loop(0, X, one, 0, unroll=2)
    ez_copy.wait()


def primal_kernel(rx, ry, h, ez, gs, part, w, after, ex_o, ey_o, grad_o):
    tables = product_tables(w[...])

    def one(x, hy_prev):
        more = (x < X - 1).astype(F32)
        e_x, e_y = product(rx[x], tables), product(ry[x], tables)
        ex_o[x], ey_o[x] = e_x, e_y
        e_z = ez[x]
        hy = h[1, x] + z_up(e_x) - (ez[jnp.minimum(x + 1, X - 1)] * more - e_z)
        hx = h[0, x] + z_up(e_y) - y_up(e_z)
        grad_o[x] = part[x] + gs[x] * (hy - hy_prev - y_down(hx))
        return hy

    lax.fori_loop(0, X, one, jnp.zeros((Y, CZ), F32), unroll=2)


def edge_rows(keep, recv, slab):
    core = lax.rem(lax.axis_index("gz"), 2)
    a, b = keep[slab], recv[slab]
    return jnp.concatenate([jnp.where(core == 0, a, b), jnp.where(core == 0, b, a)], 1)


def columns(below, above):
    rows = six_rows(below) + six_rows(above) + [jnp.zeros((32, Y), F32)]
    return jnp.concatenate(rows, 0).T.astype(BF)


def edge_table(first, last):
    piece = iota((CZ, CZ), 0) // 8
    table = jnp.where(piece < 6, six_table(first, piece), six_table(last, piece - 6))
    return jnp.where(piece < 12, table, 0.0)


def picked(table, row):
    return jnp.where(lax.rem(iota((CZ, CZ), 0), 8) == row, table, 0.0)


def gradient_kernel(k, grad, psx, psy, gs, inv, keep, recv, w, out):
    q = lax.axis_index("src") ^ k
    below, above, extra = (edge_rows(keep, recv, 4 * part + q) for part in range(3))
    before = jnp.maximum(q - 1, 0)
    has = (q > 0).astype(F32)
    row = iota((8, Y), 0)
    lane = iota((8, Y), 1)

    def curl_rows(now, previous):
        shifted = jnp.where(row < 4, pltpu.roll(previous, 4, 0), pltpu.roll(now, 4, 0))
        along_y = now - jnp.where(lane == 0, 0.0, pltpu.roll(now, 1, 1))
        return now - shifted - pltpu.roll(along_y, 7, 0)

    curl_below = curl_rows(below, edge_rows(keep, recv, before) * has)
    curl_above = curl_rows(above, edge_rows(keep, recv, 4 + before) * has)
    kind = lax.rem(row, 4)
    plane = pltpu.roll(extra, 7, 0) + pltpu.roll(extra, 6, 0)
    below = jnp.where(kind == 0, curl_below, jnp.where(kind == 1, plane, below))
    above = jnp.where(kind == 0, curl_above, jnp.where(kind == 1, 0.0, above))
    cols = columns(below, above)
    wt = w[...].T
    first, last = wt[0:1, :], wt[CZ - 1:CZ, :]
    lane1 = iota((1, CZ), 1)
    top = jnp.where(lane1 == CZ - 1, 1.0, 0.0)
    first_up = jnp.where(lane1 == CZ - 1, 0.0, pltpu.roll(first, CZ - 1, 1)) - first
    last_up = jnp.where(lane1 == CZ - 1, 0.0, pltpu.roll(last, CZ - 1, 1)) - last + top
    lam_table = edge_table(first, last)
    curl_table = edge_table(first_up, last_up)
    plane_table = edge_table(jnp.where(lane1 == 0, 1.0, 0.0), jnp.zeros((1, CZ), F32))
    for j in range(2):
        r = 4 * j
        lam = mm(cols, jnp.concatenate([picked(lam_table, r + 2), picked(lam_table, r + 3)], 1).astype(BF))
        rest = mm(cols, jnp.concatenate([picked(curl_table, r), picked(plane_table, r + 1)], 1).astype(BF))
        x = 2 * q + j
        out[j] = (
            grad[x] + psx[x] * lam[:, :CZ] + psy[x] * lam[:, CZ:]
            + gs[x] * rest[:, :CZ] - inv[x] * inv[x] * rest[:, CZ:]
        )


def output_kernel(ex, ey, h, ez, inv, keep, recv, w, e_o, h_o, e_s, h_s, sems):
    wt = w[...].T
    table = edge_table(wt[0:1, :], wt[CZ - 1:CZ, :])
    lane = iota((CZ, CZ), 1)
    piece = iota((CZ, CZ), 0) // 8
    ones = jnp.where((piece >= 6) & (piece < 9) & (lane == CZ - 1), 1.0, 0.0)

    def edges(i):
        return columns(edge_rows(keep, recv, i), edge_rows(keep, recv, 4 + i))

    def corrected(source, table, row):
        return mm(source, picked(table, row).astype(BF))

    def copies(x):
        at = pl.ds(x, 1)
        return (
            pltpu.make_async_copy(e_s.at[:, at], e_o.at[:, at], sems.at[0, x]),
            pltpu.make_async_copy(h_s.at[:, at], h_o.at[:, at], sems.at[1, x]),
        )

    def one_pair(i, carry):
        cols, hy_prev = carry
        last = i == X // 2 - 1
        cols_next = edges(jnp.minimum(i + 1, X // 2 - 1))
        x = 2 * i
        more = jnp.where(last, 0.0, 1.0)
        following = jnp.minimum(x + 2, X - 1)
        e_x = [ex[x + j] + corrected(cols, table, 4 * j) for j in range(2)]
        e_y = [ey[x + j] + corrected(cols, table, 4 * j + 1) for j in range(2)]
        e_y.append((ey[following] + corrected(cols_next, table, 1)) * more)
        e_z = [ez[x], ez[x + 1], ez[following] * more]
        for j in range(2):
            hy = h[1, x + j] + z_up(e_x[j]) + corrected(cols, ones, 4 * j) - (e_z[j + 1] - e_z[j])
            hx = h[0, x + j] + z_up(e_y[j]) + corrected(cols, ones, 4 * j + 1) - y_up(e_z[j])
            curl = hy - hy_prev - y_down(hx)
            hy_prev = hy
            e_s[0, x + j] = e_x[j]
            e_s[1, x + j] = e_y[j]
            e_s[2, x + j] = e_z[j] + inv[x + j] * curl
            h_s[0, x + j] = hx
            h_s[1, x + j] = hy
            h_s[2, x + j] = h[2, x + j] - (e_y[j + 1] - e_y[j]) + y_up(e_x[j])
            for copy in copies(x + j):
                copy.start()
        return cols_next, hy_prev

    lax.fori_loop(0, X // 2, one_pair, (edges(0), jnp.zeros((Y, CZ), F32)))
    for x in range(X):
        for copy in copies(x):
            copy.wait()


def place_kernel(g2, g1, g3, g0, out, sems):
    src = lax.axis_index("src")
    copies = []
    for k, g in zip((2, 1, 3, 0), (g2, g1, g3, g0)):
        copies.append(pltpu.make_async_copy(g, out.at[pl.ds(2 * (src ^ k), 2)], sems.at[k]))
    for copy in copies:
        copy.start()
    for copy in copies:
        copy.wait()


def swap(block, axis, mask):
    return lax.ppermute(block, axis, [(i, i ^ mask) for i in range(lax.axis_size(axis))])


SMEM = pl.BlockSpec(memory_space=pltpu.SMEM)
VMEM = pl.BlockSpec(memory_space=pltpu.VMEM)
HBM = pl.BlockSpec(memory_space=pltpu.HBM)
ANY = pl.BlockSpec(memory_space=pl.ANY)


def shape(*dims):
    return jax.ShapeDtypeStruct(dims, F32)


def call(kernel, name, in_specs, outs, us, mib, out_specs=None, scratch=()):
    return pl.pallas_call(
        kernel,
        in_specs=in_specs,
        out_specs=out_specs or [VMEM] * len(outs),
        out_shape=outs,
        scratch_shapes=scratch,
        compiler_params=pltpu.CompilerParams(vmem_limit_bytes=mib * MIB),
        cost_estimate=pl.CostEstimate(flops=1000, bytes_accessed=int(us * 3.0e6), transcendentals=0),
        name=name,
    )


def in_hbm(array):
    return pltpu.with_memory_space_constraint(array, pltpu.HBM)


def body(
    fields_e, fields_h, cot_e, cot_h, labels, region_eps, angle_index, profiles, zsheet,
    layer_term, block_inverse,
):
    e, h, ge, gh = fields_e[0], fields_h[0], cot_e[0], cot_h[0]
    zs, lt = zsheet.reshape(1, CZ), layer_term.reshape(1, CZ)
    slab = shape(X, Y, CZ)
    message = shape(SLABS, 8, CZ)

    def space(*dims, dtype=F32):
        return pltpu.VMEM(dims, dtype)

    rx, ry, ax, ay, psx, psy, gs, inv, hv, w, keep, send = call(
        rhs_kernel, "right_hand_sides",
        [SMEM, SMEM] + [HBM] * 9,
        [slab] * 8 + [shape(3, X, Y, CZ), shape(CZ, CZ)] + [message] * 2,
        6, 24,
        scratch=[
            space(2, X, Y, CZ), space(3, X, Y, CZ), space(3, X, Y, CZ),
            space(X, Y, CZ, dtype=jnp.int32), pltpu.SemaphoreType.DMA((6, X)),
            space(Y, CZ, dtype=BF), space(2, X, Y), space(1, CZ), space(1, CZ),
        ],
    )(angle_index, *map(in_hbm, (region_eps, e, h, ge, gh, labels, profiles, zs, lt, block_inverse)))

    other = swap(send, "gz", 1)
    (m0,) = call(chip_kernel, "chip", [VMEM] * 2, [message], 0.5, 4)(keep, other)
    m1, m2, m3 = (swap(m0, "gz", 2 * k) for k in (1, 2, 3))

    adjoint, ez = call(
        adjoint_kernel, "adjoint_products", [VMEM] * 5 + [HBM, ANY], [slab] * 2, 3, 8,
        scratch=[pltpu.SemaphoreType.DMA],
    )(ax, ay, psx, psy, w, in_hbm(e), m0)
    (n0,) = call(group_kernel, "group", [VMEM] * 4 + [ANY], [message], 0.5, 4)(m0, m1, m2, m3, adjoint)
    n1, n2, n3 = (swap(n0, "gz", 8 * k) for k in (1, 2, 3))

    ex, ey, grad = call(primal_kernel, "primal_products", [VMEM] * 7 + [ANY], [slab] * 3, 4, 8)(
        rx, ry, hv, ez, gs, adjoint, w, n0
    )
    own_edges, send_edges = call(
        back_kernel, "back", [VMEM] * 10 + [ANY], [shape(12, 8, CZ)] * 2, 0.5, 4
    )(keep, other, m0, m1, m2, m3, n0, n1, n2, n3, ex)
    other_edges = swap(send_edges, "gz", 1)

    def gradient(k):
        return call(
            lambda *refs: gradient_kernel(k, *refs), f"gradient_{k}", [VMEM] * 8,
            [shape(2, Y, CZ)], 1, 8,
        )(grad, psx, psy, gs, inv, own_edges, other_edges, w)[0]

    arrived = [swap(gradient(k), "src", k) for k in (2, 1, 3)]
    own = gradient(0)

    e_new, h_new = call(
        output_kernel, "outputs", [VMEM] * 8, [shape(3, X, Y, CZ)] * 2, 6, 16,
        out_specs=[HBM] * 2,
        scratch=[space(3, X, Y, CZ), space(3, X, Y, CZ), pltpu.SemaphoreType.DMA((2, X))],
    )(ex, ey, hv, ez, inv, own_edges, other_edges, w)

    total = own + arrived[0] + arrived[1] + arrived[2]
    two, one, three = (swap(total, "src", k) for k in (2, 1, 3))
    (eps_grad,) = call(
        place_kernel, "place", [ANY] * 4, [slab], 1, 4, out_specs=[HBM],
        scratch=[pltpu.SemaphoreType.DMA((4,))],
    )(two, one, three, total)
    return (e_new[None], h_new[None], eps_grad)


def solution(mesh):
    field = P("src", None, None, None, "gz")
    return jax.shard_map(
        body,
        mesh=mesh,
        in_specs=(
            field, field, field, field, P(None, None, "gz"), P(), P("src"), P(), P("gz"), P("gz"),
            P("gz", None),
        ),
        out_specs=(field, field, P(None, None, "gz")),
        check_vma=False,
    )
```

```python
import jax
import jax.numpy as jnp
from jax import lax
from jax.experimental import pallas as pl
from jax.experimental.pallas import tpu as pltpu
from jax.sharding import PartitionSpec as P

F32 = jnp.float32
BF = jnp.bfloat16
X, Y, CZ = 8, 256, 128
NN = (((1,), (0,)), ((), ()))
NT = (((1,), (1,)), ((), ()))
SLABS = 12
CORNERS = SLABS - 1
MIB = 1024 * 1024


def split(v):
    one = v.astype(BF)
    rest = v - one.astype(F32)
    two = rest.astype(BF)
    three = (rest - two.astype(F32)).astype(BF)
    return one, two, three


def in_two(v):
    one = v.astype(BF)
    return jnp.concatenate([one, (v - one.astype(F32)).astype(BF)], 1)


def mm(a, b, dims=NN):
    return lax.dot_general(a, b, dims, preferred_element_type=F32)


def iota(shape, axis):
    return lax.broadcasted_iota(jnp.int32, shape, axis)


def y_down(v):
    return v - jnp.where(iota(v.shape, 0) == 0, 0.0, pltpu.roll(v, 1, 0))


def y_up(v):
    n = v.shape[0]
    return jnp.where(iota(v.shape, 0) == n - 1, 0.0, pltpu.roll(v, n - 1, 0)) - v


def z_down(v):
    return v - jnp.where(iota(v.shape, 1) == 0, 0.0, pltpu.roll(v, 1, 1))


def z_up(v):
    n = v.shape[1]
    return jnp.where(iota(v.shape, 1) == n - 1, 0.0, pltpu.roll(v, n - 1, 1)) - v


def inverse_eps(labels, eps_ref):
    rows = [1.0 / jnp.full((1, CZ), eps_ref[r], F32) for r in range(4)]
    out = jnp.where(labels == 2, rows[2], rows[3])
    out = jnp.where(labels == 1, rows[1], out)
    return jnp.where(labels == 0, rows[0], out)


def six_rows(rows):
    one, two, three = (part.astype(F32) for part in split(rows))
    return [one, two, three, one, two, one]


def six_table(line, piece):
    one, two, three = (part.astype(F32) for part in split(line))
    return jnp.where(piece < 3, one, jnp.where(piece < 5, two, three))


def rhs_kernel(
    angle, eps, e, h, ge, gh, lab, prof_in, zs_in, lt_in, w_in,
    rx_o, ry_o, ax_o, ay_o, psx_o, psy_o, gs_o, inv_o, h_o, w, keep_o, send_o,
    e_s, ge_s, gh_s, lab_s, sems, prof_s, prof, zs, lt,
):
    core = lax.rem(lax.axis_index("gz"), 2)

    def fetch(which, x):
        at = pl.ds(x, 1)
        return (
            lambda: pltpu.make_async_copy(lab.at[at], lab_s.at[at], sems.at[0, x]),
            lambda: pltpu.make_async_copy(ge.at[:, at], ge_s.at[:, at], sems.at[1, x]),
            lambda: pltpu.make_async_copy(h.at[:, at], h_o.at[:, at], sems.at[2, x]),
            lambda: pltpu.make_async_copy(gh.at[:, at], gh_s.at[:, at], sems.at[3, x]),
            lambda: pltpu.make_async_copy(e.at[pl.ds(0, 2), at], e_s.at[:, at], sems.at[4, x]),
        )[which]()

    tables = [
        pltpu.make_async_copy(source, target, sems.at[5, n + 1])
        for n, (source, target) in enumerate(
            ((prof_in.at[angle[0]], prof), (w_in, w), (zs_in, zs), (lt_in, lt))
        )
    ]
    for copy in tables:
        copy.start()
    early, late = (0, 1), (2, 3, 4)
    for which in early:
        fetch(which, 0).start()
    for x in range(X):
        if x + 1 < X:
            for which in early:
                fetch(which, x + 1).start()
        for which in late:
            fetch(which, x).start()

    for copy in tables:
        copy.wait()
    both = jnp.concatenate([prof[0], prof[1]], 0)
    rows = jnp.concatenate(six_rows(both) + [jnp.zeros((32, Y), F32)], 0)
    prof_s[...] = rows.T.astype(BF)
    corners = [
        jnp.broadcast_to(w[p:p + 1, q:q + 1], (1, CZ))
        for p, q in ((0, 0), (0, CZ - 1), (CZ - 1, CZ - 1))
    ]
    corners = jnp.concatenate(corners + [jnp.zeros((5, CZ), F32)], 0)
    keep_o[CORNERS] = corners
    send_o[CORNERS] = corners

    row16 = iota((16, CZ), 0)
    lane16 = iota((16, CZ), 1)
    ends = jnp.where(row16 < 8, w[0:1, :], w[CZ - 1:CZ, :])
    ends_parts = [part.astype(F32) for part in split(ends)]
    slot = lax.rem(row16, 8)

    rowz = iota((CZ, CZ), 0)
    piece, within = rowz // 16, lax.rem(rowz, 16)
    z_table = jnp.where(piece < 6, six_table(zs[...], piece), 0.0)

    lane = iota((Y, CZ), 1)
    row8 = iota((8, Y), 0)
    for which in early:
        fetch(which, 0).wait()
    inv_o[0] = inverse_eps(lab_s[0], eps)

    def one_pair(i, carry):
        acc_ends = jnp.zeros((16, Y), F32)
        acc_tops = jnp.zeros((16, Y), F32)
        for j in range(2):
            x = 2 * i + j
            following = jnp.minimum(x + 1, X - 1)
            previous = jnp.maximum(x - 1, 0)
            more = (x < X - 1).astype(F32)
            less = (x > 0).astype(F32)

            @pl.when(x < X - 1)
            def _():
                for which in early:
                    fetch(which, x + 1).wait()

            for which in late:
                fetch(which, x).wait()
            inv = inv_o[x]
            inv_up = inverse_eps(lab_s[following], eps)
            inv_o[following] = inv_up
            sg = inv * ge_s[2, x]
            sg_up = inv_up * ge_s[2, following] * more
            z_pick = jnp.concatenate(
                [jnp.where(within == x, z_table, 0.0), jnp.where(within == 8 + x, z_table, 0.0)], 1
            ).astype(BF)
            cur = mm(prof_s[...], z_pick)
            h_x, h_y, h_z = h_o[0, x], h_o[1, x], h_o[2, x]
            g_hz = gh_s[2, x]
            bar_hy = gh_s[1, x] - (sg_up - sg)
            bar_hx = gh_s[0, x] + y_up(sg)
            p_x = y_down(h_z) - z_down(h_y) - cur[:, :CZ]
            p_y = z_down(h_x) - (h_z - h_o[2, previous] * less) - cur[:, CZ:]
            r_x = lt[...] * e_s[0, x] + inv * p_x
            r_y = lt[...] * e_s[1, x] + inv * p_y
            a_x = ge_s[0, x] - y_down(g_hz) - z_down(bar_hy)
            a_y = ge_s[1, x] + (g_hz - gh_s[2, previous] * less) - z_down(bar_hx)
            rx_o[x], ry_o[x], ax_o[x], ay_o[x] = r_x, r_y, a_x, a_y
            psx_o[x] = -inv * (inv * p_x)
            psy_o[x] = -inv * (inv * p_y)
            gs_o[x] = -inv * sg
            for c, field in enumerate((r_x, r_y, a_x, a_y)):
                mask = slot == 4 * j + c
                lhs = jnp.concatenate([jnp.where(mask, part, 0.0) for part in ends_parts], 0)
                lhs = jnp.concatenate([lhs, lhs], 1).astype(BF)
                out = mm(lhs, in_two(field), NT)
                acc_ends += out[0:16] + out[16:32] + out[32:48]

            packed = jnp.where(lane == CZ - 1, h_y, inv)
            packed = jnp.where(lane == CZ - 2, -pltpu.roll(h_x, CZ - 1, 1), packed)
            packed = jnp.where(lane == CZ - 3, pltpu.roll(bar_hy, CZ - 2, 1), packed)
            packed = jnp.where(lane == CZ - 4, pltpu.roll(bar_hx, CZ - 3, 1), packed)
            c16 = slot - 4 * j
            own = (c16 >= 0) & (c16 < 4)
            pick = jnp.where(
                own & (row16 < 8) & (lane16 == CZ - 1 - c16), 1.0,
                jnp.where(own & (row16 >= 8) & (c16 == i) & (lane16 == 0), 1.0, 0.0),
            )
            acc_tops += mm(jnp.concatenate([pick, pick], 1).astype(BF), in_two(packed), NT)

        tops, planes = acc_tops[0:8], acc_tops[8:16]
        outgoing = acc_ends[8:16] + jnp.where(lax.rem(row8, 4) >= 2, tops, 0.0)
        comp = lax.rem(iota((8, CZ), 0), 4)
        second = lax.rem(i, 2)
        tops = jnp.where(second == 0, tops, pltpu.roll(tops, 2, 0))
        tops_mine = comp // 2 == second
        planes_mine = comp == i

        def put(ref, low):
            def half(v):
                return jnp.where((core == 0) == low, v[:, :CZ], v[:, CZ:])

            ref[i] = half(acc_ends[0:8])
            ref[4 + i] = half(outgoing)
            slab = 8 + i // 2
            ref[slab] = jnp.where(tops_mine, half(tops), ref[slab])
            ref[10] = jnp.where(planes_mine, half(planes), ref[10])

        put(keep_o, True)
        put(send_o, False)
        return carry

    lax.fori_loop(0, X // 2, one_pair, 0)


def unpack(ref):
    m = ref[...]
    comp = lax.rem(iota((8, CZ), 0), 4)
    tops = [jnp.where(comp < 2, v, 0.0) for p in (m[8], m[9]) for v in (p, pltpu.roll(p, 6, 0))]
    planes = m[10]

    def plane(q):
        return jnp.where(
            comp == 0, pltpu.roll(planes, (8 - q) % 8, 0),
            jnp.where(comp == 1, pltpu.roll(planes, (9 - q) % 8, 0), 0.0),
        )

    return dict(
        f=m[0:4], l=m[4:8], t=jnp.stack(tops), k=jnp.stack([plane(q) for q in range(4)]),
        a=m[CORNERS, 0:1, :], c=m[CORNERS, 1:2, :], z=m[CORNERS, 2:3, :],
    )


def repack(s, ref):
    comp = lax.rem(iota((8, CZ), 0), 4)
    ref[0:4] = s["f"]
    ref[4:8] = s["l"]
    for p in range(2):
        ref[8 + p] = jnp.where(comp < 2, s["t"][2 * p], pltpu.roll(s["t"][2 * p + 1], 2, 0))
    planes = s["k"][0]
    for q in range(1, 4):
        planes = jnp.where(comp == q, pltpu.roll(s["k"][q], q, 0), planes)
    ref[10] = planes
    ref[CORNERS] = jnp.concatenate([s["a"], s["c"], s["z"], jnp.zeros((5, CZ), F32)], 0)


def order(bit, own, other):
    lower = {n: jnp.where(bit == 0, own[n], other[n]) for n in own}
    upper = {n: jnp.where(bit == 0, other[n], own[n]) for n in own}
    return lower, upper


def coupled(lower, upper):
    delta = upper["k"] * lower["t"]
    f_up = upper["f"] + upper["a"] * delta
    l_up = upper["l"] + upper["c"] * delta
    inv = 1.0 / (1.0 - upper["a"] * lower["z"])
    return f_up, l_up, inv


def combine(lower, upper):
    f_up, l_up, inv = coupled(lower, upper)
    t = (f_up + upper["a"] * lower["l"]) * inv
    u = (lower["l"] + lower["z"] * f_up) * inv
    return dict(
        f=lower["f"] + lower["c"] * t,
        l=l_up + upper["c"] * u,
        t=upper["t"],
        k=lower["k"],
        a=lower["a"] + lower["c"] * lower["c"] * upper["a"] * inv,
        c=lower["c"] * upper["c"] * inv,
        z=upper["z"] + upper["c"] * upper["c"] * lower["z"] * inv,
    )


def outside(lower, upper, below, above):
    f_up, _, inv = coupled(lower, upper)
    l_low = lower["l"] + lower["c"] * below
    f_up = f_up + upper["c"] * above
    return (f_up + upper["a"] * l_low) * inv, (l_low + lower["z"] * f_up) * inv


def pick_outside(bit, lower, upper, below, above):
    t, u = outside(lower, upper, below, above)
    return jnp.where(bit == 0, below, u), jnp.where(bit == 0, t, above)


def bits():
    gz = lax.axis_index("gz")
    core, low_z, high_z = lax.rem(gz, 2), lax.rem(gz // 2, 2), lax.rem(gz // 4, 2)
    return core, low_z, high_z, lax.rem(gz // 8, 2), gz // 16


def chip_kernel(own, other, out):
    core = bits()[0]
    repack(combine(*order(core, unpack(own), unpack(other))), out)


def four(low, high, own, m1, m2, m3):
    first = order(low, own, m1)
    pair = combine(*first)
    return first, order(high, pair, combine(*order(low, m2, m3)))


def group_kernel(m0, m1, m2, m3, after, out):
    _, low, high, _, _ = bits()
    repack(combine(*four(low, high, *(unpack(m) for m in (m0, m1, m2, m3)))[1]), out)


def back_kernel(a0, a1, m0, m1, m2, m3, n0, n1, n2, n3, after, keep_o, send_o):
    core, zl, zh, xl, xh = bits()
    chip = order(core, unpack(a0), unpack(a1))
    m0, m1, m2, m3 = (unpack(m) for m in (m0, m1, m2, m3))
    n0, n1, n2, n3 = (unpack(n) for n in (n0, n1, n2, n3))
    z_first, z_second = four(zl, zh, m0, m1, m2, m3)
    x_first, x_second = four(xl, xh, n0, n1, n2, n3)
    zero = jnp.zeros_like(m0["f"])
    edge = (zero, zero)
    edge = pick_outside(xh, *x_second, *edge)
    edge = pick_outside(xl, *x_first, *edge)
    edge = pick_outside(zh, *z_second, *edge)
    edge = pick_outside(zl, *z_first, *edge)
    lower, upper = chip
    t, u = outside(lower, upper, *edge)
    under_x = jnp.where(xl == 1, n1["t"], jnp.where(xh == 1, n3["t"], zero))
    under = jnp.where(zl == 1, m1["t"], jnp.where(zh == 1, m3["t"], under_x))
    results = []
    for block, below, above, plane in ((lower, edge[0], t, under), (upper, u, edge[1], lower["t"])):
        below = below + block["k"] * plane
        first = block["f"] + block["a"] * below + block["c"] * above
        extra = jnp.stack([first[q] * pltpu.roll(plane[q], 2, 0) for q in range(4)])
        results.append((below, above, extra))
    for part in range(3):
        low, high = results[0][part], results[1][part]
        keep_o[4 * part:4 * part + 4] = jnp.where(core == 0, low, high)
        send_o[4 * part:4 * part + 4] = jnp.where(core == 0, high, low)


def product_tables(w):
    one, two, three = split(w.T)
    full = jnp.concatenate([one, two], 1)
    return jnp.concatenate([full, full], 0), jnp.concatenate([one, three], 0)


def product(field, tables):
    one, two, three = split(field)
    wide = mm(jnp.concatenate([one, two], 1), tables[0])
    narrow = mm(jnp.concatenate([three, one], 1), tables[1])
    return wide[:, :CZ] + wide[:, CZ:] + narrow


def adjoint_kernel(ax, ay, psx, psy, w, e, after, out, ez_o, sem):
    ez_copy = pltpu.make_async_copy(e.at[2], ez_o, sem)
    ez_copy.start()
    tables = product_tables(w[...])

    def one(x, carry):
        out[x] = psx[x] * product(ax[x], tables) + psy[x] * product(ay[x], tables)
        return carry

    lax.fori_loop(0, X, one, 0, unroll=2)
    ez_copy.wait()


def primal_kernel(rx, ry, h, ez, gs, part, w, after, ex_o, ey_o, grad_o):
    tables = product_tables(w[...])

    def one(x, hy_prev):
        more = (x < X - 1).astype(F32)
        e_x, e_y = product(rx[x], tables), product(ry[x], tables)
        ex_o[x], ey_o[x] = e_x, e_y
        e_z = ez[x]
        hy = h[1, x] + z_up(e_x) - (ez[jnp.minimum(x + 1, X - 1)] * more - e_z)
        hx = h[0, x] + z_up(e_y) - y_up(e_z)
        grad_o[x] = part[x] + gs[x] * (hy - hy_prev - y_down(hx))
        return hy

    lax.fori_loop(0, X, one, jnp.zeros((Y, CZ), F32), unroll=2)


def edge_rows(keep, recv, slab):
    core = lax.rem(lax.axis_index("gz"), 2)
    a, b = keep[slab], recv[slab]
    return jnp.concatenate([jnp.where(core == 0, a, b), jnp.where(core == 0, b, a)], 1)


def columns(below, above):
    rows = six_rows(below) + six_rows(above) + [jnp.zeros((32, Y), F32)]
    return jnp.concatenate(rows, 0).T.astype(BF)


def edge_table(first, last):
    piece = iota((CZ, CZ), 0) // 8
    table = jnp.where(piece < 6, six_table(first, piece), six_table(last, piece - 6))
    return jnp.where(piece < 12, table, 0.0)


def picked(table, row):
    return jnp.where(lax.rem(iota((CZ, CZ), 0), 8) == row, table, 0.0)


def gradient_kernel(k, grad, psx, psy, gs, inv, keep, recv, w, out):
    q = lax.axis_index("src") ^ k
    below, above, extra = (edge_rows(keep, recv, 4 * part + q) for part in range(3))
    before = jnp.maximum(q - 1, 0)
    has = (q > 0).astype(F32)
    row = iota((8, Y), 0)
    lane = iota((8, Y), 1)

    def curl_rows(now, previous):
        shifted = jnp.where(row < 4, pltpu.roll(previous, 4, 0), pltpu.roll(now, 4, 0))
        along_y = now - jnp.where(lane == 0, 0.0, pltpu.roll(now, 1, 1))
        return now - shifted - pltpu.roll(along_y, 7, 0)

    curl_below = curl_rows(below, edge_rows(keep, recv, before) * has)
    curl_above = curl_rows(above, edge_rows(keep, recv, 4 + before) * has)
    kind = lax.rem(row, 4)
    plane = pltpu.roll(extra, 7, 0) + pltpu.roll(extra, 6, 0)
    below = jnp.where(kind == 0, curl_below, jnp.where(kind == 1, plane, below))
    above = jnp.where(kind == 0, curl_above, jnp.where(kind == 1, 0.0, above))
    cols = columns(below, above)
    wt = w[...].T
    first, last = wt[0:1, :], wt[CZ - 1:CZ, :]
    lane1 = iota((1, CZ), 1)
    top = jnp.where(lane1 == CZ - 1, 1.0, 0.0)
    first_up = jnp.where(lane1 == CZ - 1, 0.0, pltpu.roll(first, CZ - 1, 1)) - first
    last_up = jnp.where(lane1 == CZ - 1, 0.0, pltpu.roll(last, CZ - 1, 1)) - last + top
    lam_table = edge_table(first, last)
    curl_table = edge_table(first_up, last_up)
    plane_table = edge_table(jnp.where(lane1 == 0, 1.0, 0.0), jnp.zeros((1, CZ), F32))
    for j in range(2):
        r = 4 * j
        lam = mm(cols, jnp.concatenate([picked(lam_table, r + 2), picked(lam_table, r + 3)], 1).astype(BF))
        rest = mm(cols, jnp.concatenate([picked(curl_table, r), picked(plane_table, r + 1)], 1).astype(BF))
        x = 2 * q + j
        out[j] = (
            grad[x] + psx[x] * lam[:, :CZ] + psy[x] * lam[:, CZ:]
            + gs[x] * rest[:, :CZ] - inv[x] * inv[x] * rest[:, CZ:]
        )


def output_kernel(ex, ey, h, ez, inv, keep, recv, w, e_o, h_o, e_s, h_s, sems):
    wt = w[...].T
    table = edge_table(wt[0:1, :], wt[CZ - 1:CZ, :])
    lane = iota((CZ, CZ), 1)
    piece = iota((CZ, CZ), 0) // 8
    ones = jnp.where((piece >= 6) & (piece < 9) & (lane == CZ - 1), 1.0, 0.0)

    def edges(i):
        return columns(edge_rows(keep, recv, i), edge_rows(keep, recv, 4 + i))

    def corrected(source, table, row):
        return mm(source, picked(table, row).astype(BF))

    def copies(x):
        at = pl.ds(x, 1)
        return (
            pltpu.make_async_copy(e_s.at[:, at], e_o.at[:, at], sems.at[0, x]),
            pltpu.make_async_copy(h_s.at[:, at], h_o.at[:, at], sems.at[1, x]),
        )

    def one_pair(i, carry):
        cols, hy_prev = carry
        last = i == X // 2 - 1
        cols_next = edges(jnp.minimum(i + 1, X // 2 - 1))
        x = 2 * i
        more = jnp.where(last, 0.0, 1.0)
        following = jnp.minimum(x + 2, X - 1)
        e_x = [ex[x + j] + corrected(cols, table, 4 * j) for j in range(2)]
        e_y = [ey[x + j] + corrected(cols, table, 4 * j + 1) for j in range(2)]
        e_y.append((ey[following] + corrected(cols_next, table, 1)) * more)
        e_z = [ez[x], ez[x + 1], ez[following] * more]
        for j in range(2):
            hy = h[1, x + j] + z_up(e_x[j]) + corrected(cols, ones, 4 * j) - (e_z[j + 1] - e_z[j])
            hx = h[0, x + j] + z_up(e_y[j]) + corrected(cols, ones, 4 * j + 1) - y_up(e_z[j])
            curl = hy - hy_prev - y_down(hx)
            hy_prev = hy
            e_s[0, x + j] = e_x[j]
            e_s[1, x + j] = e_y[j]
            e_s[2, x + j] = e_z[j] + inv[x + j] * curl
            h_s[0, x + j] = hx
            h_s[1, x + j] = hy
            h_s[2, x + j] = h[2, x + j] - (e_y[j + 1] - e_y[j]) + y_up(e_x[j])
            for copy in copies(x + j):
                copy.start()
        return cols_next, hy_prev

    lax.fori_loop(0, X // 2, one_pair, (edges(0), jnp.zeros((Y, CZ), F32)))
    for x in range(X):
        for copy in copies(x):
            copy.wait()


def place_kernel(g2, g1, g3, g0, out, sems):
    src = lax.axis_index("src")
    copies = []
    for k, g in zip((2, 1, 3, 0), (g2, g1, g3, g0)):
        copies.append(pltpu.make_async_copy(g, out.at[pl.ds(2 * (src ^ k), 2)], sems.at[k]))
    for copy in copies:
        copy.start()
    for copy in copies:
        copy.wait()


def swap(block, axis, mask):
    return lax.ppermute(block, axis, [(i, i ^ mask) for i in range(lax.axis_size(axis))])


SMEM = pl.BlockSpec(memory_space=pltpu.SMEM)
VMEM = pl.BlockSpec(memory_space=pltpu.VMEM)
HBM = pl.BlockSpec(memory_space=pltpu.HBM)
ANY = pl.BlockSpec(memory_space=pl.ANY)


def shape(*dims):
    return jax.ShapeDtypeStruct(dims, F32)


def call(kernel, name, in_specs, outs, us, mib, out_specs=None, scratch=()):
    return pl.pallas_call(
        kernel,
        in_specs=in_specs,
        out_specs=out_specs or [VMEM] * len(outs),
        out_shape=outs,
        scratch_shapes=scratch,
        compiler_params=pltpu.CompilerParams(vmem_limit_bytes=mib * MIB),
        cost_estimate=pl.CostEstimate(flops=1000, bytes_accessed=int(us * 3.0e6), transcendentals=0),
        name=name,
    )


def in_hbm(array):
    return pltpu.with_memory_space_constraint(array, pltpu.HBM)


def body(
    fields_e, fields_h, cot_e, cot_h, labels, region_eps, angle_index, profiles, zsheet,
    layer_term, block_inverse,
):
    e, h, ge, gh = fields_e[0], fields_h[0], cot_e[0], cot_h[0]
    zs, lt = zsheet.reshape(1, CZ), layer_term.reshape(1, CZ)
    slab = shape(X, Y, CZ)
    message = shape(SLABS, 8, CZ)

    def space(*dims, dtype=F32):
        return pltpu.VMEM(dims, dtype)

    rx, ry, ax, ay, psx, psy, gs, inv, hv, w, keep, send = call(
        rhs_kernel, "right_hand_sides",
        [SMEM, SMEM] + [HBM] * 9,
        [slab] * 8 + [shape(3, X, Y, CZ), shape(CZ, CZ)] + [message] * 2,
        6, 24,
        scratch=[
            space(2, X, Y, CZ), space(3, X, Y, CZ), space(3, X, Y, CZ),
            space(X, Y, CZ, dtype=jnp.int32), pltpu.SemaphoreType.DMA((6, X)),
            space(Y, CZ, dtype=BF), space(2, X, Y), space(1, CZ), space(1, CZ),
        ],
    )(angle_index, *map(in_hbm, (region_eps, e, h, ge, gh, labels, profiles, zs, lt, block_inverse)))

    other = swap(send, "gz", 1)
    (m0,) = call(chip_kernel, "chip", [VMEM] * 2, [message], 0.5, 4)(keep, other)
    m1, m2, m3 = (swap(m0, "gz", 2 * k) for k in (1, 2, 3))

    adjoint, ez = call(
        adjoint_kernel, "adjoint_products", [VMEM] * 5 + [HBM, ANY], [slab] * 2, 3, 8,
        scratch=[pltpu.SemaphoreType.DMA],
    )(ax, ay, psx, psy, w, in_hbm(e), m0)
    (n0,) = call(group_kernel, "group", [VMEM] * 4 + [ANY], [message], 0.5, 4)(m0, m1, m2, m3, adjoint)
    n1, n2, n3 = (swap(n0, "gz", 8 * k) for k in (1, 2, 3))

    ex, ey, grad = call(primal_kernel, "primal_products", [VMEM] * 7 + [ANY], [slab] * 3, 4, 8)(
        rx, ry, hv, ez, gs, adjoint, w, n0
    )
    own_edges, send_edges = call(
        back_kernel, "back", [VMEM] * 10 + [ANY], [shape(12, 8, CZ)] * 2, 0.5, 4
    )(keep, other, m0, m1, m2, m3, n0, n1, n2, n3, ex)
    other_edges = swap(send_edges, "gz", 1)

    def gradient(k):
        return call(
            lambda *refs: gradient_kernel(k, *refs), f"gradient_{k}", [VMEM] * 8,
            [shape(2, Y, CZ)], 1, 8,
        )(grad, psx, psy, gs, inv, own_edges, other_edges, w)[0]

    arrived = [swap(gradient(k), "src", k) for k in (2, 1, 3)]
    own = gradient(0)

    e_new, h_new = call(
        output_kernel, "outputs", [VMEM] * 8, [shape(3, X, Y, CZ)] * 2, 6, 16,
        out_specs=[HBM] * 2,
        scratch=[space(3, X, Y, CZ), space(3, X, Y, CZ), pltpu.SemaphoreType.DMA((2, X))],
    )(ex, ey, hv, ez, inv, own_edges, other_edges, w)

    total = own + arrived[0] + arrived[1] + arrived[2]
    two, one, three = (swap(total, "src", k) for k in (2, 1, 3))
    (eps_grad,) = call(
        place_kernel, "place", [ANY] * 4, [slab], 1, 4, out_specs=[HBM],
        scratch=[pltpu.SemaphoreType.DMA((4,))],
    )(two, one, three, total)
    return (e_new[None], h_new[None], eps_grad)


def solution(mesh):
    field = P("src", None, None, None, "gz")
    return jax.shard_map(
        body,
        mesh=mesh,
        in_specs=(
            field, field, field, field, P(None, None, "gz"), P(), P("src"), P(), P("gz"), P("gz"),
            P("gz", None),
        ),
        out_specs=(field, field, P(None, None, "gz")),
        check_vma=False,
    )
```

```python
import jax
import jax.numpy as jnp
from jax import lax
from jax.experimental import pallas as pl
from jax.experimental.pallas import tpu as pltpu
from jax.sharding import PartitionSpec as P

F32 = jnp.float32
BF = jnp.bfloat16
X, Y, CZ = 8, 256, 128
NN = (((1,), (0,)), ((), ()))
NT = (((1,), (1,)), ((), ()))
SLABS = 12
CORNERS = SLABS - 1
MIB = 1024 * 1024


def split(v):
    one = v.astype(BF)
    rest = v - one.astype(F32)
    two = rest.astype(BF)
    three = (rest - two.astype(F32)).astype(BF)
    return one, two, three


def in_two(v):
    one = v.astype(BF)
    return jnp.concatenate([one, (v - one.astype(F32)).astype(BF)], 1)


def mm(a, b, dims=NN):
    return lax.dot_general(a, b, dims, preferred_element_type=F32)


def iota(shape, axis):
    return lax.broadcasted_iota(jnp.int32, shape, axis)


def y_down(v):
    return v - jnp.where(iota(v.shape, 0) == 0, 0.0, pltpu.roll(v, 1, 0))


def y_up(v):
    n = v.shape[0]
    return jnp.where(iota(v.shape, 0) == n - 1, 0.0, pltpu.roll(v, n - 1, 0)) - v


def z_down(v):
    return v - jnp.where(iota(v.shape, 1) == 0, 0.0, pltpu.roll(v, 1, 1))


def z_up(v):
    n = v.shape[1]
    return jnp.where(iota(v.shape, 1) == n - 1, 0.0, pltpu.roll(v, n - 1, 1)) - v


def inverse_eps(labels, eps_ref):
    rows = [1.0 / jnp.full((1, CZ), eps_ref[r], F32) for r in range(4)]
    out = jnp.where(labels == 2, rows[2], rows[3])
    out = jnp.where(labels == 1, rows[1], out)
    return jnp.where(labels == 0, rows[0], out)


def six_rows(rows):
    one, two, three = (part.astype(F32) for part in split(rows))
    return [one, two, three, one, two, one]


def six_table(line, piece):
    one, two, three = (part.astype(F32) for part in split(line))
    return jnp.where(piece < 3, one, jnp.where(piece < 5, two, three))


def rhs_kernel(
    angle, eps, e, h, ge, gh, lab, prof_in, zs_in, lt_in, w_in,
    rx_o, ry_o, ax_o, ay_o, psx_o, psy_o, gs_o, inv_o, h_o, w, mine_o,
    e_s, ge_s, gh_s, lab_s, sems, prof_s, prof, zs, lt,
):
    def fetch(which, x):
        at = pl.ds(x, 1)
        return (
            lambda: pltpu.make_async_copy(lab.at[at], lab_s.at[at], sems.at[0, x]),
            lambda: pltpu.make_async_copy(ge.at[:, at], ge_s.at[:, at], sems.at[1, x]),
            lambda: pltpu.make_async_copy(h.at[:, at], h_o.at[:, at], sems.at[2, x]),
            lambda: pltpu.make_async_copy(gh.at[:, at], gh_s.at[:, at], sems.at[3, x]),
            lambda: pltpu.make_async_copy(e.at[pl.ds(0, 2), at], e_s.at[:, at], sems.at[4, x]),
        )[which]()

    tables = [
        pltpu.make_async_copy(source, target, sems.at[5, n + 1])
        for n, (source, target) in enumerate(
            ((prof_in.at[angle[0]], prof), (w_in, w), (zs_in, zs), (lt_in, lt))
        )
    ]
    for copy in tables:
        copy.start()
    early, late = (0, 1), (2, 3, 4)
    for which in early:
        fetch(which, 0).start()
    for x in range(X):
        if x + 1 < X:
            for which in early:
                fetch(which, x + 1).start()
        for which in late:
            fetch(which, x).start()

    for copy in tables:
        copy.wait()
    both = jnp.concatenate([prof[0], prof[1]], 0)
    rows = jnp.concatenate(six_rows(both) + [jnp.zeros((32, Y), F32)], 0)
    prof_s[...] = rows.T.astype(BF)
    corners = [
        jnp.broadcast_to(w[p:p + 1, q:q + 1], (1, Y))
        for p, q in ((0, 0), (0, CZ - 1), (CZ - 1, CZ - 1))
    ]
    mine_o[CORNERS] = jnp.concatenate(corners + [jnp.zeros((5, Y), F32)], 0)

    row16 = iota((16, CZ), 0)
    lane16 = iota((16, CZ), 1)
    ends = jnp.where(row16 < 8, w[0:1, :], w[CZ - 1:CZ, :])
    ends_parts = [part.astype(F32) for part in split(ends)]
    slot = lax.rem(row16, 8)

    rowz = iota((CZ, CZ), 0)
    piece, within = rowz // 16, lax.rem(rowz, 16)
    z_table = jnp.where(piece < 6, six_table(zs[...], piece), 0.0)

    lane = iota((Y, CZ), 1)
    row8 = iota((8, Y), 0)
    for which in early:
        fetch(which, 0).wait()
    inv_o[0] = inverse_eps(lab_s[0], eps)

    def one_pair(i, carry):
        acc_ends = jnp.zeros((16, Y), F32)
        acc_tops = jnp.zeros((16, Y), F32)
        for j in range(2):
            x = 2 * i + j
            following = jnp.minimum(x + 1, X - 1)
            previous = jnp.maximum(x - 1, 0)
            more = (x < X - 1).astype(F32)
            less = (x > 0).astype(F32)

            @pl.when(x < X - 1)
            def _():
                for which in early:
                    fetch(which, x + 1).wait()

            for which in late:
                fetch(which, x).wait()
            inv = inv_o[x]
            inv_up = inverse_eps(lab_s[following], eps)
            inv_o[following] = inv_up
            sg = inv * ge_s[2, x]
            sg_up = inv_up * ge_s[2, following] * more
            z_pick = jnp.concatenate(
                [jnp.where(within == x, z_table, 0.0), jnp.where(within == 8 + x, z_table, 0.0)], 1
            ).astype(BF)
            cur = mm(prof_s[...], z_pick)
            h_x, h_y, h_z = h_o[0, x], h_o[1, x], h_o[2, x]
            g_hz = gh_s[2, x]
            bar_hy = gh_s[1, x] - (sg_up - sg)
            bar_hx = gh_s[0, x] + y_up(sg)
            p_x = y_down(h_z) - z_down(h_y) - cur[:, :CZ]
            p_y = z_down(h_x) - (h_z - h_o[2, previous] * less) - cur[:, CZ:]
            r_x = lt[...] * e_s[0, x] + inv * p_x
            r_y = lt[...] * e_s[1, x] + inv * p_y
            a_x = ge_s[0, x] - y_down(g_hz) - z_down(bar_hy)
            a_y = ge_s[1, x] + (g_hz - gh_s[2, previous] * less) - z_down(bar_hx)
            rx_o[x], ry_o[x], ax_o[x], ay_o[x] = r_x, r_y, a_x, a_y
            psx_o[x] = -inv * (inv * p_x)
            psy_o[x] = -inv * (inv * p_y)
            gs_o[x] = -inv * sg
            for c, field in enumerate((r_x, r_y, a_x, a_y)):
                mask = slot == 4 * j + c
                lhs = jnp.concatenate([jnp.where(mask, part, 0.0) for part in ends_parts], 0)
                lhs = jnp.concatenate([lhs, lhs], 1).astype(BF)
                out = mm(lhs, in_two(field), NT)
                acc_ends += out[0:16] + out[16:32] + out[32:48]

            packed = jnp.where(lane == CZ - 1, h_y, inv)
            packed = jnp.where(lane == CZ - 2, -pltpu.roll(h_x, CZ - 1, 1), packed)
            packed = jnp.where(lane == CZ - 3, pltpu.roll(bar_hy, CZ - 2, 1), packed)
            packed = jnp.where(lane == CZ - 4, pltpu.roll(bar_hx, CZ - 3, 1), packed)
            c16 = slot - 4 * j
            own = (c16 >= 0) & (c16 < 4)
            pick = jnp.where(
                own & (row16 < 8) & (lane16 == CZ - 1 - c16), 1.0,
                jnp.where(own & (row16 >= 8) & (c16 == i) & (lane16 == 0), 1.0, 0.0),
            )
            acc_tops += mm(jnp.concatenate([pick, pick], 1).astype(BF), in_two(packed), NT)

        tops, planes = acc_tops[0:8], acc_tops[8:16]
        comp = lax.rem(row8, 4)
        second = lax.rem(i, 2)
        mine_o[i] = acc_ends[0:8]
        mine_o[4 + i] = acc_ends[8:16] + jnp.where(comp >= 2, tops, 0.0)
        tops = jnp.where(second == 0, tops, pltpu.roll(tops, 2, 0))
        slab = 8 + i // 2
        mine_o[slab] = jnp.where(comp // 2 == second, tops, mine_o[slab])
        mine_o[10] = jnp.where(comp == i, planes, mine_o[10])
        return carry

    lax.fori_loop(0, X // 2, one_pair, 0)


def unpack(ref):
    m = ref[...]
    comp = lax.rem(iota((8, Y), 0), 4)
    tops = [jnp.where(comp < 2, v, 0.0) for p in (m[8], m[9]) for v in (p, pltpu.roll(p, 6, 0))]
    planes = m[10]

    def plane(q):
        return jnp.where(
            comp == 0, pltpu.roll(planes, (8 - q) % 8, 0),
            jnp.where(comp == 1, pltpu.roll(planes, (9 - q) % 8, 0), 0.0),
        )

    return dict(
        f=m[0:4], l=m[4:8], t=jnp.stack(tops), k=jnp.stack([plane(q) for q in range(4)]),
        a=m[CORNERS, 0:1, :], c=m[CORNERS, 1:2, :], z=m[CORNERS, 2:3, :],
    )


def repack(s, ref):
    comp = lax.rem(iota((8, Y), 0), 4)
    ref[0:4] = s["f"]
    ref[4:8] = s["l"]
    for p in range(2):
        ref[8 + p] = jnp.where(comp < 2, s["t"][2 * p], pltpu.roll(s["t"][2 * p + 1], 2, 0))
    planes = s["k"][0]
    for q in range(1, 4):
        planes = jnp.where(comp == q, pltpu.roll(s["k"][q], q, 0), planes)
    ref[10] = planes
    ref[CORNERS] = jnp.concatenate([s["a"], s["c"], s["z"], jnp.zeros((5, Y), F32)], 0)


def order(bit, own, other):
    lower = {n: jnp.where(bit == 0, own[n], other[n]) for n in own}
    upper = {n: jnp.where(bit == 0, other[n], own[n]) for n in own}
    return lower, upper


def coupled(lower, upper):
    delta = upper["k"] * lower["t"]
    f_up = upper["f"] + upper["a"] * delta
    l_up = upper["l"] + upper["c"] * delta
    inv = 1.0 / (1.0 - upper["a"] * lower["z"])
    return f_up, l_up, inv


def combine(lower, upper):
    f_up, l_up, inv = coupled(lower, upper)
    t = (f_up + upper["a"] * lower["l"]) * inv
    u = (lower["l"] + lower["z"] * f_up) * inv
    return dict(
        f=lower["f"] + lower["c"] * t,
        l=l_up + upper["c"] * u,
        t=upper["t"],
        k=lower["k"],
        a=lower["a"] + lower["c"] * lower["c"] * upper["a"] * inv,
        c=lower["c"] * upper["c"] * inv,
        z=upper["z"] + upper["c"] * upper["c"] * lower["z"] * inv,
    )


def outside(lower, upper, below, above):
    f_up, _, inv = coupled(lower, upper)
    l_low = lower["l"] + lower["c"] * below
    f_up = f_up + upper["c"] * above
    return (f_up + upper["a"] * l_low) * inv, (l_low + lower["z"] * f_up) * inv


def pick_outside(bit, lower, upper, below, above):
    t, u = outside(lower, upper, below, above)
    return jnp.where(bit == 0, below, u), jnp.where(bit == 0, t, above)


def bits():
    gz = lax.axis_index("gz")
    return lax.rem(gz // 2, 2), lax.rem(gz // 4, 2), lax.rem(gz // 8, 2), gz // 16


def chip_kernel(own, other, out):
    repack(combine(unpack(other), unpack(own)), out)


def four(low, high, own, m1, m2, m3):
    first = order(low, own, m1)
    pair = combine(*first)
    return first, order(high, pair, combine(*order(low, m2, m3)))


def group_kernel(m0, m1, m2, m3, after, out):
    low, high, _, _ = bits()
    repack(combine(*four(low, high, *(unpack(m) for m in (m0, m1, m2, m3)))[1]), out)


def back_kernel(a0, a1, m0, m1, m2, m3, n0, n1, n2, n3, after, keep_o, send_o):
    zl, zh, xl, xh = bits()
    chip = unpack(a1), unpack(a0)
    m0, m1, m2, m3 = (unpack(m) for m in (m0, m1, m2, m3))
    n0, n1, n2, n3 = (unpack(n) for n in (n0, n1, n2, n3))
    z_first, z_second = four(zl, zh, m0, m1, m2, m3)
    x_first, x_second = four(xl, xh, n0, n1, n2, n3)
    zero = jnp.zeros_like(m0["f"])
    edge = (zero, zero)
    edge = pick_outside(xh, *x_second, *edge)
    edge = pick_outside(xl, *x_first, *edge)
    edge = pick_outside(zh, *z_second, *edge)
    edge = pick_outside(zl, *z_first, *edge)
    lower, upper = chip
    t, u = outside(lower, upper, *edge)
    under_x = jnp.where(xl == 1, n1["t"], jnp.where(xh == 1, n3["t"], zero))
    under = jnp.where(zl == 1, m1["t"], jnp.where(zh == 1, m3["t"], under_x))
    pairs = ((send_o, lower, edge[0], t, under), (keep_o, upper, u, edge[1], lower["t"]))
    for out, block, below, above, plane in pairs:
        below = below + block["k"] * plane
        first = block["f"] + block["a"] * below + block["c"] * above
        out[0:4] = below
        out[4:8] = above
        out[8:12] = jnp.stack([first[q] * pltpu.roll(plane[q], 2, 0) for q in range(4)])


def product_tables(w):
    one, two, three = split(w.T)
    full = jnp.concatenate([one, two], 1)
    return jnp.concatenate([full, full], 0), jnp.concatenate([one, three], 0)


def product(field, tables):
    one, two, three = split(field)
    wide = mm(jnp.concatenate([one, two], 1), tables[0])
    narrow = mm(jnp.concatenate([three, one], 1), tables[1])
    return wide[:, :CZ] + wide[:, CZ:] + narrow


def adjoint_kernel(ax, ay, psx, psy, w, e, after, out, ez_o, sem):
    ez_copy = pltpu.make_async_copy(e.at[2], ez_o, sem)
    ez_copy.start()
    tables = product_tables(w[...])

    def one(x, carry):
        out[x] = psx[x] * product(ax[x], tables) + psy[x] * product(ay[x], tables)
        return carry

    lax.fori_loop(0, X, one, 0, unroll=2)
    ez_copy.wait()


def primal_kernel(rx, ry, h, ez, gs, part, w, after, ex_o, ey_o, grad_o):
    tables = product_tables(w[...])

    def one(x, hy_prev):
        more = (x < X - 1).astype(F32)
        e_x, e_y = product(rx[x], tables), product(ry[x], tables)
        ex_o[x], ey_o[x] = e_x, e_y
        e_z = ez[x]
        hy = h[1, x] + z_up(e_x) - (ez[jnp.minimum(x + 1, X - 1)] * more - e_z)
        hx = h[0, x] + z_up(e_y) - y_up(e_z)
        grad_o[x] = part[x] + gs[x] * (hy - hy_prev - y_down(hx))
        return hy

    lax.fori_loop(0, X, one, jnp.zeros((Y, CZ), F32), unroll=2)


def edge_rows(keep, recv, slab):
    return jnp.where(lax.rem(lax.axis_index("gz"), 2) == 0, recv[slab], keep[slab])


def columns(below, above):
    rows = six_rows(below) + six_rows(above) + [jnp.zeros((32, Y), F32)]
    return jnp.concatenate(rows, 0).T.astype(BF)


def edge_table(first, last):
    piece = iota((CZ, CZ), 0) // 8
    table = jnp.where(piece < 6, six_table(first, piece), six_table(last, piece - 6))
    return jnp.where(piece < 12, table, 0.0)


def picked(table, row):
    return jnp.where(lax.rem(iota((CZ, CZ), 0), 8) == row, table, 0.0)


def gradient_kernel(k, grad, psx, psy, gs, inv, keep, recv, w, out):
    q = lax.axis_index("src") ^ k
    below, above, extra = (edge_rows(keep, recv, 4 * part + q) for part in range(3))
    before = jnp.maximum(q - 1, 0)
    has = (q > 0).astype(F32)
    row = iota((8, Y), 0)
    lane = iota((8, Y), 1)

    def curl_rows(now, previous):
        shifted = jnp.where(row < 4, pltpu.roll(previous, 4, 0), pltpu.roll(now, 4, 0))
        along_y = now - jnp.where(lane == 0, 0.0, pltpu.roll(now, 1, 1))
        return now - shifted - pltpu.roll(along_y, 7, 0)

    curl_below = curl_rows(below, edge_rows(keep, recv, before) * has)
    curl_above = curl_rows(above, edge_rows(keep, recv, 4 + before) * has)
    kind = lax.rem(row, 4)
    plane = pltpu.roll(extra, 7, 0) + pltpu.roll(extra, 6, 0)
    below = jnp.where(kind == 0, curl_below, jnp.where(kind == 1, plane, below))
    above = jnp.where(kind == 0, curl_above, jnp.where(kind == 1, 0.0, above))
    cols = columns(below, above)
    wt = w[...].T
    first, last = wt[0:1, :], wt[CZ - 1:CZ, :]
    lane1 = iota((1, CZ), 1)
    top = jnp.where(lane1 == CZ - 1, 1.0, 0.0)
    first_up = jnp.where(lane1 == CZ - 1, 0.0, pltpu.roll(first, CZ - 1, 1)) - first
    last_up = jnp.where(lane1 == CZ - 1, 0.0, pltpu.roll(last, CZ - 1, 1)) - last + top
    lam_table = edge_table(first, last)
    curl_table = edge_table(first_up, last_up)
    plane_table = edge_table(jnp.where(lane1 == 0, 1.0, 0.0), jnp.zeros((1, CZ), F32))
    for j in range(2):
        r = 4 * j
        lam = mm(cols, jnp.concatenate([picked(lam_table, r + 2), picked(lam_table, r + 3)], 1).astype(BF))
        rest = mm(cols, jnp.concatenate([picked(curl_table, r), picked(plane_table, r + 1)], 1).astype(BF))
        x = 2 * q + j
        out[j] = (
            grad[x] + psx[x] * lam[:, :CZ] + psy[x] * lam[:, CZ:]
            + gs[x] * rest[:, :CZ] - inv[x] * inv[x] * rest[:, CZ:]
        )


def output_kernel(ex, ey, h, ez, inv, keep, recv, w, e_o, h_o, e_s, h_s, sems):
    wt = w[...].T
    table = edge_table(wt[0:1, :], wt[CZ - 1:CZ, :])
    lane = iota((CZ, CZ), 1)
    piece = iota((CZ, CZ), 0) // 8
    ones = jnp.where((piece >= 6) & (piece < 9) & (lane == CZ - 1), 1.0, 0.0)

    def edges(i):
        return columns(edge_rows(keep, recv, i), edge_rows(keep, recv, 4 + i))

    def corrected(source, table, row):
        return mm(source, picked(table, row).astype(BF))

    def copies(x):
        at = pl.ds(x, 1)
        return (
            pltpu.make_async_copy(e_s.at[:, at], e_o.at[:, at], sems.at[0, x]),
            pltpu.make_async_copy(h_s.at[:, at], h_o.at[:, at], sems.at[1, x]),
        )

    def one_pair(i, carry):
        cols, hy_prev = carry
        last = i == X // 2 - 1
        cols_next = edges(jnp.minimum(i + 1, X // 2 - 1))
        x = 2 * i
        more = jnp.where(last, 0.0, 1.0)
        following = jnp.minimum(x + 2, X - 1)
        e_x = [ex[x + j] + corrected(cols, table, 4 * j) for j in range(2)]
        e_y = [ey[x + j] + corrected(cols, table, 4 * j + 1) for j in range(2)]
        e_y.append((ey[following] + corrected(cols_next, table, 1)) * more)
        e_z = [ez[x], ez[x + 1], ez[following] * more]
        for j in range(2):
            hy = h[1, x + j] + z_up(e_x[j]) + corrected(cols, ones, 4 * j) - (e_z[j + 1] - e_z[j])
            hx = h[0, x + j] + z_up(e_y[j]) + corrected(cols, ones, 4 * j + 1) - y_up(e_z[j])
            curl = hy - hy_prev - y_down(hx)
            hy_prev = hy
            e_s[0, x + j] = e_x[j]
            e_s[1, x + j] = e_y[j]
            e_s[2, x + j] = e_z[j] + inv[x + j] * curl
            h_s[0, x + j] = hx
            h_s[1, x + j] = hy
            h_s[2, x + j] = h[2, x + j] - (e_y[j + 1] - e_y[j]) + y_up(e_x[j])
            for copy in copies(x + j):
                copy.start()
        return cols_next, hy_prev

    lax.fori_loop(0, X // 2, one_pair, (edges(0), jnp.zeros((Y, CZ), F32)))
    for x in range(X):
        for copy in copies(x):
            copy.wait()


def place_kernel(g2, g1, g3, g0, out, sems):
    src = lax.axis_index("src")
    copies = []
    for k, g in zip((2, 1, 3, 0), (g2, g1, g3, g0)):
        copies.append(pltpu.make_async_copy(g, out.at[pl.ds(2 * (src ^ k), 2)], sems.at[k]))
    for copy in copies:
        copy.start()
    for copy in copies:
        copy.wait()


def swap(block, axis, mask):
    return lax.ppermute(block, axis, [(i, i ^ mask) for i in range(lax.axis_size(axis))])


def among_second(block, mask):
    return lax.ppermute(block, "gz", [(i, i ^ mask) for i in range(1, lax.axis_size("gz"), 2)])


def across_chip(block, source):
    chips = range(0, lax.axis_size("gz"), 2)
    return lax.ppermute(block, "gz", [(i + source, i + 1 - source) for i in chips])


SMEM = pl.BlockSpec(memory_space=pltpu.SMEM)
VMEM = pl.BlockSpec(memory_space=pltpu.VMEM)
HBM = pl.BlockSpec(memory_space=pltpu.HBM)
ANY = pl.BlockSpec(memory_space=pl.ANY)


def shape(*dims):
    return jax.ShapeDtypeStruct(dims, F32)


def call(kernel, name, in_specs, outs, us, mib, out_specs=None, scratch=()):
    return pl.pallas_call(
        kernel,
        in_specs=in_specs,
        out_specs=out_specs or [VMEM] * len(outs),
        out_shape=outs,
        scratch_shapes=scratch,
        compiler_params=pltpu.CompilerParams(vmem_limit_bytes=mib * MIB),
        cost_estimate=pl.CostEstimate(flops=1000, bytes_accessed=int(us * 3.0e6), transcendentals=0),
        name=name,
    )


def in_hbm(array):
    return pltpu.with_memory_space_constraint(array, pltpu.HBM)


def body(
    fields_e, fields_h, cot_e, cot_h, labels, region_eps, angle_index, profiles, zsheet,
    layer_term, block_inverse,
):
    e, h, ge, gh = fields_e[0], fields_h[0], cot_e[0], cot_h[0]
    zs, lt = zsheet.reshape(1, CZ), layer_term.reshape(1, CZ)
    slab = shape(X, Y, CZ)
    message = shape(SLABS, 8, Y)

    def space(*dims, dtype=F32):
        return pltpu.VMEM(dims, dtype)

    rx, ry, ax, ay, psx, psy, gs, inv, hv, w, mine = call(
        rhs_kernel, "right_hand_sides",
        [SMEM, SMEM] + [HBM] * 9,
        [slab] * 8 + [shape(3, X, Y, CZ), shape(CZ, CZ)] + [message],
        6, 24,
        scratch=[
            space(2, X, Y, CZ), space(3, X, Y, CZ), space(3, X, Y, CZ),
            space(X, Y, CZ, dtype=jnp.int32), pltpu.SemaphoreType.DMA((6, X)),
            space(Y, CZ, dtype=BF), space(2, X, Y), space(1, CZ), space(1, CZ),
        ],
    )(angle_index, *map(in_hbm, (region_eps, e, h, ge, gh, labels, profiles, zs, lt, block_inverse)))

    other = across_chip(mine, 0)
    (m0,) = call(chip_kernel, "chip", [VMEM] * 2, [message], 0.5, 4)(mine, other)
    m1, m2, m3 = (among_second(m0, 2 * k) for k in (1, 2, 3))

    adjoint, ez = call(
        adjoint_kernel, "adjoint_products", [VMEM] * 5 + [HBM, ANY], [slab] * 2, 3, 8,
        scratch=[pltpu.SemaphoreType.DMA],
    )(ax, ay, psx, psy, w, in_hbm(e), m0)
    (n0,) = call(group_kernel, "group", [VMEM] * 4 + [ANY], [message], 0.5, 4)(m0, m1, m2, m3, adjoint)
    n1, n2, n3 = (among_second(n0, 8 * k) for k in (1, 2, 3))

    ex, ey, grad = call(primal_kernel, "primal_products", [VMEM] * 7 + [ANY], [slab] * 3, 4, 8)(
        rx, ry, hv, ez, gs, adjoint, w, n0
    )
    own_edges, send_edges = call(
        back_kernel, "back", [VMEM] * 10 + [ANY], [shape(12, 8, Y)] * 2, 0.5, 4
    )(mine, other, m0, m1, m2, m3, n0, n1, n2, n3, ex)
    other_edges = across_chip(send_edges, 1)

    def gradient(k):
        return call(
            lambda *refs: gradient_kernel(k, *refs), f"gradient_{k}", [VMEM] * 8,
            [shape(2, Y, CZ)], 1, 8,
        )(grad, psx, psy, gs, inv, own_edges, other_edges, w)[0]

    arrived = [swap(gradient(k), "src", k) for k in (2, 1, 3)]
    own = gradient(0)

    e_new, h_new = call(
        output_kernel, "outputs", [VMEM] * 8, [shape(3, X, Y, CZ)] * 2, 6, 16,
        out_specs=[HBM] * 2,
        scratch=[space(3, X, Y, CZ), space(3, X, Y, CZ), pltpu.SemaphoreType.DMA((2, X))],
    )(ex, ey, hv, ez, inv, own_edges, other_edges, w)

    total = own + arrived[0] + arrived[1] + arrived[2]
    two, one, three = (swap(total, "src", k) for k in (2, 1, 3))
    (eps_grad,) = call(
        place_kernel, "place", [ANY] * 4, [slab], 1, 4, out_specs=[HBM],
        scratch=[pltpu.SemaphoreType.DMA((4,))],
    )(two, one, three, total)
    return (e_new[None], h_new[None], eps_grad)


def solution(mesh):
    field = P("src", None, None, None, "gz")
    return jax.shard_map(
        body,
        mesh=mesh,
        in_specs=(
            field, field, field, field, P(None, None, "gz"), P(), P("src"), P(), P("gz"), P("gz"),
            P("gz", None),
        ),
        out_specs=(field, field, P(None, None, "gz")),
        check_vma=False,
    )
```

```python
import jax
import jax.numpy as jnp
from jax import lax
from jax.experimental import pallas as pl
from jax.experimental.pallas import tpu as pltpu
from jax.sharding import PartitionSpec as P

F32 = jnp.float32
BF = jnp.bfloat16
X, Y, CZ = 8, 256, 128
NN = (((1,), (0,)), ((), ()))
NT = (((1,), (1,)), ((), ()))
SLABS = 12
CORNERS = SLABS - 1
MIB = 1024 * 1024


def split(v):
    one = v.astype(BF)
    rest = v - one.astype(F32)
    two = rest.astype(BF)
    three = (rest - two.astype(F32)).astype(BF)
    return one, two, three


def in_two(v):
    one = v.astype(BF)
    return jnp.concatenate([one, (v - one.astype(F32)).astype(BF)], 1)


def mm(a, b, dims=NN):
    return lax.dot_general(a, b, dims, preferred_element_type=F32)


def iota(shape, axis):
    return lax.broadcasted_iota(jnp.int32, shape, axis)


def y_down(v):
    return v - jnp.where(iota(v.shape, 0) == 0, 0.0, pltpu.roll(v, 1, 0))


def y_up(v):
    n = v.shape[0]
    return jnp.where(iota(v.shape, 0) == n - 1, 0.0, pltpu.roll(v, n - 1, 0)) - v


def z_down(v):
    return v - jnp.where(iota(v.shape, 1) == 0, 0.0, pltpu.roll(v, 1, 1))


def z_up(v):
    n = v.shape[1]
    return jnp.where(iota(v.shape, 1) == n - 1, 0.0, pltpu.roll(v, n - 1, 1)) - v


def inverse_eps(labels, eps_ref):
    rows = [1.0 / jnp.full((1, CZ), eps_ref[r], F32) for r in range(4)]
    out = jnp.where(labels == 2, rows[2], rows[3])
    out = jnp.where(labels == 1, rows[1], out)
    return jnp.where(labels == 0, rows[0], out)


def six_rows(rows):
    one, two, three = (part.astype(F32) for part in split(rows))
    return [one, two, three, one, two, one]


def six_table(line, piece):
    one, two, three = (part.astype(F32) for part in split(line))
    return jnp.where(piece < 3, one, jnp.where(piece < 5, two, three))


def rhs_kernel(
    angle, eps, e, h, ge, gh, lab, prof_in, zs_in, lt_in, w_in,
    rx_o, ry_o, ax_o, ay_o, psx_o, psy_o, gs_o, inv_o, h_o, w, mine_o,
    e_s, ge_s, gh_s, lab_s, sems, prof_s, prof, zs, lt,
):
    def fetch(which, x):
        at = pl.ds(x, 1)
        return (
            lambda: pltpu.make_async_copy(lab.at[at], lab_s.at[at], sems.at[0, x]),
            lambda: pltpu.make_async_copy(ge.at[:, at], ge_s.at[:, at], sems.at[1, x]),
            lambda: pltpu.make_async_copy(h.at[:, at], h_o.at[:, at], sems.at[2, x]),
            lambda: pltpu.make_async_copy(gh.at[:, at], gh_s.at[:, at], sems.at[3, x]),
            lambda: pltpu.make_async_copy(e.at[pl.ds(0, 2), at], e_s.at[:, at], sems.at[4, x]),
        )[which]()

    tables = [
        pltpu.make_async_copy(source, target, sems.at[5, n + 1])
        for n, (source, target) in enumerate(
            ((prof_in.at[angle[0]], prof), (w_in, w), (zs_in, zs), (lt_in, lt))
        )
    ]
    for copy in tables:
        copy.start()
    early, late = (0, 1), (2, 3, 4)
    for which in early:
        fetch(which, 0).start()
    for x in range(X):
        if x + 1 < X:
            for which in early:
                fetch(which, x + 1).start()
        for which in late:
            fetch(which, x).start()

    for copy in tables:
        copy.wait()
    both = jnp.concatenate([prof[0], prof[1]], 0)
    rows = jnp.concatenate(six_rows(both) + [jnp.zeros((32, Y), F32)], 0)
    prof_s[...] = rows.T.astype(BF)
    corners = [
        jnp.broadcast_to(w[p:p + 1, q:q + 1], (1, Y))
        for p, q in ((0, 0), (0, CZ - 1), (CZ - 1, CZ - 1))
    ]
    mine_o[CORNERS] = jnp.concatenate(corners + [jnp.zeros((5, Y), F32)], 0)

    row16 = iota((16, CZ), 0)
    lane16 = iota((16, CZ), 1)
    ends = jnp.where(row16 < 8, w[0:1, :], w[CZ - 1:CZ, :])
    ends_parts = [part.astype(F32) for part in split(ends)]
    slot = lax.rem(row16, 8)

    rowz = iota((CZ, CZ), 0)
    piece, within = rowz // 16, lax.rem(rowz, 16)
    z_table = jnp.where(piece < 6, six_table(zs[...], piece), 0.0)

    lane = iota((Y, CZ), 1)
    row8 = iota((8, Y), 0)
    for which in early:
        fetch(which, 0).wait()
    inv_o[0] = inverse_eps(lab_s[0], eps)

    def one_pair(i, carry):
        acc_ends = jnp.zeros((16, Y), F32)
        acc_tops = jnp.zeros((16, Y), F32)
        for j in range(2):
            x = 2 * i + j
            following = jnp.minimum(x + 1, X - 1)
            previous = jnp.maximum(x - 1, 0)
            more = (x < X - 1).astype(F32)
            less = (x > 0).astype(F32)

            @pl.when(x < X - 1)
            def _():
                for which in early:
                    fetch(which, x + 1).wait()

            for which in late:
                fetch(which, x).wait()
            inv = inv_o[x]
            inv_up = inverse_eps(lab_s[following], eps)
            inv_o[following] = inv_up
            sg = inv * ge_s[2, x]
            sg_up = inv_up * ge_s[2, following] * more
            z_pick = jnp.concatenate(
                [jnp.where(within == x, z_table, 0.0), jnp.where(within == 8 + x, z_table, 0.0)], 1
            ).astype(BF)
            cur = mm(prof_s[...], z_pick)
            h_x, h_y, h_z = h_o[0, x], h_o[1, x], h_o[2, x]
            g_hz = gh_s[2, x]
            bar_hy = gh_s[1, x] - (sg_up - sg)
            bar_hx = gh_s[0, x] + y_up(sg)
            p_x = y_down(h_z) - z_down(h_y) - cur[:, :CZ]
            p_y = z_down(h_x) - (h_z - h_o[2, previous] * less) - cur[:, CZ:]
            r_x = lt[...] * e_s[0, x] + inv * p_x
            r_y = lt[...] * e_s[1, x] + inv * p_y
            a_x = ge_s[0, x] - y_down(g_hz) - z_down(bar_hy)
            a_y = ge_s[1, x] + (g_hz - gh_s[2, previous] * less) - z_down(bar_hx)
            rx_o[x], ry_o[x], ax_o[x], ay_o[x] = r_x, r_y, a_x, a_y
            psx_o[x] = -inv * (inv * p_x)
            psy_o[x] = -inv * (inv * p_y)
            gs_o[x] = -inv * sg
            for c, field in enumerate((r_x, r_y, a_x, a_y)):
                mask = slot == 4 * j + c
                lhs = jnp.concatenate([jnp.where(mask, part, 0.0) for part in ends_parts], 0)
                lhs = jnp.concatenate([lhs, lhs], 1).astype(BF)
                out = mm(lhs, in_two(field), NT)
                acc_ends += out[0:16] + out[16:32] + out[32:48]

            packed = jnp.where(lane == CZ - 1, h_y, inv)
            packed = jnp.where(lane == CZ - 2, -pltpu.roll(h_x, CZ - 1, 1), packed)
            packed = jnp.where(lane == CZ - 3, pltpu.roll(bar_hy, CZ - 2, 1), packed)
            packed = jnp.where(lane == CZ - 4, pltpu.roll(bar_hx, CZ - 3, 1), packed)
            c16 = slot - 4 * j
            own = (c16 >= 0) & (c16 < 4)
            pick = jnp.where(
                own & (row16 < 8) & (lane16 == CZ - 1 - c16), 1.0,
                jnp.where(own & (row16 >= 8) & (c16 == i) & (lane16 == 0), 1.0, 0.0),
            )
            acc_tops += mm(jnp.concatenate([pick, pick], 1).astype(BF), in_two(packed), NT)

        tops, planes = acc_tops[0:8], acc_tops[8:16]
        comp = lax.rem(row8, 4)
        second = lax.rem(i, 2)
        mine_o[i] = acc_ends[0:8]
        mine_o[4 + i] = acc_ends[8:16] + jnp.where(comp >= 2, tops, 0.0)
        tops = jnp.where(second == 0, tops, pltpu.roll(tops, 2, 0))
        slab = 8 + i // 2
        mine_o[slab] = jnp.where(comp // 2 == second, tops, mine_o[slab])
        mine_o[10] = jnp.where(comp == i, planes, mine_o[10])
        return carry

    lax.fori_loop(0, X // 2, one_pair, 0)


def unpack(ref):
    m = ref[...]
    comp = lax.rem(iota((8, Y), 0), 4)
    tops = [jnp.where(comp < 2, v, 0.0) for p in (m[8], m[9]) for v in (p, pltpu.roll(p, 6, 0))]
    planes = m[10]

    def plane(q):
        return jnp.where(
            comp == 0, pltpu.roll(planes, (8 - q) % 8, 0),
            jnp.where(comp == 1, pltpu.roll(planes, (9 - q) % 8, 0), 0.0),
        )

    return dict(
        f=m[0:4], l=m[4:8], t=jnp.stack(tops), k=jnp.stack([plane(q) for q in range(4)]),
        a=m[CORNERS, 0:1, :], c=m[CORNERS, 1:2, :], z=m[CORNERS, 2:3, :],
    )


def repack(s, ref):
    comp = lax.rem(iota((8, Y), 0), 4)
    ref[0:4] = s["f"]
    ref[4:8] = s["l"]
    for p in range(2):
        ref[8 + p] = jnp.where(comp < 2, s["t"][2 * p], pltpu.roll(s["t"][2 * p + 1], 2, 0))
    planes = s["k"][0]
    for q in range(1, 4):
        planes = jnp.where(comp == q, pltpu.roll(s["k"][q], q, 0), planes)
    ref[10] = planes
    ref[CORNERS] = jnp.concatenate([s["a"], s["c"], s["z"], jnp.zeros((5, Y), F32)], 0)


def order(bit, own, other):
    lower = {n: jnp.where(bit == 0, own[n], other[n]) for n in own}
    upper = {n: jnp.where(bit == 0, other[n], own[n]) for n in own}
    return lower, upper


def coupled(lower, upper):
    delta = upper["k"] * lower["t"]
    f_up = upper["f"] + upper["a"] * delta
    l_up = upper["l"] + upper["c"] * delta
    inv = 1.0 / (1.0 - upper["a"] * lower["z"])
    return f_up, l_up, inv


def combine(lower, upper):
    f_up, l_up, inv = coupled(lower, upper)
    t = (f_up + upper["a"] * lower["l"]) * inv
    u = (lower["l"] + lower["z"] * f_up) * inv
    return dict(
        f=lower["f"] + lower["c"] * t,
        l=l_up + upper["c"] * u,
        t=upper["t"],
        k=lower["k"],
        a=lower["a"] + lower["c"] * lower["c"] * upper["a"] * inv,
        c=lower["c"] * upper["c"] * inv,
        z=upper["z"] + upper["c"] * upper["c"] * lower["z"] * inv,
    )


def outside(lower, upper, below, above):
    f_up, _, inv = coupled(lower, upper)
    l_low = lower["l"] + lower["c"] * below
    f_up = f_up + upper["c"] * above
    return (f_up + upper["a"] * l_low) * inv, (l_low + lower["z"] * f_up) * inv


def pick_outside(bit, lower, upper, below, above):
    t, u = outside(lower, upper, below, above)
    return jnp.where(bit == 0, below, u), jnp.where(bit == 0, t, above)


def bits():
    gz = lax.axis_index("gz")
    return lax.rem(gz // 2, 2), lax.rem(gz // 4, 2), lax.rem(gz // 8, 2), gz // 16


def chip_kernel(own, other, out):
    repack(combine(unpack(other), unpack(own)), out)


def four(low, high, own, m1, m2, m3):
    first = order(low, own, m1)
    pair = combine(*first)
    return first, order(high, pair, combine(*order(low, m2, m3)))


def group_kernel(m0, m1, m2, m3, after, out):
    low, high, _, _ = bits()
    repack(combine(*four(low, high, *(unpack(m) for m in (m0, m1, m2, m3)))[1]), out)


def back_kernel(a0, a1, m0, m1, m2, m3, n0, n1, n2, n3, after, keep_o, send_o):
    zl, zh, xl, xh = bits()
    chip = unpack(a1), unpack(a0)
    m0, m1, m2, m3 = (unpack(m) for m in (m0, m1, m2, m3))
    n0, n1, n2, n3 = (unpack(n) for n in (n0, n1, n2, n3))
    z_first, z_second = four(zl, zh, m0, m1, m2, m3)
    x_first, x_second = four(xl, xh, n0, n1, n2, n3)
    zero = jnp.zeros_like(m0["f"])
    edge = (zero, zero)
    edge = pick_outside(xh, *x_second, *edge)
    edge = pick_outside(xl, *x_first, *edge)
    edge = pick_outside(zh, *z_second, *edge)
    edge = pick_outside(zl, *z_first, *edge)
    lower, upper = chip
    t, u = outside(lower, upper, *edge)
    under_x = jnp.where(xl == 1, n1["t"], jnp.where(xh == 1, n3["t"], zero))
    under = jnp.where(zl == 1, m1["t"], jnp.where(zh == 1, m3["t"], under_x))
    pairs = ((send_o, lower, edge[0], t, under), (keep_o, upper, u, edge[1], lower["t"]))
    for out, block, below, above, plane in pairs:
        below = below + block["k"] * plane
        first = block["f"] + block["a"] * below + block["c"] * above
        out[0:4] = below
        out[4:8] = above
        out[8:12] = jnp.stack([first[q] * pltpu.roll(plane[q], 2, 0) for q in range(4)])


def product_tables(w):
    one, two, three = split(w.T)
    full = jnp.concatenate([one, two], 1)
    return jnp.concatenate([full, full], 0), jnp.concatenate([one, three], 0)


def product(field, tables):
    one, two, three = split(field)
    wide = mm(jnp.concatenate([one, two], 1), tables[0])
    narrow = mm(jnp.concatenate([three, one], 1), tables[1])
    return wide[:, :CZ] + wide[:, CZ:] + narrow


def adjoint_kernel(ax, ay, psx, psy, w, e, after, out, ez_o, sem):
    ez_copy = pltpu.make_async_copy(e.at[2], ez_o, sem)
    ez_copy.start()
    tables = product_tables(w[...])

    def one(x, carry):
        out[x] = psx[x] * product(ax[x], tables) + psy[x] * product(ay[x], tables)
        return carry

    lax.fori_loop(0, X, one, 0, unroll=2)
    ez_copy.wait()


def primal_kernel(rx, ry, h, ez, gs, part, w, after, ex_o, ey_o, grad_o):
    tables = product_tables(w[...])

    def one(x, hy_prev):
        more = (x < X - 1).astype(F32)
        e_x, e_y = product(rx[x], tables), product(ry[x], tables)
        ex_o[x], ey_o[x] = e_x, e_y
        e_z = ez[x]
        hy = h[1, x] + z_up(e_x) - (ez[jnp.minimum(x + 1, X - 1)] * more - e_z)
        hx = h[0, x] + z_up(e_y) - y_up(e_z)
        grad_o[x] = part[x] + gs[x] * (hy - hy_prev - y_down(hx))
        return hy

    lax.fori_loop(0, X, one, jnp.zeros((Y, CZ), F32), unroll=2)


def edge_rows(keep, recv, slab):
    return jnp.where(lax.rem(lax.axis_index("gz"), 2) == 0, recv[slab], keep[slab])


def columns(below, above):
    rows = six_rows(below) + six_rows(above) + [jnp.zeros((32, Y), F32)]
    return jnp.concatenate(rows, 0).T.astype(BF)


def edge_table(first, last):
    piece = iota((CZ, CZ), 0) // 8
    table = jnp.where(piece < 6, six_table(first, piece), six_table(last, piece - 6))
    return jnp.where(piece < 12, table, 0.0)


def picked(table, row):
    return jnp.where(lax.rem(iota((CZ, CZ), 0), 8) == row, table, 0.0)


def gradient_kernel(k, grad, psx, psy, gs, inv, keep, recv, w, out):
    q = lax.axis_index("src") ^ k
    below, above, extra = (edge_rows(keep, recv, 4 * part + q) for part in range(3))
    before = jnp.maximum(q - 1, 0)
    has = (q > 0).astype(F32)
    row = iota((8, Y), 0)
    lane = iota((8, Y), 1)

    def curl_rows(now, previous):
        shifted = jnp.where(row < 4, pltpu.roll(previous, 4, 0), pltpu.roll(now, 4, 0))
        along_y = now - jnp.where(lane == 0, 0.0, pltpu.roll(now, 1, 1))
        return now - shifted - pltpu.roll(along_y, 7, 0)

    curl_below = curl_rows(below, edge_rows(keep, recv, before) * has)
    curl_above = curl_rows(above, edge_rows(keep, recv, 4 + before) * has)
    kind = lax.rem(row, 4)
    plane = pltpu.roll(extra, 7, 0) + pltpu.roll(extra, 6, 0)
    below = jnp.where(kind == 0, curl_below, jnp.where(kind == 1, plane, below))
    above = jnp.where(kind == 0, curl_above, jnp.where(kind == 1, 0.0, above))
    cols = columns(below, above)
    wt = w[...].T
    first, last = wt[0:1, :], wt[CZ - 1:CZ, :]
    lane1 = iota((1, CZ), 1)
    top = jnp.where(lane1 == CZ - 1, 1.0, 0.0)
    first_up = jnp.where(lane1 == CZ - 1, 0.0, pltpu.roll(first, CZ - 1, 1)) - first
    last_up = jnp.where(lane1 == CZ - 1, 0.0, pltpu.roll(last, CZ - 1, 1)) - last + top
    lam_table = edge_table(first, last)
    curl_table = edge_table(first_up, last_up)
    plane_table = edge_table(jnp.where(lane1 == 0, 1.0, 0.0), jnp.zeros((1, CZ), F32))
    for j in range(2):
        r = 4 * j
        lam = mm(cols, jnp.concatenate([picked(lam_table, r + 2), picked(lam_table, r + 3)], 1).astype(BF))
        rest = mm(cols, jnp.concatenate([picked(curl_table, r), picked(plane_table, r + 1)], 1).astype(BF))
        x = 2 * q + j
        out[j] = (
            grad[x] + psx[x] * lam[:, :CZ] + psy[x] * lam[:, CZ:]
            + gs[x] * rest[:, :CZ] - inv[x] * inv[x] * rest[:, CZ:]
        )


def output_kernel(ex, ey, h, ez, inv, keep, recv, w, e_o, h_o, e_s, h_s, sems):
    wt = w[...].T
    table = edge_table(wt[0:1, :], wt[CZ - 1:CZ, :])
    lane = iota((CZ, CZ), 1)
    piece = iota((CZ, CZ), 0) // 8
    ones = jnp.where((piece >= 6) & (piece < 9) & (lane == CZ - 1), 1.0, 0.0)

    def edges(i):
        return columns(edge_rows(keep, recv, i), edge_rows(keep, recv, 4 + i))

    def corrected(source, table, row):
        return mm(source, picked(table, row).astype(BF))

    def copies(x):
        at = pl.ds(x, 1)
        return (
            pltpu.make_async_copy(e_s.at[:, at], e_o.at[:, at], sems.at[0, x]),
            pltpu.make_async_copy(h_s.at[:, at], h_o.at[:, at], sems.at[1, x]),
        )

    def one_pair(i, carry):
        cols, hy_prev = carry
        last = i == X // 2 - 1
        cols_next = edges(jnp.minimum(i + 1, X // 2 - 1))
        x = 2 * i
        more = jnp.where(last, 0.0, 1.0)
        following = jnp.minimum(x + 2, X - 1)
        e_x = [ex[x + j] + corrected(cols, table, 4 * j) for j in range(2)]
        e_y = [ey[x + j] + corrected(cols, table, 4 * j + 1) for j in range(2)]
        e_y.append((ey[following] + corrected(cols_next, table, 1)) * more)
        e_z = [ez[x], ez[x + 1], ez[following] * more]
        for j in range(2):
            hy = h[1, x + j] + z_up(e_x[j]) + corrected(cols, ones, 4 * j) - (e_z[j + 1] - e_z[j])
            hx = h[0, x + j] + z_up(e_y[j]) + corrected(cols, ones, 4 * j + 1) - y_up(e_z[j])
            curl = hy - hy_prev - y_down(hx)
            hy_prev = hy
            e_s[0, x + j] = e_x[j]
            e_s[1, x + j] = e_y[j]
            e_s[2, x + j] = e_z[j] + inv[x + j] * curl
            h_s[0, x + j] = hx
            h_s[1, x + j] = hy
            h_s[2, x + j] = h[2, x + j] - (e_y[j + 1] - e_y[j]) + y_up(e_x[j])
            for copy in copies(x + j):
                copy.start()
        return cols_next, hy_prev

    lax.fori_loop(0, X // 2, one_pair, (edges(0), jnp.zeros((Y, CZ), F32)))
    for x in range(X):
        for copy in copies(x):
            copy.wait()


def place_kernel(g2, g1, g3, g0, out, sems):
    src = lax.axis_index("src")
    copies = []
    for k, g in zip((2, 1, 3, 0), (g2, g1, g3, g0)):
        copies.append(pltpu.make_async_copy(g, out.at[pl.ds(2 * (src ^ k), 2)], sems.at[k]))
    for copy in copies:
        copy.start()
    for copy in copies:
        copy.wait()


def swap(block, axis, mask):
    return lax.ppermute(block, axis, [(i, i ^ mask) for i in range(lax.axis_size(axis))])


def among_second(block, mask):
    pairs = [(i, i ^ mask if i % 2 else i) for i in range(lax.axis_size("gz"))]
    return lax.ppermute(block, "gz", pairs)


SMEM = pl.BlockSpec(memory_space=pltpu.SMEM)
VMEM = pl.BlockSpec(memory_space=pltpu.VMEM)
HBM = pl.BlockSpec(memory_space=pltpu.HBM)
ANY = pl.BlockSpec(memory_space=pl.ANY)


def shape(*dims):
    return jax.ShapeDtypeStruct(dims, F32)


def call(kernel, name, in_specs, outs, us, mib, out_specs=None, scratch=()):
    return pl.pallas_call(
        kernel,
        in_specs=in_specs,
        out_specs=out_specs or [VMEM] * len(outs),
        out_shape=outs,
        scratch_shapes=scratch,
        compiler_params=pltpu.CompilerParams(vmem_limit_bytes=mib * MIB),
        cost_estimate=pl.CostEstimate(flops=1000, bytes_accessed=int(us * 3.0e6), transcendentals=0),
        name=name,
    )


def in_hbm(array):
    return pltpu.with_memory_space_constraint(array, pltpu.HBM)


def body(
    fields_e, fields_h, cot_e, cot_h, labels, region_eps, angle_index, profiles, zsheet,
    layer_term, block_inverse,
):
    e, h, ge, gh = fields_e[0], fields_h[0], cot_e[0], cot_h[0]
    zs, lt = zsheet.reshape(1, CZ), layer_term.reshape(1, CZ)
    slab = shape(X, Y, CZ)
    message = shape(SLABS, 8, Y)

    def space(*dims, dtype=F32):
        return pltpu.VMEM(dims, dtype)

    rx, ry, ax, ay, psx, psy, gs, inv, hv, w, mine = call(
        rhs_kernel, "right_hand_sides",
        [SMEM, SMEM] + [HBM] * 9,
        [slab] * 8 + [shape(3, X, Y, CZ), shape(CZ, CZ)] + [message],
        6, 24,
        scratch=[
            space(2, X, Y, CZ), space(3, X, Y, CZ), space(3, X, Y, CZ),
            space(X, Y, CZ, dtype=jnp.int32), pltpu.SemaphoreType.DMA((6, X)),
            space(Y, CZ, dtype=BF), space(2, X, Y), space(1, CZ), space(1, CZ),
        ],
    )(angle_index, *map(in_hbm, (region_eps, e, h, ge, gh, labels, profiles, zs, lt, block_inverse)))

    other = swap(mine, "gz", 1)
    (m0,) = call(chip_kernel, "chip", [VMEM] * 2, [message], 0.5, 4)(mine, other)
    m1, m2, m3 = (among_second(m0, 2 * k) for k in (1, 2, 3))

    adjoint, ez = call(
        adjoint_kernel, "adjoint_products", [VMEM] * 5 + [HBM, ANY], [slab] * 2, 3, 8,
        scratch=[pltpu.SemaphoreType.DMA],
    )(ax, ay, psx, psy, w, in_hbm(e), m0)
    (n0,) = call(group_kernel, "group", [VMEM] * 4 + [ANY], [message], 0.5, 4)(m0, m1, m2, m3, adjoint)
    n1, n2, n3 = (among_second(n0, 8 * k) for k in (1, 2, 3))

    ex, ey, grad = call(primal_kernel, "primal_products", [VMEM] * 7 + [ANY], [slab] * 3, 4, 8)(
        rx, ry, hv, ez, gs, adjoint, w, n0
    )
    own_edges, send_edges = call(
        back_kernel, "back", [VMEM] * 10 + [ANY], [shape(12, 8, Y)] * 2, 0.5, 4
    )(mine, other, m0, m1, m2, m3, n0, n1, n2, n3, ex)
    other_edges = swap(send_edges, "gz", 1)

    def gradient(k):
        return call(
            lambda *refs: gradient_kernel(k, *refs), f"gradient_{k}", [VMEM] * 8,
            [shape(2, Y, CZ)], 1, 8,
        )(grad, psx, psy, gs, inv, own_edges, other_edges, w)[0]

    arrived = [swap(gradient(k), "src", k) for k in (2, 1, 3)]
    own = gradient(0)

    e_new, h_new = call(
        output_kernel, "outputs", [VMEM] * 8, [shape(3, X, Y, CZ)] * 2, 6, 16,
        out_specs=[HBM] * 2,
        scratch=[space(3, X, Y, CZ), space(3, X, Y, CZ), pltpu.SemaphoreType.DMA((2, X))],
    )(ex, ey, hv, ez, inv, own_edges, other_edges, w)

    total = own + arrived[0] + arrived[1] + arrived[2]
    two, one, three = (swap(total, "src", k) for k in (2, 1, 3))
    (eps_grad,) = call(
        place_kernel, "place", [ANY] * 4, [slab], 1, 4, out_specs=[HBM],
        scratch=[pltpu.SemaphoreType.DMA((4,))],
    )(two, one, three, total)
    return (e_new[None], h_new[None], eps_grad)


def solution(mesh):
    field = P("src", None, None, None, "gz")
    return jax.shard_map(
        body,
        mesh=mesh,
        in_specs=(
            field, field, field, field, P(None, None, "gz"), P(), P("src"), P(), P("gz"), P("gz"),
            P("gz", None),
        ),
        out_specs=(field, field, P(None, None, "gz")),
        check_vma=False,
    )
```

```python
import jax
import jax.numpy as jnp
from jax import lax
from jax.experimental import pallas as pl
from jax.experimental.pallas import tpu as pltpu
from jax.sharding import PartitionSpec as P

F32 = jnp.float32
BF = jnp.bfloat16
X, Y, CZ = 8, 256, 128
NN = (((1,), (0,)), ((), ()))
NT = (((1,), (1,)), ((), ()))
SLABS = 12
CORNERS = SLABS - 1
MIB = 1024 * 1024


def split(v):
    one = v.astype(BF)
    rest = v - one.astype(F32)
    two = rest.astype(BF)
    three = (rest - two.astype(F32)).astype(BF)
    return one, two, three


def in_two(v):
    one = v.astype(BF)
    return jnp.concatenate([one, (v - one.astype(F32)).astype(BF)], 1)


def mm(a, b, dims=NN):
    return lax.dot_general(a, b, dims, preferred_element_type=F32)


def iota(shape, axis):
    return lax.broadcasted_iota(jnp.int32, shape, axis)


def y_down(v):
    return v - jnp.where(iota(v.shape, 0) == 0, 0.0, pltpu.roll(v, 1, 0))


def y_up(v):
    n = v.shape[0]
    return jnp.where(iota(v.shape, 0) == n - 1, 0.0, pltpu.roll(v, n - 1, 0)) - v


def z_down(v):
    return v - jnp.where(iota(v.shape, 1) == 0, 0.0, pltpu.roll(v, 1, 1))


def z_up(v):
    n = v.shape[1]
    return jnp.where(iota(v.shape, 1) == n - 1, 0.0, pltpu.roll(v, n - 1, 1)) - v


def inverse_eps(labels, eps_ref):
    rows = [1.0 / jnp.full((1, CZ), eps_ref[r], F32) for r in range(4)]
    out = jnp.where(labels == 2, rows[2], rows[3])
    out = jnp.where(labels == 1, rows[1], out)
    return jnp.where(labels == 0, rows[0], out)


def six_rows(rows):
    one, two, three = (part.astype(F32) for part in split(rows))
    return [one, two, three, one, two, one]


def six_table(line, piece):
    one, two, three = (part.astype(F32) for part in split(line))
    return jnp.where(piece < 3, one, jnp.where(piece < 5, two, three))


def rhs_kernel(
    angle, eps, e, h, ge, gh, lab, prof_in, zs_in, lt_in, w_in,
    rx_o, ry_o, ax_o, ay_o, psx_o, psy_o, gs_o, inv_o, h_o, w, keep_o, send_o,
    e_s, ge_s, gh_s, lab_s, sems, prof_s, prof, zs, lt,
):
    core = lax.rem(lax.axis_index("gz"), 2)

    def fetch(which, x):
        at = pl.ds(x, 1)
        return (
            lambda: pltpu.make_async_copy(lab.at[at], lab_s.at[at], sems.at[0, x]),
            lambda: pltpu.make_async_copy(ge.at[:, at], ge_s.at[:, at], sems.at[1, x]),
            lambda: pltpu.make_async_copy(h.at[:, at], h_o.at[:, at], sems.at[2, x]),
            lambda: pltpu.make_async_copy(gh.at[:, at], gh_s.at[:, at], sems.at[3, x]),
            lambda: pltpu.make_async_copy(e.at[pl.ds(0, 2), at], e_s.at[:, at], sems.at[4, x]),
        )[which]()

    tables = [
        pltpu.make_async_copy(source, target, sems.at[5, n + 1])
        for n, (source, target) in enumerate(
            ((prof_in.at[angle[0]], prof), (w_in, w), (zs_in, zs), (lt_in, lt))
        )
    ]
    for copy in tables:
        copy.start()
    early, late = (0, 1), (2, 3, 4)
    for which in early:
        fetch(which, 0).start()
    for x in range(X):
        if x + 1 < X:
            for which in early:
                fetch(which, x + 1).start()
        for which in late:
            fetch(which, x).start()

    for copy in tables:
        copy.wait()
    both = jnp.concatenate([prof[0], prof[1]], 0)
    rows = jnp.concatenate(six_rows(both) + [jnp.zeros((32, Y), F32)], 0)
    prof_s[...] = rows.T.astype(BF)
    corners = [
        jnp.broadcast_to(w[p:p + 1, q:q + 1], (1, CZ))
        for p, q in ((0, 0), (0, CZ - 1), (CZ - 1, CZ - 1))
    ]
    corners = jnp.concatenate(corners + [jnp.zeros((5, CZ), F32)], 0)
    keep_o[CORNERS] = corners
    send_o[CORNERS] = corners

    row16 = iota((16, CZ), 0)
    lane16 = iota((16, CZ), 1)
    ends = jnp.where(row16 < 8, w[0:1, :], w[CZ - 1:CZ, :])
    ends_parts = [part.astype(F32) for part in split(ends)]
    slot = lax.rem(row16, 8)

    rowz = iota((CZ, CZ), 0)
    piece, within = rowz // 16, lax.rem(rowz, 16)
    z_table = jnp.where(piece < 6, six_table(zs[...], piece), 0.0)

    lane = iota((Y, CZ), 1)
    row8 = iota((8, Y), 0)
    for which in early:
        fetch(which, 0).wait()
    inv_o[0] = inverse_eps(lab_s[0], eps)

    def one_pair(i, carry):
        acc_ends = jnp.zeros((16, Y), F32)
        acc_tops = jnp.zeros((16, Y), F32)
        for j in range(2):
            x = 2 * i + j
            following = jnp.minimum(x + 1, X - 1)
            previous = jnp.maximum(x - 1, 0)
            more = (x < X - 1).astype(F32)
            less = (x > 0).astype(F32)

            @pl.when(x < X - 1)
            def _():
                for which in early:
                    fetch(which, x + 1).wait()

            for which in late:
                fetch(which, x).wait()
            inv = inv_o[x]
            inv_up = inverse_eps(lab_s[following], eps)
            inv_o[following] = inv_up
            sg = inv * ge_s[2, x]
            sg_up = inv_up * ge_s[2, following] * more
            z_pick = jnp.concatenate(
                [jnp.where(within == x, z_table, 0.0), jnp.where(within == 8 + x, z_table, 0.0)], 1
            ).astype(BF)
            cur = mm(prof_s[...], z_pick)
            h_x, h_y, h_z = h_o[0, x], h_o[1, x], h_o[2, x]
            g_hz = gh_s[2, x]
            bar_hy = gh_s[1, x] - (sg_up - sg)
            bar_hx = gh_s[0, x] + y_up(sg)
            p_x = y_down(h_z) - z_down(h_y) - cur[:, :CZ]
            p_y = z_down(h_x) - (h_z - h_o[2, previous] * less) - cur[:, CZ:]
            r_x = lt[...] * e_s[0, x] + inv * p_x
            r_y = lt[...] * e_s[1, x] + inv * p_y
            a_x = ge_s[0, x] - y_down(g_hz) - z_down(bar_hy)
            a_y = ge_s[1, x] + (g_hz - gh_s[2, previous] * less) - z_down(bar_hx)
            rx_o[x], ry_o[x], ax_o[x], ay_o[x] = r_x, r_y, a_x, a_y
            psx_o[x] = -inv * (inv * p_x)
            psy_o[x] = -inv * (inv * p_y)
            gs_o[x] = -inv * sg
            for c, field in enumerate((r_x, r_y, a_x, a_y)):
                mask = slot == 4 * j + c
                lhs = jnp.concatenate([jnp.where(mask, part, 0.0) for part in ends_parts], 0)
                lhs = jnp.concatenate([lhs, lhs], 1).astype(BF)
                out = mm(lhs, in_two(field), NT)
                acc_ends += out[0:16] + out[16:32] + out[32:48]

            packed = jnp.where(lane == CZ - 1, h_y, inv)
            packed = jnp.where(lane == CZ - 2, -pltpu.roll(h_x, CZ - 1, 1), packed)
            packed = jnp.where(lane == CZ - 3, pltpu.roll(bar_hy, CZ - 2, 1), packed)
            packed = jnp.where(lane == CZ - 4, pltpu.roll(bar_hx, CZ - 3, 1), packed)
            c16 = slot - 4 * j
            own = (c16 >= 0) & (c16 < 4)
            pick = jnp.where(
                own & (row16 < 8) & (lane16 == CZ - 1 - c16), 1.0,
                jnp.where(own & (row16 >= 8) & (c16 == i) & (lane16 == 0), 1.0, 0.0),
            )
            acc_tops += mm(jnp.concatenate([pick, pick], 1).astype(BF), in_two(packed), NT)

        tops, planes = acc_tops[0:8], acc_tops[8:16]
        outgoing = acc_ends[8:16] + jnp.where(lax.rem(row8, 4) >= 2, tops, 0.0)
        comp = lax.rem(iota((8, CZ), 0), 4)
        second = lax.rem(i, 2)
        tops = jnp.where(second == 0, tops, pltpu.roll(tops, 2, 0))
        tops_mine = comp // 2 == second
        planes_mine = comp == i

        def put(ref, low):
            def half(v):
                return jnp.where((core == 0) == low, v[:, :CZ], v[:, CZ:])

            ref[i] = half(acc_ends[0:8])
            ref[4 + i] = half(outgoing)
            slab = 8 + i // 2
            ref[slab] = jnp.where(tops_mine, half(tops), ref[slab])
            ref[10] = jnp.where(planes_mine, half(planes), ref[10])

        put(keep_o, True)
        put(send_o, False)
        return carry

    lax.fori_loop(0, X // 2, one_pair, 0)


def unpack(ref):
    m = ref[...]
    comp = lax.rem(iota((8, CZ), 0), 4)
    tops = [jnp.where(comp < 2, v, 0.0) for p in (m[8], m[9]) for v in (p, pltpu.roll(p, 6, 0))]
    planes = m[10]

    def plane(q):
        return jnp.where(
            comp == 0, pltpu.roll(planes, (8 - q) % 8, 0),
            jnp.where(comp == 1, pltpu.roll(planes, (9 - q) % 8, 0), 0.0),
        )

    return dict(
        f=m[0:4], l=m[4:8], t=jnp.stack(tops), k=jnp.stack([plane(q) for q in range(4)]),
        a=m[CORNERS, 0:1, :], c=m[CORNERS, 1:2, :], z=m[CORNERS, 2:3, :],
    )


def repack(s, ref):
    comp = lax.rem(iota((8, CZ), 0), 4)
    ref[0:4] = s["f"]
    ref[4:8] = s["l"]
    for p in range(2):
        ref[8 + p] = jnp.where(comp < 2, s["t"][2 * p], pltpu.roll(s["t"][2 * p + 1], 2, 0))
    planes = s["k"][0]
    for q in range(1, 4):
        planes = jnp.where(comp == q, pltpu.roll(s["k"][q], q, 0), planes)
    ref[10] = planes
    ref[CORNERS] = jnp.concatenate([s["a"], s["c"], s["z"], jnp.zeros((5, CZ), F32)], 0)


def order(bit, own, other):
    lower = {n: jnp.where(bit == 0, own[n], other[n]) for n in own}
    upper = {n: jnp.where(bit == 0, other[n], own[n]) for n in own}
    return lower, upper


def coupled(lower, upper):
    delta = upper["k"] * lower["t"]
    f_up = upper["f"] + upper["a"] * delta
    l_up = upper["l"] + upper["c"] * delta
    inv = 1.0 / (1.0 - upper["a"] * lower["z"])
    return f_up, l_up, inv


def combine(lower, upper):
    f_up, l_up, inv = coupled(lower, upper)
    t = (f_up + upper["a"] * lower["l"]) * inv
    u = (lower["l"] + lower["z"] * f_up) * inv
    return dict(
        f=lower["f"] + lower["c"] * t,
        l=l_up + upper["c"] * u,
        t=upper["t"],
        k=lower["k"],
        a=lower["a"] + lower["c"] * lower["c"] * upper["a"] * inv,
        c=lower["c"] * upper["c"] * inv,
        z=upper["z"] + upper["c"] * upper["c"] * lower["z"] * inv,
    )


def outside(lower, upper, below, above):
    f_up, _, inv = coupled(lower, upper)
    l_low = lower["l"] + lower["c"] * below
    f_up = f_up + upper["c"] * above
    return (f_up + upper["a"] * l_low) * inv, (l_low + lower["z"] * f_up) * inv


def pick_outside(bit, lower, upper, below, above):
    t, u = outside(lower, upper, below, above)
    return jnp.where(bit == 0, below, u), jnp.where(bit == 0, t, above)


def bits():
    gz = lax.axis_index("gz")
    core, low_z, high_z = lax.rem(gz, 2), lax.rem(gz // 2, 2), lax.rem(gz // 4, 2)
    return core, low_z, high_z, lax.rem(gz // 8, 2), gz // 16


def chip_kernel(own, other, out):
    core = bits()[0]
    repack(combine(*order(core, unpack(own), unpack(other))), out)


def four(low, high, own, m1, m2, m3):
    first = order(low, own, m1)
    pair = combine(*first)
    return first, order(high, pair, combine(*order(low, m2, m3)))


def group_kernel(m3, m2, m1, m0, after, out):
    _, low, high, _, _ = bits()
    repack(combine(*four(low, high, *(unpack(m) for m in (m0, m1, m2, m3)))[1]), out)


def back_kernel(n3, n2, n1, n0, m3, m2, m1, m0, a0, a1, after, keep_o, send_o):
    core, zl, zh, xl, xh = bits()
    chip = order(core, unpack(a0), unpack(a1))
    m0, m1, m2, m3 = (unpack(m) for m in (m0, m1, m2, m3))
    n0, n1, n2, n3 = (unpack(n) for n in (n0, n1, n2, n3))
    z_first, z_second = four(zl, zh, m0, m1, m2, m3)
    x_first, x_second = four(xl, xh, n0, n1, n2, n3)
    zero = jnp.zeros_like(m0["f"])
    edge = (zero, zero)
    edge = pick_outside(xh, *x_second, *edge)
    edge = pick_outside(xl, *x_first, *edge)
    edge = pick_outside(zh, *z_second, *edge)
    edge = pick_outside(zl, *z_first, *edge)
    lower, upper = chip
    t, u = outside(lower, upper, *edge)
    under_x = jnp.where(xl == 1, n1["t"], jnp.where(xh == 1, n3["t"], zero))
    under = jnp.where(zl == 1, m1["t"], jnp.where(zh == 1, m3["t"], under_x))
    results = []
    for block, below, above, plane in ((lower, edge[0], t, under), (upper, u, edge[1], lower["t"])):
        below = below + block["k"] * plane
        first = block["f"] + block["a"] * below + block["c"] * above
        extra = jnp.stack([first[q] * pltpu.roll(plane[q], 2, 0) for q in range(4)])
        results.append((below, above, extra))
    for part in range(3):
        low, high = results[0][part], results[1][part]
        keep_o[4 * part:4 * part + 4] = jnp.where(core == 0, low, high)
        send_o[4 * part:4 * part + 4] = jnp.where(core == 0, high, low)


def product_tables(w):
    one, two, three = split(w.T)
    full = jnp.concatenate([one, two], 1)
    return jnp.concatenate([full, full], 0), jnp.concatenate([one, three], 0)


def product(field, tables):
    one, two, three = split(field)
    wide = mm(jnp.concatenate([one, two], 1), tables[0])
    narrow = mm(jnp.concatenate([three, one], 1), tables[1])
    return wide[:, :CZ] + wide[:, CZ:] + narrow


def adjoint_kernel(ax, ay, psx, psy, w, e, after, out, ez_o, sem):
    ez_copy = pltpu.make_async_copy(e.at[2], ez_o, sem)
    ez_copy.start()
    tables = product_tables(w[...])

    def one(x, carry):
        out[x] = psx[x] * product(ax[x], tables) + psy[x] * product(ay[x], tables)
        return carry

    lax.fori_loop(0, X, one, 0, unroll=2)
    ez_copy.wait()


def primal_kernel(rx, ry, h, ez, gs, part, w, after, ex_o, ey_o, grad_o):
    tables = product_tables(w[...])

    def one(x, hy_prev):
        more = (x < X - 1).astype(F32)
        e_x, e_y = product(rx[x], tables), product(ry[x], tables)
        ex_o[x], ey_o[x] = e_x, e_y
        e_z = ez[x]
        hy = h[1, x] + z_up(e_x) - (ez[jnp.minimum(x + 1, X - 1)] * more - e_z)
        hx = h[0, x] + z_up(e_y) - y_up(e_z)
        grad_o[x] = part[x] + gs[x] * (hy - hy_prev - y_down(hx))
        return hy

    lax.fori_loop(0, X, one, jnp.zeros((Y, CZ), F32), unroll=2)


def edge_rows(keep, recv, slab):
    core = lax.rem(lax.axis_index("gz"), 2)
    a, b = keep[slab], recv[slab]
    return jnp.concatenate([jnp.where(core == 0, a, b), jnp.where(core == 0, b, a)], 1)


def columns(below, above):
    rows = six_rows(below) + six_rows(above) + [jnp.zeros((32, Y), F32)]
    return jnp.concatenate(rows, 0).T.astype(BF)


def edge_table(first, last):
    piece = iota((CZ, CZ), 0) // 8
    table = jnp.where(piece < 6, six_table(first, piece), six_table(last, piece - 6))
    return jnp.where(piece < 12, table, 0.0)


def picked(table, row):
    return jnp.where(lax.rem(iota((CZ, CZ), 0), 8) == row, table, 0.0)


def gradient_kernel(k, grad, psx, psy, gs, inv, keep, recv, w, out):
    q = lax.axis_index("src") ^ k
    below, above, extra = (edge_rows(keep, recv, 4 * part + q) for part in range(3))
    before = jnp.maximum(q - 1, 0)
    has = (q > 0).astype(F32)
    row = iota((8, Y), 0)
    lane = iota((8, Y), 1)

    def curl_rows(now, previous):
        shifted = jnp.where(row < 4, pltpu.roll(previous, 4, 0), pltpu.roll(now, 4, 0))
        along_y = now - jnp.where(lane == 0, 0.0, pltpu.roll(now, 1, 1))
        return now - shifted - pltpu.roll(along_y, 7, 0)

    curl_below = curl_rows(below, edge_rows(keep, recv, before) * has)
    curl_above = curl_rows(above, edge_rows(keep, recv, 4 + before) * has)
    kind = lax.rem(row, 4)
    plane = pltpu.roll(extra, 7, 0) + pltpu.roll(extra, 6, 0)
    below = jnp.where(kind == 0, curl_below, jnp.where(kind == 1, plane, below))
    above = jnp.where(kind == 0, curl_above, jnp.where(kind == 1, 0.0, above))
    cols = columns(below, above)
    wt = w[...].T
    first, last = wt[0:1, :], wt[CZ - 1:CZ, :]
    lane1 = iota((1, CZ), 1)
    top = jnp.where(lane1 == CZ - 1, 1.0, 0.0)
    first_up = jnp.where(lane1 == CZ - 1, 0.0, pltpu.roll(first, CZ - 1, 1)) - first
    last_up = jnp.where(lane1 == CZ - 1, 0.0, pltpu.roll(last, CZ - 1, 1)) - last + top
    lam_table = edge_table(first, last)
    curl_table = edge_table(first_up, last_up)
    plane_table = edge_table(jnp.where(lane1 == 0, 1.0, 0.0), jnp.zeros((1, CZ), F32))
    for j in range(2):
        r = 4 * j
        lam = mm(cols, jnp.concatenate([picked(lam_table, r + 2), picked(lam_table, r + 3)], 1).astype(BF))
        rest = mm(cols, jnp.concatenate([picked(curl_table, r), picked(plane_table, r + 1)], 1).astype(BF))
        x = 2 * q + j
        out[j] = (
            grad[x] + psx[x] * lam[:, :CZ] + psy[x] * lam[:, CZ:]
            + gs[x] * rest[:, :CZ] - inv[x] * inv[x] * rest[:, CZ:]
        )


def output_kernel(ex, ey, h, ez, inv, keep, recv, w, e_o, h_o, e_s, h_s, sems):
    wt = w[...].T
    table = edge_table(wt[0:1, :], wt[CZ - 1:CZ, :])
    lane = iota((CZ, CZ), 1)
    piece = iota((CZ, CZ), 0) // 8
    ones = jnp.where((piece >= 6) & (piece < 9) & (lane == CZ - 1), 1.0, 0.0)

    def edges(i):
        return columns(edge_rows(keep, recv, i), edge_rows(keep, recv, 4 + i))

    def corrected(source, table, row):
        return mm(source, picked(table, row).astype(BF))

    def copies(x):
        at = pl.ds(x, 1)
        return (
            pltpu.make_async_copy(e_s.at[:, at], e_o.at[:, at], sems.at[0, x]),
            pltpu.make_async_copy(h_s.at[:, at], h_o.at[:, at], sems.at[1, x]),
        )

    def one_pair(i, carry):
        cols, hy_prev = carry
        last = i == X // 2 - 1
        cols_next = edges(jnp.minimum(i + 1, X // 2 - 1))
        x = 2 * i
        more = jnp.where(last, 0.0, 1.0)
        following = jnp.minimum(x + 2, X - 1)
        e_x = [ex[x + j] + corrected(cols, table, 4 * j) for j in range(2)]
        e_y = [ey[x + j] + corrected(cols, table, 4 * j + 1) for j in range(2)]
        e_y.append((ey[following] + corrected(cols_next, table, 1)) * more)
        e_z = [ez[x], ez[x + 1], ez[following] * more]
        for j in range(2):
            hy = h[1, x + j] + z_up(e_x[j]) + corrected(cols, ones, 4 * j) - (e_z[j + 1] - e_z[j])
            hx = h[0, x + j] + z_up(e_y[j]) + corrected(cols, ones, 4 * j + 1) - y_up(e_z[j])
            curl = hy - hy_prev - y_down(hx)
            hy_prev = hy
            e_s[0, x + j] = e_x[j]
            e_s[1, x + j] = e_y[j]
            e_s[2, x + j] = e_z[j] + inv[x + j] * curl
            h_s[0, x + j] = hx
            h_s[1, x + j] = hy
            h_s[2, x + j] = h[2, x + j] - (e_y[j + 1] - e_y[j]) + y_up(e_x[j])
            for copy in copies(x + j):
                copy.start()
        return cols_next, hy_prev

    lax.fori_loop(0, X // 2, one_pair, (edges(0), jnp.zeros((Y, CZ), F32)))
    for x in range(X):
        for copy in copies(x):
            copy.wait()


def place_kernel(g2, g1, g3, g0, out, sems):
    src = lax.axis_index("src")
    copies = []
    for k, g in zip((2, 1, 3, 0), (g2, g1, g3, g0)):
        copies.append(pltpu.make_async_copy(g, out.at[pl.ds(2 * (src ^ k), 2)], sems.at[k]))
    for copy in copies:
        copy.start()
    for copy in copies:
        copy.wait()


def swap(block, axis, mask):
    return lax.ppermute(block, axis, [(i, i ^ mask) for i in range(lax.axis_size(axis))])


SMEM = pl.BlockSpec(memory_space=pltpu.SMEM)
VMEM = pl.BlockSpec(memory_space=pltpu.VMEM)
HBM = pl.BlockSpec(memory_space=pltpu.HBM)
ANY = pl.BlockSpec(memory_space=pl.ANY)


def shape(*dims):
    return jax.ShapeDtypeStruct(dims, F32)


def call(kernel, name, in_specs, outs, us, mib, out_specs=None, scratch=()):
    return pl.pallas_call(
        kernel,
        in_specs=in_specs,
        out_specs=out_specs or [VMEM] * len(outs),
        out_shape=outs,
        scratch_shapes=scratch,
        compiler_params=pltpu.CompilerParams(vmem_limit_bytes=mib * MIB),
        cost_estimate=pl.CostEstimate(flops=1000, bytes_accessed=int(us * 3.0e6), transcendentals=0),
        name=name,
    )


def in_hbm(array):
    return pltpu.with_memory_space_constraint(array, pltpu.HBM)


def body(
    fields_e, fields_h, cot_e, cot_h, labels, region_eps, angle_index, profiles, zsheet,
    layer_term, block_inverse,
):
    e, h, ge, gh = fields_e[0], fields_h[0], cot_e[0], cot_h[0]
    zs, lt = zsheet.reshape(1, CZ), layer_term.reshape(1, CZ)
    slab = shape(X, Y, CZ)
    message = shape(SLABS, 8, CZ)

    def space(*dims, dtype=F32):
        return pltpu.VMEM(dims, dtype)

    rx, ry, ax, ay, psx, psy, gs, inv, hv, w, keep, send = call(
        rhs_kernel, "right_hand_sides",
        [SMEM, SMEM] + [HBM] * 9,
        [slab] * 8 + [shape(3, X, Y, CZ), shape(CZ, CZ)] + [message] * 2,
        6, 24,
        scratch=[
            space(2, X, Y, CZ), space(3, X, Y, CZ), space(3, X, Y, CZ),
            space(X, Y, CZ, dtype=jnp.int32), pltpu.SemaphoreType.DMA((6, X)),
            space(Y, CZ, dtype=BF), space(2, X, Y), space(1, CZ), space(1, CZ),
        ],
    )(angle_index, *map(in_hbm, (region_eps, e, h, ge, gh, labels, profiles, zs, lt, block_inverse)))

    other = swap(send, "gz", 1)
    (m0,) = call(chip_kernel, "chip", [VMEM] * 2, [message], 0.5, 4)(keep, other)
    m3, m2, m1 = (swap(m0, "gz", 2 * k) for k in (3, 2, 1))

    adjoint, ez = call(
        adjoint_kernel, "adjoint_products", [VMEM] * 5 + [HBM, ANY], [slab] * 2, 3, 8,
        scratch=[pltpu.SemaphoreType.DMA],
    )(ax, ay, psx, psy, w, in_hbm(e), m0)
    (n0,) = call(group_kernel, "group", [VMEM] * 4 + [ANY], [message], 0.5, 4)(m3, m2, m1, m0, adjoint)
    n3, n2, n1 = (swap(n0, "gz", 8 * k) for k in (3, 2, 1))

    ex, ey, grad = call(primal_kernel, "primal_products", [VMEM] * 7 + [ANY], [slab] * 3, 4, 8)(
        rx, ry, hv, ez, gs, adjoint, w, n0
    )
    own_edges, send_edges = call(
        back_kernel, "back", [VMEM] * 10 + [ANY], [shape(12, 8, CZ)] * 2, 0.5, 4
    )(n3, n2, n1, n0, m3, m2, m1, m0, keep, other, ex)
    other_edges = swap(send_edges, "gz", 1)

    def gradient(k):
        return call(
            lambda *refs: gradient_kernel(k, *refs), f"gradient_{k}", [VMEM] * 8,
            [shape(2, Y, CZ)], 1, 8,
        )(grad, psx, psy, gs, inv, own_edges, other_edges, w)[0]

    arrived = [swap(gradient(k), "src", k) for k in (2, 1, 3)]
    own = gradient(0)

    e_new, h_new = call(
        output_kernel, "outputs", [VMEM] * 8, [shape(3, X, Y, CZ)] * 2, 6, 16,
        out_specs=[HBM] * 2,
        scratch=[space(3, X, Y, CZ), space(3, X, Y, CZ), pltpu.SemaphoreType.DMA((2, X))],
    )(ex, ey, hv, ez, inv, own_edges, other_edges, w)

    total = own + arrived[0] + arrived[1] + arrived[2]
    two, one, three = (swap(total, "src", k) for k in (2, 1, 3))
    (eps_grad,) = call(
        place_kernel, "place", [ANY] * 4, [slab], 1, 4, out_specs=[HBM],
        scratch=[pltpu.SemaphoreType.DMA((4,))],
    )(two, one, three, total)
    return (e_new[None], h_new[None], eps_grad)


def solution(mesh):
    field = P("src", None, None, None, "gz")
    return jax.shard_map(
        body,
        mesh=mesh,
        in_specs=(
            field, field, field, field, P(None, None, "gz"), P(), P("src"), P(), P("gz"), P("gz"),
            P("gz", None),
        ),
        out_specs=(field, field, P(None, None, "gz")),
        check_vma=False,
    )
```

```python
import jax
import jax.numpy as jnp
from jax import lax
from jax.experimental import pallas as pl
from jax.experimental.pallas import tpu as pltpu
from jax.sharding import PartitionSpec as P

F32 = jnp.float32
BF = jnp.bfloat16
X, Y, CZ = 8, 256, 128
NN = (((1,), (0,)), ((), ()))
NT = (((1,), (1,)), ((), ()))
SLABS = 12
CORNERS = SLABS - 1
MIB = 1024 * 1024


def split(v):
    one = v.astype(BF)
    rest = v - one.astype(F32)
    two = rest.astype(BF)
    three = (rest - two.astype(F32)).astype(BF)
    return one, two, three


def in_two(v):
    one = v.astype(BF)
    return jnp.concatenate([one, (v - one.astype(F32)).astype(BF)], 1)


def mm(a, b, dims=NN):
    return lax.dot_general(a, b, dims, preferred_element_type=F32)


def iota(shape, axis):
    return lax.broadcasted_iota(jnp.int32, shape, axis)


def y_down(v):
    return v - jnp.where(iota(v.shape, 0) == 0, 0.0, pltpu.roll(v, 1, 0))


def y_up(v):
    n = v.shape[0]
    return jnp.where(iota(v.shape, 0) == n - 1, 0.0, pltpu.roll(v, n - 1, 0)) - v


def z_down(v):
    return v - jnp.where(iota(v.shape, 1) == 0, 0.0, pltpu.roll(v, 1, 1))


def z_up(v):
    n = v.shape[1]
    return jnp.where(iota(v.shape, 1) == n - 1, 0.0, pltpu.roll(v, n - 1, 1)) - v


def inverse_eps(labels, eps_ref):
    rows = [1.0 / jnp.full((1, CZ), eps_ref[r], F32) for r in range(4)]
    out = jnp.where(labels == 2, rows[2], rows[3])
    out = jnp.where(labels == 1, rows[1], out)
    return jnp.where(labels == 0, rows[0], out)


def six_rows(rows):
    one, two, three = (part.astype(F32) for part in split(rows))
    return [one, two, three, one, two, one]


def six_table(line, piece):
    one, two, three = (part.astype(F32) for part in split(line))
    return jnp.where(piece < 3, one, jnp.where(piece < 5, two, three))


def rhs_kernel(
    angle, eps, e, h, ge, gh, lab, prof_in, zs_in, lt_in, w_in,
    rx_o, ry_o, ax_o, ay_o, psx_o, psy_o, gs_o, inv_o, h_o, w, keep_o, send_o,
    e_s, ge_s, gh_s, lab_s, sems, prof_s, prof, zs, lt,
):
    core = lax.rem(lax.axis_index("gz"), 2)

    def fetch(which, x):
        at = pl.ds(x, 1)
        return (
            lambda: pltpu.make_async_copy(lab.at[at], lab_s.at[at], sems.at[0, x]),
            lambda: pltpu.make_async_copy(ge.at[:, at], ge_s.at[:, at], sems.at[1, x]),
            lambda: pltpu.make_async_copy(h.at[:, at], h_o.at[:, at], sems.at[2, x]),
            lambda: pltpu.make_async_copy(gh.at[:, at], gh_s.at[:, at], sems.at[3, x]),
            lambda: pltpu.make_async_copy(e.at[pl.ds(0, 2), at], e_s.at[:, at], sems.at[4, x]),
        )[which]()

    tables = [
        pltpu.make_async_copy(source, target, sems.at[5, n + 1])
        for n, (source, target) in enumerate(
            ((prof_in.at[angle[0]], prof), (w_in, w), (zs_in, zs), (lt_in, lt))
        )
    ]
    for copy in tables:
        copy.start()
    early, late = (0, 1), (2, 3, 4)
    for which in early:
        fetch(which, 0).start()
    for x in range(X):
        if x + 1 < X:
            for which in early:
                fetch(which, x + 1).start()
        for which in late:
            fetch(which, x).start()

    for copy in tables:
        copy.wait()
    both = jnp.concatenate([prof[0], prof[1]], 0)
    rows = jnp.concatenate(six_rows(both) + [jnp.zeros((32, Y), F32)], 0)
    prof_s[...] = rows.T.astype(BF)
    corners = [
        jnp.broadcast_to(w[p:p + 1, q:q + 1], (1, CZ))
        for p, q in ((0, 0), (0, CZ - 1), (CZ - 1, CZ - 1))
    ]
    corners = jnp.concatenate(corners + [jnp.zeros((5, CZ), F32)], 0)
    keep_o[CORNERS] = corners
    send_o[CORNERS] = corners

    row16 = iota((16, CZ), 0)
    lane16 = iota((16, CZ), 1)
    ends = jnp.where(row16 < 8, w[0:1, :], w[CZ - 1:CZ, :])
    ends_parts = [part.astype(F32) for part in split(ends)]
    slot = lax.rem(row16, 8)

    rowz = iota((CZ, CZ), 0)
    piece, within = rowz // 16, lax.rem(rowz, 16)
    z_table = jnp.where(piece < 6, six_table(zs[...], piece), 0.0)

    lane = iota((Y, CZ), 1)
    row8 = iota((8, Y), 0)
    for which in early:
        fetch(which, 0).wait()
    inv_o[0] = inverse_eps(lab_s[0], eps)

    def one_pair(i, carry):
        acc_ends = jnp.zeros((16, Y), F32)
        acc_tops = jnp.zeros((16, Y), F32)
        for j in range(2):
            x = 2 * i + j
            following = jnp.minimum(x + 1, X - 1)
            previous = jnp.maximum(x - 1, 0)
            more = (x < X - 1).astype(F32)
            less = (x > 0).astype(F32)

            @pl.when(x < X - 1)
            def _():
                for which in early:
                    fetch(which, x + 1).wait()

            for which in late:
                fetch(which, x).wait()
            inv = inv_o[x]
            inv_up = inverse_eps(lab_s[following], eps)
            inv_o[following] = inv_up
            sg = inv * ge_s[2, x]
            sg_up = inv_up * ge_s[2, following] * more
            z_pick = jnp.concatenate(
                [jnp.where(within == x, z_table, 0.0), jnp.where(within == 8 + x, z_table, 0.0)], 1
            ).astype(BF)
            cur = mm(prof_s[...], z_pick)
            h_x, h_y, h_z = h_o[0, x], h_o[1, x], h_o[2, x]
            g_hz = gh_s[2, x]
            bar_hy = gh_s[1, x] - (sg_up - sg)
            bar_hx = gh_s[0, x] + y_up(sg)
            p_x = y_down(h_z) - z_down(h_y) - cur[:, :CZ]
            p_y = z_down(h_x) - (h_z - h_o[2, previous] * less) - cur[:, CZ:]
            r_x = lt[...] * e_s[0, x] + inv * p_x
            r_y = lt[...] * e_s[1, x] + inv * p_y
            a_x = ge_s[0, x] - y_down(g_hz) - z_down(bar_hy)
            a_y = ge_s[1, x] + (g_hz - gh_s[2, previous] * less) - z_down(bar_hx)
            rx_o[x], ry_o[x], ax_o[x], ay_o[x] = r_x, r_y, a_x, a_y
            psx_o[x] = -inv * (inv * p_x)
            psy_o[x] = -inv * (inv * p_y)
            gs_o[x] = -inv * sg
            for c, field in enumerate((r_x, r_y, a_x, a_y)):
                mask = slot == 4 * j + c
                lhs = jnp.concatenate([jnp.where(mask, part, 0.0) for part in ends_parts], 0)
                lhs = jnp.concatenate([lhs, lhs], 1).astype(BF)
                out = mm(lhs, in_two(field), NT)
                acc_ends += out[0:16] + out[16:32] + out[32:48]

            packed = jnp.where(lane == CZ - 1, h_y, inv)
            packed = jnp.where(lane == CZ - 2, -pltpu.roll(h_x, CZ - 1, 1), packed)
            packed = jnp.where(lane == CZ - 3, pltpu.roll(bar_hy, CZ - 2, 1), packed)
            packed = jnp.where(lane == CZ - 4, pltpu.roll(bar_hx, CZ - 3, 1), packed)
            c16 = slot - 4 * j
            own = (c16 >= 0) & (c16 < 4)
            pick = jnp.where(
                own & (row16 < 8) & (lane16 == CZ - 1 - c16), 1.0,
                jnp.where(own & (row16 >= 8) & (c16 == i) & (lane16 == 0), 1.0, 0.0),
            )
            acc_tops += mm(jnp.concatenate([pick, pick], 1).astype(BF), in_two(packed), NT)

        tops, planes = acc_tops[0:8], acc_tops[8:16]
        outgoing = acc_ends[8:16] + jnp.where(lax.rem(row8, 4) >= 2, tops, 0.0)
        comp = lax.rem(iota((8, CZ), 0), 4)
        second = lax.rem(i, 2)
        tops = jnp.where(second == 0, tops, pltpu.roll(tops, 2, 0))
        tops_mine = comp // 2 == second
        planes_mine = comp == i

        def put(ref, low):
            def half(v):
                return jnp.where((core == 0) == low, v[:, :CZ], v[:, CZ:])

            ref[i] = half(acc_ends[0:8])
            ref[4 + i] = half(outgoing)
            slab = 8 + i // 2
            ref[slab] = jnp.where(tops_mine, half(tops), ref[slab])
            ref[10] = jnp.where(planes_mine, half(planes), ref[10])

        put(keep_o, True)
        put(send_o, False)
        return carry

    lax.fori_loop(0, X // 2, one_pair, 0)


def unpack(ref):
    m = ref[...]
    comp = lax.rem(iota((8, CZ), 0), 4)
    tops = [jnp.where(comp < 2, v, 0.0) for p in (m[8], m[9]) for v in (p, pltpu.roll(p, 6, 0))]
    planes = m[10]

    def plane(q):
        return jnp.where(
            comp == 0, pltpu.roll(planes, (8 - q) % 8, 0),
            jnp.where(comp == 1, pltpu.roll(planes, (9 - q) % 8, 0), 0.0),
        )

    return dict(
        f=m[0:4], l=m[4:8], t=jnp.stack(tops), k=jnp.stack([plane(q) for q in range(4)]),
        a=m[CORNERS, 0:1, :], c=m[CORNERS, 1:2, :], z=m[CORNERS, 2:3, :],
    )


def repack(s, ref):
    comp = lax.rem(iota((8, CZ), 0), 4)
    ref[0:4] = s["f"]
    ref[4:8] = s["l"]
    for p in range(2):
        ref[8 + p] = jnp.where(comp < 2, s["t"][2 * p], pltpu.roll(s["t"][2 * p + 1], 2, 0))
    planes = s["k"][0]
    for q in range(1, 4):
        planes = jnp.where(comp == q, pltpu.roll(s["k"][q], q, 0), planes)
    ref[10] = planes
    ref[CORNERS] = jnp.concatenate([s["a"], s["c"], s["z"], jnp.zeros((5, CZ), F32)], 0)


def order(bit, own, other):
    lower = {n: jnp.where(bit == 0, own[n], other[n]) for n in own}
    upper = {n: jnp.where(bit == 0, other[n], own[n]) for n in own}
    return lower, upper


def coupled(lower, upper):
    delta = upper["k"] * lower["t"]
    f_up = upper["f"] + upper["a"] * delta
    l_up = upper["l"] + upper["c"] * delta
    inv = 1.0 / (1.0 - upper["a"] * lower["z"])
    return f_up, l_up, inv


def combine(lower, upper):
    f_up, l_up, inv = coupled(lower, upper)
    t = (f_up + upper["a"] * lower["l"]) * inv
    u = (lower["l"] + lower["z"] * f_up) * inv
    return dict(
        f=lower["f"] + lower["c"] * t,
        l=l_up + upper["c"] * u,
        t=upper["t"],
        k=lower["k"],
        a=lower["a"] + lower["c"] * lower["c"] * upper["a"] * inv,
        c=lower["c"] * upper["c"] * inv,
        z=upper["z"] + upper["c"] * upper["c"] * lower["z"] * inv,
    )


def outside(lower, upper, below, above):
    f_up, _, inv = coupled(lower, upper)
    l_low = lower["l"] + lower["c"] * below
    f_up = f_up + upper["c"] * above
    return (f_up + upper["a"] * l_low) * inv, (l_low + lower["z"] * f_up) * inv


def pick_outside(bit, lower, upper, below, above):
    t, u = outside(lower, upper, below, above)
    return jnp.where(bit == 0, below, u), jnp.where(bit == 0, t, above)


def bits():
    gz = lax.axis_index("gz")
    core, low_z, high_z = lax.rem(gz, 2), lax.rem(gz // 2, 2), lax.rem(gz // 4, 2)
    return core, low_z, high_z, lax.rem(gz // 8, 2), gz // 16


def chip_kernel(own, other, out):
    core = bits()[0]
    repack(combine(*order(core, unpack(own), unpack(other))), out)


def four(low, high, own, m1, m2, m3):
    first = order(low, own, m1)
    pair = combine(*first)
    return first, order(high, pair, combine(*order(low, m2, m3)))


def group_kernel(m3, m2, m1, m0, after, out):
    _, low, high, _, _ = bits()
    repack(combine(*four(low, high, *(unpack(m) for m in (m0, m1, m2, m3)))[1]), out)


def back_kernel(n2, n3, n1, n0, m3, m2, m1, m0, a0, a1, after, keep_o, send_o):
    core, zl, zh, xl, xh = bits()
    chip = order(core, unpack(a0), unpack(a1))
    m0, m1, m2, m3 = (unpack(m) for m in (m0, m1, m2, m3))
    n0, n1, n2, n3 = (unpack(n) for n in (n0, n1, n2, n3))
    z_first, z_second = four(zl, zh, m0, m1, m2, m3)
    x_first, x_second = four(xl, xh, n0, n1, n2, n3)
    zero = jnp.zeros_like(m0["f"])
    edge = (zero, zero)
    edge = pick_outside(xh, *x_second, *edge)
    edge = pick_outside(xl, *x_first, *edge)
    edge = pick_outside(zh, *z_second, *edge)
    edge = pick_outside(zl, *z_first, *edge)
    lower, upper = chip
    t, u = outside(lower, upper, *edge)
    under_x = jnp.where(xl == 1, n1["t"], jnp.where(xh == 1, n3["t"], zero))
    under = jnp.where(zl == 1, m1["t"], jnp.where(zh == 1, m3["t"], under_x))
    results = []
    for block, below, above, plane in ((lower, edge[0], t, under), (upper, u, edge[1], lower["t"])):
        below = below + block["k"] * plane
        first = block["f"] + block["a"] * below + block["c"] * above
        extra = jnp.stack([first[q] * pltpu.roll(plane[q], 2, 0) for q in range(4)])
        results.append((below, above, extra))
    for part in range(3):
        low, high = results[0][part], results[1][part]
        keep_o[4 * part:4 * part + 4] = jnp.where(core == 0, low, high)
        send_o[4 * part:4 * part + 4] = jnp.where(core == 0, high, low)


def product_tables(w):
    one, two, three = split(w.T)
    full = jnp.concatenate([one, two], 1)
    return jnp.concatenate([full, full], 0), jnp.concatenate([one, three], 0)


def product(field, tables):
    one, two, three = split(field)
    wide = mm(jnp.concatenate([one, two], 1), tables[0])
    narrow = mm(jnp.concatenate([three, one], 1), tables[1])
    return wide[:, :CZ] + wide[:, CZ:] + narrow


def adjoint_kernel(ax, ay, psx, psy, w, e, after, out, ez_o, sem):
    ez_copy = pltpu.make_async_copy(e.at[2], ez_o, sem)
    ez_copy.start()
    tables = product_tables(w[...])

    def one(x, carry):
        out[x] = psx[x] * product(ax[x], tables) + psy[x] * product(ay[x], tables)
        return carry

    lax.fori_loop(0, X, one, 0, unroll=2)
    ez_copy.wait()


def primal_kernel(rx, ry, h, ez, gs, part, w, after, ex_o, ey_o, grad_o):
    tables = product_tables(w[...])

    def one(x, hy_prev):
        more = (x < X - 1).astype(F32)
        e_x, e_y = product(rx[x], tables), product(ry[x], tables)
        ex_o[x], ey_o[x] = e_x, e_y
        e_z = ez[x]
        hy = h[1, x] + z_up(e_x) - (ez[jnp.minimum(x + 1, X - 1)] * more - e_z)
        hx = h[0, x] + z_up(e_y) - y_up(e_z)
        grad_o[x] = part[x] + gs[x] * (hy - hy_prev - y_down(hx))
        return hy

    lax.fori_loop(0, X, one, jnp.zeros((Y, CZ), F32), unroll=2)


def edge_rows(keep, recv, slab):
    core = lax.rem(lax.axis_index("gz"), 2)
    a, b = keep[slab], recv[slab]
    return jnp.concatenate([jnp.where(core == 0, a, b), jnp.where(core == 0, b, a)], 1)


def columns(below, above):
    rows = six_rows(below) + six_rows(above) + [jnp.zeros((32, Y), F32)]
    return jnp.concatenate(rows, 0).T.astype(BF)


def edge_table(first, last):
    piece = iota((CZ, CZ), 0) // 8
    table = jnp.where(piece < 6, six_table(first, piece), six_table(last, piece - 6))
    return jnp.where(piece < 12, table, 0.0)


def picked(table, row):
    return jnp.where(lax.rem(iota((CZ, CZ), 0), 8) == row, table, 0.0)


def gradient_kernel(k, grad, psx, psy, gs, inv, keep, recv, w, out):
    q = lax.axis_index("src") ^ k
    below, above, extra = (edge_rows(keep, recv, 4 * part + q) for part in range(3))
    before = jnp.maximum(q - 1, 0)
    has = (q > 0).astype(F32)
    row = iota((8, Y), 0)
    lane = iota((8, Y), 1)

    def curl_rows(now, previous):
        shifted = jnp.where(row < 4, pltpu.roll(previous, 4, 0), pltpu.roll(now, 4, 0))
        along_y = now - jnp.where(lane == 0, 0.0, pltpu.roll(now, 1, 1))
        return now - shifted - pltpu.roll(along_y, 7, 0)

    curl_below = curl_rows(below, edge_rows(keep, recv, before) * has)
    curl_above = curl_rows(above, edge_rows(keep, recv, 4 + before) * has)
    kind = lax.rem(row, 4)
    plane = pltpu.roll(extra, 7, 0) + pltpu.roll(extra, 6, 0)
    below = jnp.where(kind == 0, curl_below, jnp.where(kind == 1, plane, below))
    above = jnp.where(kind == 0, curl_above, jnp.where(kind == 1, 0.0, above))
    cols = columns(below, above)
    wt = w[...].T
    first, last = wt[0:1, :], wt[CZ - 1:CZ, :]
    lane1 = iota((1, CZ), 1)
    top = jnp.where(lane1 == CZ - 1, 1.0, 0.0)
    first_up = jnp.where(lane1 == CZ - 1, 0.0, pltpu.roll(first, CZ - 1, 1)) - first
    last_up = jnp.where(lane1 == CZ - 1, 0.0, pltpu.roll(last, CZ - 1, 1)) - last + top
    lam_table = edge_table(first, last)
    curl_table = edge_table(first_up, last_up)
    plane_table = edge_table(jnp.where(lane1 == 0, 1.0, 0.0), jnp.zeros((1, CZ), F32))
    for j in range(2):
        r = 4 * j
        lam = mm(cols, jnp.concatenate([picked(lam_table, r + 2), picked(lam_table, r + 3)], 1).astype(BF))
        rest = mm(cols, jnp.concatenate([picked(curl_table, r), picked(plane_table, r + 1)], 1).astype(BF))
        x = 2 * q + j
        out[j] = (
            grad[x] + psx[x] * lam[:, :CZ] + psy[x] * lam[:, CZ:]
            + gs[x] * rest[:, :CZ] - inv[x] * inv[x] * rest[:, CZ:]
        )


def output_kernel(ex, ey, h, ez, inv, keep, recv, w, e_o, h_o, e_s, h_s, sems):
    wt = w[...].T
    table = edge_table(wt[0:1, :], wt[CZ - 1:CZ, :])
    lane = iota((CZ, CZ), 1)
    piece = iota((CZ, CZ), 0) // 8
    ones = jnp.where((piece >= 6) & (piece < 9) & (lane == CZ - 1), 1.0, 0.0)

    def edges(i):
        return columns(edge_rows(keep, recv, i), edge_rows(keep, recv, 4 + i))

    def corrected(source, table, row):
        return mm(source, picked(table, row).astype(BF))

    def copies(x):
        at = pl.ds(x, 1)
        return (
            pltpu.make_async_copy(e_s.at[:, at], e_o.at[:, at], sems.at[0, x]),
            pltpu.make_async_copy(h_s.at[:, at], h_o.at[:, at], sems.at[1, x]),
        )

    def one_pair(i, carry):
        cols, hy_prev = carry
        last = i == X // 2 - 1
        cols_next = edges(jnp.minimum(i + 1, X // 2 - 1))
        x = 2 * i
        more = jnp.where(last, 0.0, 1.0)
        following = jnp.minimum(x + 2, X - 1)
        e_x = [ex[x + j] + corrected(cols, table, 4 * j) for j in range(2)]
        e_y = [ey[x + j] + corrected(cols, table, 4 * j + 1) for j in range(2)]
        e_y.append((ey[following] + corrected(cols_next, table, 1)) * more)
        e_z = [ez[x], ez[x + 1], ez[following] * more]
        for j in range(2):
            hy = h[1, x + j] + z_up(e_x[j]) + corrected(cols, ones, 4 * j) - (e_z[j + 1] - e_z[j])
            hx = h[0, x + j] + z_up(e_y[j]) + corrected(cols, ones, 4 * j + 1) - y_up(e_z[j])
            curl = hy - hy_prev - y_down(hx)
            hy_prev = hy
            e_s[0, x + j] = e_x[j]
            e_s[1, x + j] = e_y[j]
            e_s[2, x + j] = e_z[j] + inv[x + j] * curl
            h_s[0, x + j] = hx
            h_s[1, x + j] = hy
            h_s[2, x + j] = h[2, x + j] - (e_y[j + 1] - e_y[j]) + y_up(e_x[j])
            for copy in copies(x + j):
                copy.start()
        return cols_next, hy_prev

    lax.fori_loop(0, X // 2, one_pair, (edges(0), jnp.zeros((Y, CZ), F32)))
    for x in range(X):
        for copy in copies(x):
            copy.wait()


def place_kernel(g2, g3, g1, g0, out, sems):
    src = lax.axis_index("src")
    copies = []
    for k, g in zip((2, 1, 3, 0), (g2, g1, g3, g0)):
        copies.append(pltpu.make_async_copy(g, out.at[pl.ds(2 * (src ^ k), 2)], sems.at[k]))
    for copy in copies:
        copy.start()
    for copy in copies:
        copy.wait()


def swap(block, axis, mask):
    return lax.ppermute(block, axis, [(i, i ^ mask) for i in range(lax.axis_size(axis))])


SMEM = pl.BlockSpec(memory_space=pltpu.SMEM)
VMEM = pl.BlockSpec(memory_space=pltpu.VMEM)
HBM = pl.BlockSpec(memory_space=pltpu.HBM)
ANY = pl.BlockSpec(memory_space=pl.ANY)


def shape(*dims):
    return jax.ShapeDtypeStruct(dims, F32)


def call(kernel, name, in_specs, outs, us, mib, out_specs=None, scratch=()):
    return pl.pallas_call(
        kernel,
        in_specs=in_specs,
        out_specs=out_specs or [VMEM] * len(outs),
        out_shape=outs,
        scratch_shapes=scratch,
        compiler_params=pltpu.CompilerParams(vmem_limit_bytes=mib * MIB),
        cost_estimate=pl.CostEstimate(flops=1000, bytes_accessed=int(us * 3.0e6), transcendentals=0),
        name=name,
    )


def in_hbm(array):
    return pltpu.with_memory_space_constraint(array, pltpu.HBM)


def body(
    fields_e, fields_h, cot_e, cot_h, labels, region_eps, angle_index, profiles, zsheet,
    layer_term, block_inverse,
):
    e, h, ge, gh = fields_e[0], fields_h[0], cot_e[0], cot_h[0]
    zs, lt = zsheet.reshape(1, CZ), layer_term.reshape(1, CZ)
    slab = shape(X, Y, CZ)
    message = shape(SLABS, 8, CZ)

    def space(*dims, dtype=F32):
        return pltpu.VMEM(dims, dtype)

    rx, ry, ax, ay, psx, psy, gs, inv, hv, w, keep, send = call(
        rhs_kernel, "right_hand_sides",
        [SMEM, SMEM] + [HBM] * 9,
        [slab] * 8 + [shape(3, X, Y, CZ), shape(CZ, CZ)] + [message] * 2,
        6, 24,
        scratch=[
            space(2, X, Y, CZ), space(3, X, Y, CZ), space(3, X, Y, CZ),
            space(X, Y, CZ, dtype=jnp.int32), pltpu.SemaphoreType.DMA((6, X)),
            space(Y, CZ, dtype=BF), space(2, X, Y), space(1, CZ), space(1, CZ),
        ],
    )(angle_index, *map(in_hbm, (region_eps, e, h, ge, gh, labels, profiles, zs, lt, block_inverse)))

    other = swap(send, "gz", 1)
    (m0,) = call(chip_kernel, "chip", [VMEM] * 2, [message], 0.5, 4)(keep, other)
    m3, m2, m1 = (swap(m0, "gz", 2 * k) for k in (3, 2, 1))

    adjoint, ez = call(
        adjoint_kernel, "adjoint_products", [VMEM] * 5 + [HBM, ANY], [slab] * 2, 3, 8,
        scratch=[pltpu.SemaphoreType.DMA],
    )(ax, ay, psx, psy, w, in_hbm(e), m0)
    (n0,) = call(group_kernel, "group", [VMEM] * 4 + [ANY], [message], 0.5, 4)(m3, m2, m1, m0, adjoint)
    n2, n3, n1 = (swap(n0, "gz", 8 * k) for k in (2, 3, 1))

    ex, ey, grad = call(primal_kernel, "primal_products", [VMEM] * 7 + [ANY], [slab] * 3, 4, 8)(
        rx, ry, hv, ez, gs, adjoint, w, n0
    )
    own_edges, send_edges = call(
        back_kernel, "back", [VMEM] * 10 + [ANY], [shape(12, 8, CZ)] * 2, 0.5, 4
    )(n2, n3, n1, n0, m3, m2, m1, m0, keep, other, ex)
    other_edges = swap(send_edges, "gz", 1)

    def gradient(k):
        return call(
            lambda *refs: gradient_kernel(k, *refs), f"gradient_{k}", [VMEM] * 8,
            [shape(2, Y, CZ)], 1, 8,
        )(grad, psx, psy, gs, inv, own_edges, other_edges, w)[0]

    arrived = [swap(gradient(k), "src", k) for k in (2, 3, 1)]
    own = gradient(0)

    e_new, h_new = call(
        output_kernel, "outputs", [VMEM] * 8, [shape(3, X, Y, CZ)] * 2, 6, 16,
        out_specs=[HBM] * 2,
        scratch=[space(3, X, Y, CZ), space(3, X, Y, CZ), pltpu.SemaphoreType.DMA((2, X))],
    )(ex, ey, hv, ez, inv, own_edges, other_edges, w)

    total = own + arrived[0] + arrived[1] + arrived[2]
    two, three, one = (swap(total, "src", k) for k in (2, 3, 1))
    (eps_grad,) = call(
        place_kernel, "place", [ANY] * 4, [slab], 1, 4, out_specs=[HBM],
        scratch=[pltpu.SemaphoreType.DMA((4,))],
    )(two, three, one, total)
    return (e_new[None], h_new[None], eps_grad)


def solution(mesh):
    field = P("src", None, None, None, "gz")
    return jax.shard_map(
        body,
        mesh=mesh,
        in_specs=(
            field, field, field, field, P(None, None, "gz"), P(), P("src"), P(), P("gz"), P("gz"),
            P("gz", None),
        ),
        out_specs=(field, field, P(None, None, "gz")),
        check_vma=False,
    )
```

```python
import jax
import jax.numpy as jnp
from jax import lax
from jax.experimental import pallas as pl
from jax.experimental.pallas import tpu as pltpu
from jax.sharding import PartitionSpec as P

F32 = jnp.float32
BF = jnp.bfloat16
X, Y, CZ = 8, 256, 128
NN = (((1,), (0,)), ((), ()))
NT = (((1,), (1,)), ((), ()))
SLABS = 12
CORNERS = SLABS - 1
MIB = 1024 * 1024


def split(v):
    one = v.astype(BF)
    rest = v - one.astype(F32)
    two = rest.astype(BF)
    three = (rest - two.astype(F32)).astype(BF)
    return one, two, three


def in_two(v):
    one = v.astype(BF)
    return jnp.concatenate([one, (v - one.astype(F32)).astype(BF)], 1)


def mm(a, b, dims=NN):
    return lax.dot_general(a, b, dims, preferred_element_type=F32)


def iota(shape, axis):
    return lax.broadcasted_iota(jnp.int32, shape, axis)


def y_down(v):
    return v - jnp.where(iota(v.shape, 0) == 0, 0.0, pltpu.roll(v, 1, 0))


def y_up(v):
    n = v.shape[0]
    return jnp.where(iota(v.shape, 0) == n - 1, 0.0, pltpu.roll(v, n - 1, 0)) - v


def z_down(v):
    return v - jnp.where(iota(v.shape, 1) == 0, 0.0, pltpu.roll(v, 1, 1))


def z_up(v):
    n = v.shape[1]
    return jnp.where(iota(v.shape, 1) == n - 1, 0.0, pltpu.roll(v, n - 1, 1)) - v


def inverse_eps(labels, eps_ref):
    rows = [1.0 / jnp.full((1, CZ), eps_ref[r], F32) for r in range(4)]
    out = jnp.where(labels == 2, rows[2], rows[3])
    out = jnp.where(labels == 1, rows[1], out)
    return jnp.where(labels == 0, rows[0], out)


def six_rows(rows):
    one, two, three = (part.astype(F32) for part in split(rows))
    return [one, two, three, one, two, one]


def six_table(line, piece):
    one, two, three = (part.astype(F32) for part in split(line))
    return jnp.where(piece < 3, one, jnp.where(piece < 5, two, three))


def rhs_kernel(
    angle, eps, e, h, ge, gh, lab, prof_in, zs_in, lt_in, w_in,
    rx_o, ry_o, ax_o, ay_o, psx_o, psy_o, gs_o, inv_o, h_o, w, keep_o, send_o,
    e_s, ge_s, gh_s, lab_s, sems, prof_s, prof, zs, lt,
):
    core = lax.rem(lax.axis_index("gz"), 2)

    def fetch(which, x):
        at = pl.ds(x, 1)
        return (
            lambda: pltpu.make_async_copy(lab.at[at], lab_s.at[at], sems.at[0, x]),
            lambda: pltpu.make_async_copy(ge.at[:, at], ge_s.at[:, at], sems.at[1, x]),
            lambda: pltpu.make_async_copy(h.at[:, at], h_o.at[:, at], sems.at[2, x]),
            lambda: pltpu.make_async_copy(gh.at[:, at], gh_s.at[:, at], sems.at[3, x]),
            lambda: pltpu.make_async_copy(e.at[pl.ds(0, 2), at], e_s.at[:, at], sems.at[4, x]),
        )[which]()

    tables = [
        pltpu.make_async_copy(source, target, sems.at[5, n + 1])
        for n, (source, target) in enumerate(
            ((prof_in.at[angle[0]], prof), (w_in, w), (zs_in, zs), (lt_in, lt))
        )
    ]
    for copy in tables:
        copy.start()
    early, late = (0, 1), (2, 3, 4)
    for which in early:
        fetch(which, 0).start()
    for x in range(X):
        if x + 1 < X:
            for which in early:
                fetch(which, x + 1).start()
        for which in late:
            fetch(which, x).start()

    for copy in tables:
        copy.wait()
    both = jnp.concatenate([prof[0], prof[1]], 0)
    rows = jnp.concatenate(six_rows(both) + [jnp.zeros((32, Y), F32)], 0)
    prof_s[...] = rows.T.astype(BF)
    corners = [
        jnp.broadcast_to(w[p:p + 1, q:q + 1], (1, CZ))
        for p, q in ((0, 0), (0, CZ - 1), (CZ - 1, CZ - 1))
    ]
    corners = jnp.concatenate(corners + [jnp.zeros((5, CZ), F32)], 0)
    keep_o[CORNERS] = corners
    send_o[CORNERS] = corners

    row16 = iota((16, CZ), 0)
    lane16 = iota((16, CZ), 1)
    ends = jnp.where(row16 < 8, w[0:1, :], w[CZ - 1:CZ, :])
    ends_parts = [part.astype(F32) for part in split(ends)]
    slot = lax.rem(row16, 8)

    rowz = iota((CZ, CZ), 0)
    piece, within = rowz // 16, lax.rem(rowz, 16)
    z_table = jnp.where(piece < 6, six_table(zs[...], piece), 0.0)

    lane = iota((Y, CZ), 1)
    row8 = iota((8, Y), 0)
    for which in early:
        fetch(which, 0).wait()
    inv_o[0] = inverse_eps(lab_s[0], eps)

    def one_pair(i, carry):
        acc_ends = jnp.zeros((16, Y), F32)
        acc_tops = jnp.zeros((16, Y), F32)
        for j in range(2):
            x = 2 * i + j
            following = jnp.minimum(x + 1, X - 1)
            previous = jnp.maximum(x - 1, 0)
            more = (x < X - 1).astype(F32)
            less = (x > 0).astype(F32)

            @pl.when(x < X - 1)
            def _():
                for which in early:
                    fetch(which, x + 1).wait()

            for which in late:
                fetch(which, x).wait()
            inv = inv_o[x]
            inv_up = inverse_eps(lab_s[following], eps)
            inv_o[following] = inv_up
            sg = inv * ge_s[2, x]
            sg_up = inv_up * ge_s[2, following] * more
            z_pick = jnp.concatenate(
                [jnp.where(within == x, z_table, 0.0), jnp.where(within == 8 + x, z_table, 0.0)], 1
            ).astype(BF)
            cur = mm(prof_s[...], z_pick)
            h_x, h_y, h_z = h_o[0, x], h_o[1, x], h_o[2, x]
            g_hz = gh_s[2, x]
            bar_hy = gh_s[1, x] - (sg_up - sg)
            bar_hx = gh_s[0, x] + y_up(sg)
            p_x = y_down(h_z) - z_down(h_y) - cur[:, :CZ]
            p_y = z_down(h_x) - (h_z - h_o[2, previous] * less) - cur[:, CZ:]
            r_x = lt[...] * e_s[0, x] + inv * p_x
            r_y = lt[...] * e_s[1, x] + inv * p_y
            a_x = ge_s[0, x] - y_down(g_hz) - z_down(bar_hy)
            a_y = ge_s[1, x] + (g_hz - gh_s[2, previous] * less) - z_down(bar_hx)
            rx_o[x], ry_o[x], ax_o[x], ay_o[x] = r_x, r_y, a_x, a_y
            psx_o[x] = -inv * (inv * p_x)
            psy_o[x] = -inv * (inv * p_y)
            gs_o[x] = -inv * sg
            for c, field in enumerate((r_x, r_y, a_x, a_y)):
                mask = slot == 4 * j + c
                lhs = jnp.concatenate([jnp.where(mask, part, 0.0) for part in ends_parts], 0)
                lhs = jnp.concatenate([lhs, lhs], 1).astype(BF)
                out = mm(lhs, in_two(field), NT)
                acc_ends += out[0:16] + out[16:32] + out[32:48]

            packed = jnp.where(lane == CZ - 1, h_y, inv)
            packed = jnp.where(lane == CZ - 2, -pltpu.roll(h_x, CZ - 1, 1), packed)
            packed = jnp.where(lane == CZ - 3, pltpu.roll(bar_hy, CZ - 2, 1), packed)
            packed = jnp.where(lane == CZ - 4, pltpu.roll(bar_hx, CZ - 3, 1), packed)
            c16 = slot - 4 * j
            own = (c16 >= 0) & (c16 < 4)
            pick = jnp.where(
                own & (row16 < 8) & (lane16 == CZ - 1 - c16), 1.0,
                jnp.where(own & (row16 >= 8) & (c16 == i) & (lane16 == 0), 1.0, 0.0),
            )
            acc_tops += mm(jnp.concatenate([pick, pick], 1).astype(BF), in_two(packed), NT)

        tops, planes = acc_tops[0:8], acc_tops[8:16]
        outgoing = acc_ends[8:16] + jnp.where(lax.rem(row8, 4) >= 2, tops, 0.0)
        comp = lax.rem(iota((8, CZ), 0), 4)
        second = lax.rem(i, 2)
        tops = jnp.where(second == 0, tops, pltpu.roll(tops, 2, 0))
        tops_mine = comp // 2 == second
        planes_mine = comp == i

        def put(ref, low):
            def half(v):
                return jnp.where((core == 0) == low, v[:, :CZ], v[:, CZ:])

            ref[i] = half(acc_ends[0:8])
            ref[4 + i] = half(outgoing)
            slab = 8 + i // 2
            ref[slab] = jnp.where(tops_mine, half(tops), ref[slab])
            ref[10] = jnp.where(planes_mine, half(planes), ref[10])

        put(keep_o, True)
        put(send_o, False)
        return carry

    lax.fori_loop(0, X // 2, one_pair, 0, unroll=True)


def unpack(ref):
    m = ref[...]
    comp = lax.rem(iota((8, CZ), 0), 4)
    tops = [jnp.where(comp < 2, v, 0.0) for p in (m[8], m[9]) for v in (p, pltpu.roll(p, 6, 0))]
    planes = m[10]

    def plane(q):
        return jnp.where(
            comp == 0, pltpu.roll(planes, (8 - q) % 8, 0),
            jnp.where(comp == 1, pltpu.roll(planes, (9 - q) % 8, 0), 0.0),
        )

    return dict(
        f=m[0:4], l=m[4:8], t=jnp.stack(tops), k=jnp.stack([plane(q) for q in range(4)]),
        a=m[CORNERS, 0:1, :], c=m[CORNERS, 1:2, :], z=m[CORNERS, 2:3, :],
    )


def repack(s, ref):
    comp = lax.rem(iota((8, CZ), 0), 4)
    ref[0:4] = s["f"]
    ref[4:8] = s["l"]
    for p in range(2):
        ref[8 + p] = jnp.where(comp < 2, s["t"][2 * p], pltpu.roll(s["t"][2 * p + 1], 2, 0))
    planes = s["k"][0]
    for q in range(1, 4):
        planes = jnp.where(comp == q, pltpu.roll(s["k"][q], q, 0), planes)
    ref[10] = planes
    ref[CORNERS] = jnp.concatenate([s["a"], s["c"], s["z"], jnp.zeros((5, CZ), F32)], 0)


def order(bit, own, other):
    lower = {n: jnp.where(bit == 0, own[n], other[n]) for n in own}
    upper = {n: jnp.where(bit == 0, other[n], own[n]) for n in own}
    return lower, upper


def coupled(lower, upper):
    delta = upper["k"] * lower["t"]
    f_up = upper["f"] + upper["a"] * delta
    l_up = upper["l"] + upper["c"] * delta
    inv = 1.0 / (1.0 - upper["a"] * lower["z"])
    return f_up, l_up, inv


def combine(lower, upper):
    f_up, l_up, inv = coupled(lower, upper)
    t = (f_up + upper["a"] * lower["l"]) * inv
    u = (lower["l"] + lower["z"] * f_up) * inv
    return dict(
        f=lower["f"] + lower["c"] * t,
        l=l_up + upper["c"] * u,
        t=upper["t"],
        k=lower["k"],
        a=lower["a"] + lower["c"] * lower["c"] * upper["a"] * inv,
        c=lower["c"] * upper["c"] * inv,
        z=upper["z"] + upper["c"] * upper["c"] * lower["z"] * inv,
    )


def outside(lower, upper, below, above):
    f_up, _, inv = coupled(lower, upper)
    l_low = lower["l"] + lower["c"] * below
    f_up = f_up + upper["c"] * above
    return (f_up + upper["a"] * l_low) * inv, (l_low + lower["z"] * f_up) * inv


def pick_outside(bit, lower, upper, below, above):
    t, u = outside(lower, upper, below, above)
    return jnp.where(bit == 0, below, u), jnp.where(bit == 0, t, above)


def bits():
    gz = lax.axis_index("gz")
    core, low_z, high_z = lax.rem(gz, 2), lax.rem(gz // 2, 2), lax.rem(gz // 4, 2)
    return core, low_z, high_z, lax.rem(gz // 8, 2), gz // 16


def chip_kernel(own, other, out):
    core = bits()[0]
    repack(combine(*order(core, unpack(own), unpack(other))), out)


def four(low, high, own, m1, m2, m3):
    first = order(low, own, m1)
    pair = combine(*first)
    return first, order(high, pair, combine(*order(low, m2, m3)))


def group_kernel(m3, m2, m1, m0, after, out):
    _, low, high, _, _ = bits()
    repack(combine(*four(low, high, *(unpack(m) for m in (m0, m1, m2, m3)))[1]), out)


def back_kernel(n2, n3, n1, n0, m3, m2, m1, m0, a0, a1, after, keep_o, send_o):
    core, zl, zh, xl, xh = bits()
    chip = order(core, unpack(a0), unpack(a1))
    m0, m1, m2, m3 = (unpack(m) for m in (m0, m1, m2, m3))
    n0, n1, n2, n3 = (unpack(n) for n in (n0, n1, n2, n3))
    z_first, z_second = four(zl, zh, m0, m1, m2, m3)
    x_first, x_second = four(xl, xh, n0, n1, n2, n3)
    zero = jnp.zeros_like(m0["f"])
    edge = (zero, zero)
    edge = pick_outside(xh, *x_second, *edge)
    edge = pick_outside(xl, *x_first, *edge)
    edge = pick_outside(zh, *z_second, *edge)
    edge = pick_outside(zl, *z_first, *edge)
    lower, upper = chip
    t, u = outside(lower, upper, *edge)
    under_x = jnp.where(xl == 1, n1["t"], jnp.where(xh == 1, n3["t"], zero))
    under = jnp.where(zl == 1, m1["t"], jnp.where(zh == 1, m3["t"], under_x))
    results = []
    for block, below, above, plane in ((lower, edge[0], t, under), (upper, u, edge[1], lower["t"])):
        below = below + block["k"] * plane
        first = block["f"] + block["a"] * below + block["c"] * above
        extra = jnp.stack([first[q] * pltpu.roll(plane[q], 2, 0) for q in range(4)])
        results.append((below, above, extra))
    for part in range(3):
        low, high = results[0][part], results[1][part]
        keep_o[4 * part:4 * part + 4] = jnp.where(core == 0, low, high)
        send_o[4 * part:4 * part + 4] = jnp.where(core == 0, high, low)


def product_tables(w):
    one, two, three = split(w.T)
    full = jnp.concatenate([one, two], 1)
    return jnp.concatenate([full, full], 0), jnp.concatenate([one, three], 0)


def product(field, tables):
    one, two, three = split(field)
    wide = mm(jnp.concatenate([one, two], 1), tables[0])
    narrow = mm(jnp.concatenate([three, one], 1), tables[1])
    return wide[:, :CZ] + wide[:, CZ:] + narrow


def adjoint_kernel(ax, ay, psx, psy, w, e, after, out, ez_o, sem):
    ez_copy = pltpu.make_async_copy(e.at[2], ez_o, sem)
    ez_copy.start()
    tables = product_tables(w[...])

    def one(x, carry):
        out[x] = psx[x] * product(ax[x], tables) + psy[x] * product(ay[x], tables)
        return carry

    lax.fori_loop(0, X, one, 0, unroll=2)
    ez_copy.wait()


def primal_kernel(rx, ry, h, ez, gs, part, w, after, ex_o, ey_o, grad_o):
    tables = product_tables(w[...])

    def one(x, hy_prev):
        more = (x < X - 1).astype(F32)
        e_x, e_y = product(rx[x], tables), product(ry[x], tables)
        ex_o[x], ey_o[x] = e_x, e_y
        e_z = ez[x]
        hy = h[1, x] + z_up(e_x) - (ez[jnp.minimum(x + 1, X - 1)] * more - e_z)
        hx = h[0, x] + z_up(e_y) - y_up(e_z)
        grad_o[x] = part[x] + gs[x] * (hy - hy_prev - y_down(hx))
        return hy

    lax.fori_loop(0, X, one, jnp.zeros((Y, CZ), F32), unroll=2)


def edge_rows(keep, recv, slab):
    core = lax.rem(lax.axis_index("gz"), 2)
    a, b = keep[slab], recv[slab]
    return jnp.concatenate([jnp.where(core == 0, a, b), jnp.where(core == 0, b, a)], 1)


def columns(below, above):
    rows = six_rows(below) + six_rows(above) + [jnp.zeros((32, Y), F32)]
    return jnp.concatenate(rows, 0).T.astype(BF)


def edge_table(first, last):
    piece = iota((CZ, CZ), 0) // 8
    table = jnp.where(piece < 6, six_table(first, piece), six_table(last, piece - 6))
    return jnp.where(piece < 12, table, 0.0)


def picked(table, row):
    return jnp.where(lax.rem(iota((CZ, CZ), 0), 8) == row, table, 0.0)


def gradient_kernel(k, grad, psx, psy, gs, inv, keep, recv, w, out):
    q = lax.axis_index("src") ^ k
    below, above, extra = (edge_rows(keep, recv, 4 * part + q) for part in range(3))
    before = jnp.maximum(q - 1, 0)
    has = (q > 0).astype(F32)
    row = iota((8, Y), 0)
    lane = iota((8, Y), 1)

    def curl_rows(now, previous):
        shifted = jnp.where(row < 4, pltpu.roll(previous, 4, 0), pltpu.roll(now, 4, 0))
        along_y = now - jnp.where(lane == 0, 0.0, pltpu.roll(now, 1, 1))
        return now - shifted - pltpu.roll(along_y, 7, 0)

    curl_below = curl_rows(below, edge_rows(keep, recv, before) * has)
    curl_above = curl_rows(above, edge_rows(keep, recv, 4 + before) * has)
    kind = lax.rem(row, 4)
    plane = pltpu.roll(extra, 7, 0) + pltpu.roll(extra, 6, 0)
    below = jnp.where(kind == 0, curl_below, jnp.where(kind == 1, plane, below))
    above = jnp.where(kind == 0, curl_above, jnp.where(kind == 1, 0.0, above))
    cols = columns(below, above)
    wt = w[...].T
    first, last = wt[0:1, :], wt[CZ - 1:CZ, :]
    lane1 = iota((1, CZ), 1)
    top = jnp.where(lane1 == CZ - 1, 1.0, 0.0)
    first_up = jnp.where(lane1 == CZ - 1, 0.0, pltpu.roll(first, CZ - 1, 1)) - first
    last_up = jnp.where(lane1 == CZ - 1, 0.0, pltpu.roll(last, CZ - 1, 1)) - last + top
    lam_table = edge_table(first, last)
    curl_table = edge_table(first_up, last_up)
    plane_table = edge_table(jnp.where(lane1 == 0, 1.0, 0.0), jnp.zeros((1, CZ), F32))
    for j in range(2):
        r = 4 * j
        lam = mm(cols, jnp.concatenate([picked(lam_table, r + 2), picked(lam_table, r + 3)], 1).astype(BF))
        rest = mm(cols, jnp.concatenate([picked(curl_table, r), picked(plane_table, r + 1)], 1).astype(BF))
        x = 2 * q + j
        out[j] = (
            grad[x] + psx[x] * lam[:, :CZ] + psy[x] * lam[:, CZ:]
            + gs[x] * rest[:, :CZ] - inv[x] * inv[x] * rest[:, CZ:]
        )


def output_kernel(ex, ey, h, ez, inv, keep, recv, w, e_o, h_o, e_s, h_s, sems):
    wt = w[...].T
    table = edge_table(wt[0:1, :], wt[CZ - 1:CZ, :])
    lane = iota((CZ, CZ), 1)
    piece = iota((CZ, CZ), 0) // 8
    ones = jnp.where((piece >= 6) & (piece < 9) & (lane == CZ - 1), 1.0, 0.0)

    def edges(i):
        return columns(edge_rows(keep, recv, i), edge_rows(keep, recv, 4 + i))

    def corrected(source, table, row):
        return mm(source, picked(table, row).astype(BF))

    def copies(x):
        at = pl.ds(x, 1)
        return (
            pltpu.make_async_copy(e_s.at[:, at], e_o.at[:, at], sems.at[0, x]),
            pltpu.make_async_copy(h_s.at[:, at], h_o.at[:, at], sems.at[1, x]),
        )

    def one_pair(i, carry):
        cols, hy_prev = carry
        last = i == X // 2 - 1
        cols_next = edges(jnp.minimum(i + 1, X // 2 - 1))
        x = 2 * i
        more = jnp.where(last, 0.0, 1.0)
        following = jnp.minimum(x + 2, X - 1)
        e_x = [ex[x + j] + corrected(cols, table, 4 * j) for j in range(2)]
        e_y = [ey[x + j] + corrected(cols, table, 4 * j + 1) for j in range(2)]
        e_y.append((ey[following] + corrected(cols_next, table, 1)) * more)
        e_z = [ez[x], ez[x + 1], ez[following] * more]
        for j in range(2):
            hy = h[1, x + j] + z_up(e_x[j]) + corrected(cols, ones, 4 * j) - (e_z[j + 1] - e_z[j])
            hx = h[0, x + j] + z_up(e_y[j]) + corrected(cols, ones, 4 * j + 1) - y_up(e_z[j])
            curl = hy - hy_prev - y_down(hx)
            hy_prev = hy
            e_s[0, x + j] = e_x[j]
            e_s[1, x + j] = e_y[j]
            e_s[2, x + j] = e_z[j] + inv[x + j] * curl
            h_s[0, x + j] = hx
            h_s[1, x + j] = hy
            h_s[2, x + j] = h[2, x + j] - (e_y[j + 1] - e_y[j]) + y_up(e_x[j])
            for copy in copies(x + j):
                copy.start()
        return cols_next, hy_prev

    lax.fori_loop(0, X // 2, one_pair, (edges(0), jnp.zeros((Y, CZ), F32)))
    for x in range(X):
        for copy in copies(x):
            copy.wait()


def place_kernel(g1, g2, g3, g0, out, sems):
    src = lax.axis_index("src")
    copies = []
    for k, g in zip((1, 2, 3, 0), (g1, g2, g3, g0)):
        copies.append(pltpu.make_async_copy(g, out.at[pl.ds(2 * (src ^ k), 2)], sems.at[k]))
    for copy in copies:
        copy.start()
    for copy in copies:
        copy.wait()


def swap(block, axis, mask):
    return lax.ppermute(block, axis, [(i, i ^ mask) for i in range(lax.axis_size(axis))])


SMEM = pl.BlockSpec(memory_space=pltpu.SMEM)
VMEM = pl.BlockSpec(memory_space=pltpu.VMEM)
HBM = pl.BlockSpec(memory_space=pltpu.HBM)
ANY = pl.BlockSpec(memory_space=pl.ANY)


def shape(*dims):
    return jax.ShapeDtypeStruct(dims, F32)


def call(kernel, name, in_specs, outs, us, mib, out_specs=None, scratch=()):
    return pl.pallas_call(
        kernel,
        in_specs=in_specs,
        out_specs=out_specs or [VMEM] * len(outs),
        out_shape=outs,
        scratch_shapes=scratch,
        compiler_params=pltpu.CompilerParams(vmem_limit_bytes=mib * MIB),
        cost_estimate=pl.CostEstimate(flops=1000, bytes_accessed=int(us * 3.0e6), transcendentals=0),
        name=name,
    )


def in_hbm(array):
    return pltpu.with_memory_space_constraint(array, pltpu.HBM)


def body(
    fields_e, fields_h, cot_e, cot_h, labels, region_eps, angle_index, profiles, zsheet,
    layer_term, block_inverse,
):
    e, h, ge, gh = fields_e[0], fields_h[0], cot_e[0], cot_h[0]
    zs, lt = zsheet.reshape(1, CZ), layer_term.reshape(1, CZ)
    slab = shape(X, Y, CZ)
    message = shape(SLABS, 8, CZ)

    def space(*dims, dtype=F32):
        return pltpu.VMEM(dims, dtype)

    rx, ry, ax, ay, psx, psy, gs, inv, hv, w, keep, send = call(
        rhs_kernel, "right_hand_sides",
        [SMEM, SMEM] + [HBM] * 9,
        [slab] * 8 + [shape(3, X, Y, CZ), shape(CZ, CZ)] + [message] * 2,
        6, 24,
        scratch=[
            space(2, X, Y, CZ), space(3, X, Y, CZ), space(3, X, Y, CZ),
            space(X, Y, CZ, dtype=jnp.int32), pltpu.SemaphoreType.DMA((6, X)),
            space(Y, CZ, dtype=BF), space(2, X, Y), space(1, CZ), space(1, CZ),
        ],
    )(angle_index, *map(in_hbm, (region_eps, e, h, ge, gh, labels, profiles, zs, lt, block_inverse)))

    other = swap(send, "gz", 1)
    (m0,) = call(chip_kernel, "chip", [VMEM] * 2, [message], 0.5, 4)(keep, other)
    m3, m2, m1 = (swap(m0, "gz", 2 * k) for k in (3, 2, 1))

    adjoint, ez = call(
        adjoint_kernel, "adjoint_products", [VMEM] * 5 + [HBM, ANY], [slab] * 2, 3, 8,
        scratch=[pltpu.SemaphoreType.DMA],
    )(ax, ay, psx, psy, w, in_hbm(e), m0)
    (n0,) = call(group_kernel, "group", [VMEM] * 4 + [ANY], [message], 0.5, 4)(m3, m2, m1, m0, adjoint)
    n2, n3, n1 = (swap(n0, "gz", 8 * k) for k in (2, 3, 1))

    ex, ey, grad = call(primal_kernel, "primal_products", [VMEM] * 7 + [ANY], [slab] * 3, 4, 8)(
        rx, ry, hv, ez, gs, adjoint, w, n0
    )
    own_edges, send_edges = call(
        back_kernel, "back", [VMEM] * 10 + [ANY], [shape(12, 8, CZ)] * 2, 0.5, 4
    )(n2, n3, n1, n0, m3, m2, m1, m0, keep, other, ex)
    other_edges = swap(send_edges, "gz", 1)

    def gradient(k):
        return call(
            lambda *refs: gradient_kernel(k, *refs), f"gradient_{k}", [VMEM] * 8,
            [shape(2, Y, CZ)], 1, 8,
        )(grad, psx, psy, gs, inv, own_edges, other_edges, w)[0]

    arrived = [swap(gradient(k), "src", k) for k in (1, 2, 3)]
    own = gradient(0)

    e_new, h_new = call(
        output_kernel, "outputs", [VMEM] * 8, [shape(3, X, Y, CZ)] * 2, 6, 16,
        out_specs=[HBM] * 2,
        scratch=[space(3, X, Y, CZ), space(3, X, Y, CZ), pltpu.SemaphoreType.DMA((2, X))],
    )(ex, ey, hv, ez, inv, own_edges, other_edges, w)

    total = own + arrived[0] + arrived[1] + arrived[2]
    one, two, three = (swap(total, "src", k) for k in (1, 2, 3))
    (eps_grad,) = call(
        place_kernel, "place", [ANY] * 4, [slab], 1, 4, out_specs=[HBM],
        scratch=[pltpu.SemaphoreType.DMA((4,))],
    )(one, two, three, total)
    return (e_new[None], h_new[None], eps_grad)


def solution(mesh):
    field = P("src", None, None, None, "gz")
    return jax.shard_map(
        body,
        mesh=mesh,
        in_specs=(
            field, field, field, field, P(None, None, "gz"), P(), P("src"), P(), P("gz"), P("gz"),
            P("gz", None),
        ),
        out_specs=(field, field, P(None, None, "gz")),
        check_vma=False,
    )
```

```python
import jax
import jax.numpy as jnp
from jax import lax
from jax.experimental import pallas as pl
from jax.experimental.pallas import tpu as pltpu
from jax.sharding import PartitionSpec as P

F32 = jnp.float32
BF = jnp.bfloat16
X, Y, CZ = 8, 256, 128
NN = (((1,), (0,)), ((), ()))
NT = (((1,), (1,)), ((), ()))
SLABS = 12
CORNERS = SLABS - 1
MIB = 1024 * 1024


def split(v):
    one = v.astype(BF)
    rest = v - one.astype(F32)
    two = rest.astype(BF)
    three = (rest - two.astype(F32)).astype(BF)
    return one, two, three


def in_two(v):
    one = v.astype(BF)
    return jnp.concatenate([one, (v - one.astype(F32)).astype(BF)], 1)


def mm(a, b, dims=NN):
    return lax.dot_general(a, b, dims, preferred_element_type=F32)


def iota(shape, axis):
    return lax.broadcasted_iota(jnp.int32, shape, axis)


def y_down(v):
    return v - jnp.where(iota(v.shape, 0) == 0, 0.0, pltpu.roll(v, 1, 0))


def y_up(v):
    n = v.shape[0]
    return jnp.where(iota(v.shape, 0) == n - 1, 0.0, pltpu.roll(v, n - 1, 0)) - v


def z_down(v):
    return v - jnp.where(iota(v.shape, 1) == 0, 0.0, pltpu.roll(v, 1, 1))


def z_up(v):
    n = v.shape[1]
    return jnp.where(iota(v.shape, 1) == n - 1, 0.0, pltpu.roll(v, n - 1, 1)) - v


def inverse_eps(labels, eps_ref):
    rows = [1.0 / jnp.full((1, CZ), eps_ref[r], F32) for r in range(4)]
    out = jnp.where(labels == 2, rows[2], rows[3])
    out = jnp.where(labels == 1, rows[1], out)
    return jnp.where(labels == 0, rows[0], out)


def six_rows(rows):
    one, two, three = (part.astype(F32) for part in split(rows))
    return [one, two, three, one, two, one]


def six_table(line, piece):
    one, two, three = (part.astype(F32) for part in split(line))
    return jnp.where(piece < 3, one, jnp.where(piece < 5, two, three))


def rhs_kernel(
    angle, eps, e, h, ge, gh, lab, prof_in, zs_in, lt_in, w_in,
    rx_o, ry_o, ax_o, ay_o, psx_o, psy_o, gs_o, inv_o, h_o, w, keep_o, send_o,
    e_s, ge_s, gh_s, lab_s, sems, prof_s, prof, zs, lt,
):
    core = lax.rem(lax.axis_index("gz"), 2)

    def fetch(which, x):
        at = pl.ds(x, 1)
        return (
            lambda: pltpu.make_async_copy(lab.at[at], lab_s.at[at], sems.at[0, x]),
            lambda: pltpu.make_async_copy(ge.at[:, at], ge_s.at[:, at], sems.at[1, x]),
            lambda: pltpu.make_async_copy(h.at[:, at], h_o.at[:, at], sems.at[2, x]),
            lambda: pltpu.make_async_copy(gh.at[:, at], gh_s.at[:, at], sems.at[3, x]),
            lambda: pltpu.make_async_copy(e.at[pl.ds(0, 2), at], e_s.at[:, at], sems.at[4, x]),
        )[which]()

    tables = [
        pltpu.make_async_copy(source, target, sems.at[5, n + 1])
        for n, (source, target) in enumerate(
            ((prof_in.at[angle[0]], prof), (w_in, w), (zs_in, zs), (lt_in, lt))
        )
    ]
    for copy in tables:
        copy.start()
    early, late = (0, 1), (2, 3, 4)
    for which in early:
        fetch(which, 0).start()
    for x in range(X):
        if x + 1 < X:
            for which in early:
                fetch(which, x + 1).start()
        for which in late:
            fetch(which, x).start()

    for copy in tables:
        copy.wait()
    both = jnp.concatenate([prof[0], prof[1]], 0)
    rows = jnp.concatenate(six_rows(both) + [jnp.zeros((32, Y), F32)], 0)
    prof_s[...] = rows.T.astype(BF)
    corners = [
        jnp.broadcast_to(w[p:p + 1, q:q + 1], (1, CZ))
        for p, q in ((0, 0), (0, CZ - 1), (CZ - 1, CZ - 1))
    ]
    corners = jnp.concatenate(corners + [jnp.zeros((5, CZ), F32)], 0)
    keep_o[CORNERS] = corners
    send_o[CORNERS] = corners

    row16 = iota((16, CZ), 0)
    lane16 = iota((16, CZ), 1)
    ends = jnp.where(row16 < 8, w[0:1, :], w[CZ - 1:CZ, :])
    ends_parts = [part.astype(F32) for part in split(ends)]
    slot = lax.rem(row16, 8)

    rowz = iota((CZ, CZ), 0)
    piece, within = rowz // 16, lax.rem(rowz, 16)
    z_table = jnp.where(piece < 6, six_table(zs[...], piece), 0.0)

    lane = iota((Y, CZ), 1)
    row8 = iota((8, Y), 0)
    for which in early:
        fetch(which, 0).wait()
    inv_o[0] = inverse_eps(lab_s[0], eps)

    def one_pair(i, carry):
        acc_ends = jnp.zeros((16, Y), F32)
        acc_tops = jnp.zeros((16, Y), F32)
        for j in range(2):
            x = 2 * i + j
            following = jnp.minimum(x + 1, X - 1)
            previous = jnp.maximum(x - 1, 0)
            more = (x < X - 1).astype(F32)
            less = (x > 0).astype(F32)

            @pl.when(x < X - 1)
            def _():
                for which in early:
                    fetch(which, x + 1).wait()

            for which in late:
                fetch(which, x).wait()
            inv = inv_o[x]
            inv_up = inverse_eps(lab_s[following], eps)
            inv_o[following] = inv_up
            sg = inv * ge_s[2, x]
            sg_up = inv_up * ge_s[2, following] * more
            z_pick = jnp.concatenate(
                [jnp.where(within == x, z_table, 0.0), jnp.where(within == 8 + x, z_table, 0.0)], 1
            ).astype(BF)
            cur = mm(prof_s[...], z_pick)
            h_x, h_y, h_z = h_o[0, x], h_o[1, x], h_o[2, x]
            g_hz = gh_s[2, x]
            bar_hy = gh_s[1, x] - (sg_up - sg)
            bar_hx = gh_s[0, x] + y_up(sg)
            p_x = y_down(h_z) - z_down(h_y) - cur[:, :CZ]
            p_y = z_down(h_x) - (h_z - h_o[2, previous] * less) - cur[:, CZ:]
            r_x = lt[...] * e_s[0, x] + inv * p_x
            r_y = lt[...] * e_s[1, x] + inv * p_y
            a_x = ge_s[0, x] - y_down(g_hz) - z_down(bar_hy)
            a_y = ge_s[1, x] + (g_hz - gh_s[2, previous] * less) - z_down(bar_hx)
            rx_o[x], ry_o[x], ax_o[x], ay_o[x] = r_x, r_y, a_x, a_y
            psx_o[x] = -inv * (inv * p_x)
            psy_o[x] = -inv * (inv * p_y)
            gs_o[x] = -inv * sg
            for c, field in enumerate((r_x, r_y, a_x, a_y)):
                mask = slot == 4 * j + c
                lhs = jnp.concatenate([jnp.where(mask, part, 0.0) for part in ends_parts], 0)
                lhs = jnp.concatenate([lhs, lhs], 1).astype(BF)
                out = mm(lhs, in_two(field), NT)
                acc_ends += out[0:16] + out[16:32] + out[32:48]

            packed = jnp.where(lane == CZ - 1, h_y, inv)
            packed = jnp.where(lane == CZ - 2, -pltpu.roll(h_x, CZ - 1, 1), packed)
            packed = jnp.where(lane == CZ - 3, pltpu.roll(bar_hy, CZ - 2, 1), packed)
            packed = jnp.where(lane == CZ - 4, pltpu.roll(bar_hx, CZ - 3, 1), packed)
            c16 = slot - 4 * j
            own = (c16 >= 0) & (c16 < 4)
            pick = jnp.where(
                own & (row16 < 8) & (lane16 == CZ - 1 - c16), 1.0,
                jnp.where(own & (row16 >= 8) & (c16 == i) & (lane16 == 0), 1.0, 0.0),
            )
            acc_tops += mm(jnp.concatenate([pick, pick], 1).astype(BF), in_two(packed), NT)

        tops, planes = acc_tops[0:8], acc_tops[8:16]
        outgoing = acc_ends[8:16] + jnp.where(lax.rem(row8, 4) >= 2, tops, 0.0)
        comp = lax.rem(iota((8, CZ), 0), 4)
        second = lax.rem(i, 2)
        tops = jnp.where(second == 0, tops, pltpu.roll(tops, 2, 0))
        tops_mine = comp // 2 == second
        planes_mine = comp == i

        def put(ref, low):
            def half(v):
                return jnp.where((core == 0) == low, v[:, :CZ], v[:, CZ:])

            ref[i] = half(acc_ends[0:8])
            ref[4 + i] = half(outgoing)
            slab = 8 + i // 2
            ref[slab] = jnp.where(tops_mine, half(tops), ref[slab])
            ref[10] = jnp.where(planes_mine, half(planes), ref[10])

        put(keep_o, True)
        put(send_o, False)
        return carry

    lax.fori_loop(0, X // 2, one_pair, 0, unroll=True)


def unpack(ref):
    m = ref[...]
    comp = lax.rem(iota((8, CZ), 0), 4)
    tops = [jnp.where(comp < 2, v, 0.0) for p in (m[8], m[9]) for v in (p, pltpu.roll(p, 6, 0))]
    planes = m[10]

    def plane(q):
        return jnp.where(
            comp == 0, pltpu.roll(planes, (8 - q) % 8, 0),
            jnp.where(comp == 1, pltpu.roll(planes, (9 - q) % 8, 0), 0.0),
        )

    return dict(
        f=m[0:4], l=m[4:8], t=jnp.stack(tops), k=jnp.stack([plane(q) for q in range(4)]),
        a=m[CORNERS, 0:1, :], c=m[CORNERS, 1:2, :], z=m[CORNERS, 2:3, :],
    )


def repack(s, ref):
    comp = lax.rem(iota((8, CZ), 0), 4)
    ref[0:4] = s["f"]
    ref[4:8] = s["l"]
    for p in range(2):
        ref[8 + p] = jnp.where(comp < 2, s["t"][2 * p], pltpu.roll(s["t"][2 * p + 1], 2, 0))
    planes = s["k"][0]
    for q in range(1, 4):
        planes = jnp.where(comp == q, pltpu.roll(s["k"][q], q, 0), planes)
    ref[10] = planes
    ref[CORNERS] = jnp.concatenate([s["a"], s["c"], s["z"], jnp.zeros((5, CZ), F32)], 0)


def order(bit, own, other):
    lower = {n: jnp.where(bit == 0, own[n], other[n]) for n in own}
    upper = {n: jnp.where(bit == 0, other[n], own[n]) for n in own}
    return lower, upper


def coupled(lower, upper):
    delta = upper["k"] * lower["t"]
    f_up = upper["f"] + upper["a"] * delta
    l_up = upper["l"] + upper["c"] * delta
    inv = 1.0 / (1.0 - upper["a"] * lower["z"])
    return f_up, l_up, inv


def combine(lower, upper):
    f_up, l_up, inv = coupled(lower, upper)
    t = (f_up + upper["a"] * lower["l"]) * inv
    u = (lower["l"] + lower["z"] * f_up) * inv
    return dict(
        f=lower["f"] + lower["c"] * t,
        l=l_up + upper["c"] * u,
        t=upper["t"],
        k=lower["k"],
        a=lower["a"] + lower["c"] * lower["c"] * upper["a"] * inv,
        c=lower["c"] * upper["c"] * inv,
        z=upper["z"] + upper["c"] * upper["c"] * lower["z"] * inv,
    )


def outside(lower, upper, below, above):
    f_up, _, inv = coupled(lower, upper)
    l_low = lower["l"] + lower["c"] * below
    f_up = f_up + upper["c"] * above
    return (f_up + upper["a"] * l_low) * inv, (l_low + lower["z"] * f_up) * inv


def pick_outside(bit, lower, upper, below, above):
    t, u = outside(lower, upper, below, above)
    return jnp.where(bit == 0, below, u), jnp.where(bit == 0, t, above)


def bits():
    gz = lax.axis_index("gz")
    core, low_z, high_z = lax.rem(gz, 2), lax.rem(gz // 2, 2), lax.rem(gz // 4, 2)
    return core, low_z, high_z, lax.rem(gz // 8, 2), gz // 16


def chip_kernel(own, other, out):
    core = bits()[0]
    repack(combine(*order(core, unpack(own), unpack(other))), out)


def four(low, high, own, m1, m2, m3):
    first = order(low, own, m1)
    pair = combine(*first)
    return first, order(high, pair, combine(*order(low, m2, m3)))


def group_kernel(m3, m2, m1, m0, after, out):
    _, low, high, _, _ = bits()
    repack(combine(*four(low, high, *(unpack(m) for m in (m0, m1, m2, m3)))[1]), out)


def back_kernel(n2, n3, n1, n0, m3, m2, m1, m0, a0, a1, after, keep_o, send_o):
    core, zl, zh, xl, xh = bits()
    chip = order(core, unpack(a0), unpack(a1))
    m0, m1, m2, m3 = (unpack(m) for m in (m0, m1, m2, m3))
    n0, n1, n2, n3 = (unpack(n) for n in (n0, n1, n2, n3))
    z_first, z_second = four(zl, zh, m0, m1, m2, m3)
    x_first, x_second = four(xl, xh, n0, n1, n2, n3)
    zero = jnp.zeros_like(m0["f"])
    edge = (zero, zero)
    edge = pick_outside(xh, *x_second, *edge)
    edge = pick_outside(xl, *x_first, *edge)
    edge = pick_outside(zh, *z_second, *edge)
    edge = pick_outside(zl, *z_first, *edge)
    lower, upper = chip
    t, u = outside(lower, upper, *edge)
    under_x = jnp.where(xl == 1, n1["t"], jnp.where(xh == 1, n3["t"], zero))
    under = jnp.where(zl == 1, m1["t"], jnp.where(zh == 1, m3["t"], under_x))
    results = []
    for block, below, above, plane in ((lower, edge[0], t, under), (upper, u, edge[1], lower["t"])):
        below = below + block["k"] * plane
        first = block["f"] + block["a"] * below + block["c"] * above
        extra = jnp.stack([first[q] * pltpu.roll(plane[q], 2, 0) for q in range(4)])
        results.append((below, above, extra))
    for part in range(3):
        low, high = results[0][part], results[1][part]
        keep_o[4 * part:4 * part + 4] = jnp.where(core == 0, low, high)
        send_o[4 * part:4 * part + 4] = jnp.where(core == 0, high, low)


def product_tables(w):
    one, two, three = split(w.T)
    full = jnp.concatenate([one, two], 1)
    return jnp.concatenate([full, full], 0), jnp.concatenate([one, three], 0)


def product(field, tables):
    one, two, three = split(field)
    wide = mm(jnp.concatenate([one, two], 1), tables[0])
    narrow = mm(jnp.concatenate([three, one], 1), tables[1])
    return wide[:, :CZ] + wide[:, CZ:] + narrow


def adjoint_kernel(ax, ay, psx, psy, w, e, after, out, ez_o, sem):
    ez_copy = pltpu.make_async_copy(e.at[2], ez_o, sem)
    ez_copy.start()
    tables = product_tables(w[...])

    def one(x, carry):
        out[x] = psx[x] * product(ax[x], tables) + psy[x] * product(ay[x], tables)
        return carry

    lax.fori_loop(0, X, one, 0, unroll=2)
    ez_copy.wait()


def primal_kernel(rx, ry, h, ez, gs, part, w, after, ex_o, ey_o, grad_o):
    tables = product_tables(w[...])

    def one(x, hy_prev):
        more = (x < X - 1).astype(F32)
        e_x, e_y = product(rx[x], tables), product(ry[x], tables)
        ex_o[x], ey_o[x] = e_x, e_y
        e_z = ez[x]
        hy = h[1, x] + z_up(e_x) - (ez[jnp.minimum(x + 1, X - 1)] * more - e_z)
        hx = h[0, x] + z_up(e_y) - y_up(e_z)
        grad_o[x] = part[x] + gs[x] * (hy - hy_prev - y_down(hx))
        return hy

    lax.fori_loop(0, X, one, jnp.zeros((Y, CZ), F32), unroll=2)


def edge_rows(keep, recv, slab):
    core = lax.rem(lax.axis_index("gz"), 2)
    a, b = keep[slab], recv[slab]
    return jnp.concatenate([jnp.where(core == 0, a, b), jnp.where(core == 0, b, a)], 1)


def columns(below, above):
    rows = six_rows(below) + six_rows(above) + [jnp.zeros((32, Y), F32)]
    return jnp.concatenate(rows, 0).T.astype(BF)


def edge_table(first, last):
    piece = iota((CZ, CZ), 0) // 8
    table = jnp.where(piece < 6, six_table(first, piece), six_table(last, piece - 6))
    return jnp.where(piece < 12, table, 0.0)


def picked(table, row):
    return jnp.where(lax.rem(iota((CZ, CZ), 0), 8) == row, table, 0.0)


def gradient_kernel(k, grad, psx, psy, gs, inv, keep, recv, w, out):
    q = lax.axis_index("src") ^ k
    below, above, extra = (edge_rows(keep, recv, 4 * part + q) for part in range(3))
    before = jnp.maximum(q - 1, 0)
    has = (q > 0).astype(F32)
    row = iota((8, Y), 0)
    lane = iota((8, Y), 1)

    def curl_rows(now, previous):
        shifted = jnp.where(row < 4, pltpu.roll(previous, 4, 0), pltpu.roll(now, 4, 0))
        along_y = now - jnp.where(lane == 0, 0.0, pltpu.roll(now, 1, 1))
        return now - shifted - pltpu.roll(along_y, 7, 0)

    curl_below = curl_rows(below, edge_rows(keep, recv, before) * has)
    curl_above = curl_rows(above, edge_rows(keep, recv, 4 + before) * has)
    kind = lax.rem(row, 4)
    plane = pltpu.roll(extra, 7, 0) + pltpu.roll(extra, 6, 0)
    below = jnp.where(kind == 0, curl_below, jnp.where(kind == 1, plane, below))
    above = jnp.where(kind == 0, curl_above, jnp.where(kind == 1, 0.0, above))
    cols = columns(below, above)
    wt = w[...].T
    first, last = wt[0:1, :], wt[CZ - 1:CZ, :]
    lane1 = iota((1, CZ), 1)
    top = jnp.where(lane1 == CZ - 1, 1.0, 0.0)
    first_up = jnp.where(lane1 == CZ - 1, 0.0, pltpu.roll(first, CZ - 1, 1)) - first
    last_up = jnp.where(lane1 == CZ - 1, 0.0, pltpu.roll(last, CZ - 1, 1)) - last + top
    lam_table = edge_table(first, last)
    curl_table = edge_table(first_up, last_up)
    plane_table = edge_table(jnp.where(lane1 == 0, 1.0, 0.0), jnp.zeros((1, CZ), F32))
    for j in range(2):
        r = 4 * j
        lam = mm(cols, jnp.concatenate([picked(lam_table, r + 2), picked(lam_table, r + 3)], 1).astype(BF))
        rest = mm(cols, jnp.concatenate([picked(curl_table, r), picked(plane_table, r + 1)], 1).astype(BF))
        x = 2 * q + j
        out[j] = (
            grad[x] + psx[x] * lam[:, :CZ] + psy[x] * lam[:, CZ:]
            + gs[x] * rest[:, :CZ] - inv[x] * inv[x] * rest[:, CZ:]
        )


def output_kernel(ex, ey, h, ez, inv, keep, recv, w, e_o, h_o, e_s, h_s, sems):
    wt = w[...].T
    table = edge_table(wt[0:1, :], wt[CZ - 1:CZ, :])
    lane = iota((CZ, CZ), 1)
    piece = iota((CZ, CZ), 0) // 8
    ones = jnp.where((piece >= 6) & (piece < 9) & (lane == CZ - 1), 1.0, 0.0)

    def edges(i):
        return columns(edge_rows(keep, recv, i), edge_rows(keep, recv, 4 + i))

    def corrected(source, table, row):
        return mm(source, picked(table, row).astype(BF))

    def copies(x):
        at = pl.ds(x, 1)
        return (
            pltpu.make_async_copy(e_s.at[:, at], e_o.at[:, at], sems.at[0, x]),
            pltpu.make_async_copy(h_s.at[:, at], h_o.at[:, at], sems.at[1, x]),
        )

    def one_pair(i, carry):
        cols, hy_prev = carry
        last = i == X // 2 - 1
        cols_next = edges(jnp.minimum(i + 1, X // 2 - 1))
        x = 2 * i
        more = jnp.where(last, 0.0, 1.0)
        following = jnp.minimum(x + 2, X - 1)
        e_x = [ex[x + j] + corrected(cols, table, 4 * j) for j in range(2)]
        e_y = [ey[x + j] + corrected(cols, table, 4 * j + 1) for j in range(2)]
        e_y.append((ey[following] + corrected(cols_next, table, 1)) * more)
        e_z = [ez[x], ez[x + 1], ez[following] * more]
        for j in range(2):
            hy = h[1, x + j] + z_up(e_x[j]) + corrected(cols, ones, 4 * j) - (e_z[j + 1] - e_z[j])
            hx = h[0, x + j] + z_up(e_y[j]) + corrected(cols, ones, 4 * j + 1) - y_up(e_z[j])
            curl = hy - hy_prev - y_down(hx)
            hy_prev = hy
            e_s[0, x + j] = e_x[j]
            e_s[1, x + j] = e_y[j]
            e_s[2, x + j] = e_z[j] + inv[x + j] * curl
            h_s[0, x + j] = hx
            h_s[1, x + j] = hy
            h_s[2, x + j] = h[2, x + j] - (e_y[j + 1] - e_y[j]) + y_up(e_x[j])
            for copy in copies(x + j):
                copy.start()
        return cols_next, hy_prev

    lax.fori_loop(0, X // 2, one_pair, (edges(0), jnp.zeros((Y, CZ), F32)))
    for x in range(X):
        for copy in copies(x):
            copy.wait()


def place(masks, quarters, out, sems):
    src = lax.axis_index("src")
    copies = [
        pltpu.make_async_copy(g, out.at[pl.ds(2 * (src ^ k), 2)], sems.at[n])
        for n, (k, g) in enumerate(zip(masks, quarters))
    ]
    for copy in copies:
        copy.start()
    for copy in copies:
        copy.wait()


def place_first(g0, g2, out, sems):
    place((0, 2), (g0, g2), out, sems)


def place_rest(g3, g1, partial, out, sems):
    place((3, 1), (g3, g1), out, sems)


def swap(block, axis, mask):
    return lax.ppermute(block, axis, [(i, i ^ mask) for i in range(lax.axis_size(axis))])


SMEM = pl.BlockSpec(memory_space=pltpu.SMEM)
VMEM = pl.BlockSpec(memory_space=pltpu.VMEM)
HBM = pl.BlockSpec(memory_space=pltpu.HBM)
ANY = pl.BlockSpec(memory_space=pl.ANY)


def shape(*dims):
    return jax.ShapeDtypeStruct(dims, F32)


def call(kernel, name, in_specs, outs, us, mib, out_specs=None, scratch=(), aliases=None):
    return pl.pallas_call(
        kernel,
        in_specs=in_specs,
        out_specs=out_specs or [VMEM] * len(outs),
        out_shape=outs,
        scratch_shapes=scratch,
        input_output_aliases=aliases or {},
        compiler_params=pltpu.CompilerParams(vmem_limit_bytes=mib * MIB),
        cost_estimate=pl.CostEstimate(flops=1000, bytes_accessed=int(us * 3.0e6), transcendentals=0),
        name=name,
    )


def in_hbm(array):
    return pltpu.with_memory_space_constraint(array, pltpu.HBM)


def body(
    fields_e, fields_h, cot_e, cot_h, labels, region_eps, angle_index, profiles, zsheet,
    layer_term, block_inverse,
):
    e, h, ge, gh = fields_e[0], fields_h[0], cot_e[0], cot_h[0]
    zs, lt = zsheet.reshape(1, CZ), layer_term.reshape(1, CZ)
    slab = shape(X, Y, CZ)
    message = shape(SLABS, 8, CZ)

    def space(*dims, dtype=F32):
        return pltpu.VMEM(dims, dtype)

    rx, ry, ax, ay, psx, psy, gs, inv, hv, w, keep, send = call(
        rhs_kernel, "right_hand_sides",
        [SMEM, SMEM] + [HBM] * 9,
        [slab] * 8 + [shape(3, X, Y, CZ), shape(CZ, CZ)] + [message] * 2,
        6, 24,
        scratch=[
            space(2, X, Y, CZ), space(3, X, Y, CZ), space(3, X, Y, CZ),
            space(X, Y, CZ, dtype=jnp.int32), pltpu.SemaphoreType.DMA((6, X)),
            space(Y, CZ, dtype=BF), space(2, X, Y), space(1, CZ), space(1, CZ),
        ],
    )(angle_index, *map(in_hbm, (region_eps, e, h, ge, gh, labels, profiles, zs, lt, block_inverse)))

    other = swap(send, "gz", 1)
    (m0,) = call(chip_kernel, "chip", [VMEM] * 2, [message], 0.5, 4)(keep, other)
    m3, m2, m1 = (swap(m0, "gz", 2 * k) for k in (3, 2, 1))

    adjoint, ez = call(
        adjoint_kernel, "adjoint_products", [VMEM] * 5 + [HBM, ANY], [slab] * 2, 3, 8,
        scratch=[pltpu.SemaphoreType.DMA],
    )(ax, ay, psx, psy, w, in_hbm(e), m0)
    (n0,) = call(group_kernel, "group", [VMEM] * 4 + [ANY], [message], 0.5, 4)(m3, m2, m1, m0, adjoint)
    n2, n3, n1 = (swap(n0, "gz", 8 * k) for k in (2, 3, 1))

    ex, ey, grad = call(primal_kernel, "primal_products", [VMEM] * 7 + [ANY], [slab] * 3, 4, 8)(
        rx, ry, hv, ez, gs, adjoint, w, n0
    )
    own_edges, send_edges = call(
        back_kernel, "back", [VMEM] * 10 + [ANY], [shape(12, 8, CZ)] * 2, 0.5, 4
    )(n2, n3, n1, n0, m3, m2, m1, m0, keep, other, ex)
    other_edges = swap(send_edges, "gz", 1)

    def gradient(k):
        return call(
            lambda *refs: gradient_kernel(k, *refs), f"gradient_{k}", [VMEM] * 8,
            [shape(2, Y, CZ)], 1, 8,
        )(grad, psx, psy, gs, inv, own_edges, other_edges, w)[0]

    arrived = [swap(gradient(k), "src", k) for k in (2, 3, 1)]
    own = gradient(0)

    e_new, h_new = call(
        output_kernel, "outputs", [VMEM] * 8, [shape(3, X, Y, CZ)] * 2, 6, 16,
        out_specs=[HBM] * 2,
        scratch=[space(3, X, Y, CZ), space(3, X, Y, CZ), pltpu.SemaphoreType.DMA((2, X))],
    )(ex, ey, hv, ez, inv, own_edges, other_edges, w)

    total = own + arrived[0] + arrived[1] + arrived[2]
    two, three, one = (swap(total, "src", k) for k in (2, 3, 1))
    (partial,) = call(
        place_first, "place_first", [ANY] * 2, [slab], 1, 4, out_specs=[HBM],
        scratch=[pltpu.SemaphoreType.DMA((2,))],
    )(total, two)
    (eps_grad,) = call(
        place_rest, "place_rest", [ANY] * 2 + [HBM], [slab], 1, 4, out_specs=[HBM],
        scratch=[pltpu.SemaphoreType.DMA((2,))], aliases={2: 0},
    )(three, one, partial)
    return (e_new[None], h_new[None], eps_grad)


def solution(mesh):
    field = P("src", None, None, None, "gz")
    return jax.shard_map(
        body,
        mesh=mesh,
        in_specs=(
            field, field, field, field, P(None, None, "gz"), P(), P("src"), P(), P("gz"), P("gz"),
            P("gz", None),
        ),
        out_specs=(field, field, P(None, None, "gz")),
        check_vma=False,
    )
```
